256 devices in a mesh: row: 16 (over y, x_lo, core), col: 16 (over z, x_hi).
Axes of the slice: x: 4 (x_hi: 2, x_lo: 2; x = x_hi * 2 + x_lo), y: 4, z: 8, core: 2. Of those that a mesh axis runs over, the one named last changes fastest.
Arguments:
- fine_tiles: bfloat16 [128, 256, 512], P('row', 'col'), may hold values from -6 to 6
- out_grad: bfloat16 [64, 128, 1024], P('row'), may hold values from -6 to 6
- down_proj: bfloat16 [2048, 1024], P('col'), may hold values from -0.125 to 0.125
- qkv_proj: bfloat16 [1024, 3, 1024], P(None, None, 'col'), may hold values from -3 to 3
- out_proj: bfloat16 [1024, 1024], P('col'), may hold values from -0.1875 to 0.1875
- norm_gain: bfloat16 [1024], replicated, may hold values from 0.099609375 to 1.8984375
Outputs:
- coarse_out: bfloat16 [64, 128, 1024], P('row')
- merged_grad: bfloat16 [64, 128, 2048], P('row', None, 'col')
- down_grad: float32 [2048, 1024], P('col', 'row')
- qkv_grad: float32 [1024, 3, 1024], P('row', None, 'col')
- out_proj_grad: float32 [1024, 1024], P('col', 'row')
- gain_grad: float32 [1024], P('row')
The draws below stay inside these ranges and needn't reach their ends.
All inputs are finite; a program needn't handle non-finite values.
Results may differ from the reference program's by a relative error of at most 0.029.
Values may be sent and summed in bfloat16 or wider, within the bound.
A program may use at most 128 MiB of HBM per device.

```python
import math
import jax
import jax.numpy as jnp
from jax import lax

D2 = 512
D3 = 1024
HEAD = 64
H3 = 64
W3 = 128
H2 = 128
W2 = 256


def draw_qkv_proj(key, part):
    key = jax.random.fold_in(key, 11)
    key_base = jax.random.fold_in(key, 0)
    drawn = jnp.clip(jax.random.normal(key_base, (D3, 3, D3), jnp.float32), -6.0, 6.0) / math.sqrt(D3)
    lifted = jnp.array([2.0, 2.0, 1.0], jnp.float32).reshape(1, 3, 1)
    return jnp.clip(drawn * lifted, -3.0, 3.0).astype(jnp.bfloat16)


def block_scale(rng, extent, cuts, least, top_value):
    level = 1.0
    for dim, parts in cuts:
        draws = jax.random.uniform(jax.random.fold_in(jax.random.fold_in(rng, 6), dim), (parts,), jnp.float32, least / len(cuts), top_value / len(cuts))
        level = level * jnp.repeat(jnp.exp(draws), extent[dim] // parts).reshape((-1,) + (1,) * (len(extent) - 1 - dim))
    return level


def noise(own_key, extent, width, bound, cuts=(), kind=jnp.bfloat16):
    values = width * jax.random.normal(own_key, extent, jnp.float32)
    if cuts:
        values = values * block_scale(own_key, extent, cuts, -0.22, 0.18)
    return jnp.clip(values, -bound, bound).astype(kind)


def setup_inputs(seed: int = 0) -> dict:
    splits = jax.random.split(jax.random.key(seed), 7)
    return {
        "fine_tiles": noise(splits[0], (H2, W2, D2), 1.0, 6.0, ((0, 16), (1, 16))),
        "out_grad": noise(splits[1], (H3, W3, D3), 1.0, 6.0, ((0, 16),)),
        "down_proj": noise(splits[2], (4 * D2, D3), (4 * D2) ** -0.5, 0.125, ((0, 16),)),
        "qkv_proj": draw_qkv_proj(jax.random.fold_in(splits[6], 71), 0),
        "out_proj": noise(splits[4], (D3, D3), D3 ** -0.5, 0.1875, ((0, 16),)),
        "norm_gain": jnp.clip(1.0 + 0.18 * jax.random.normal(splits[5], (D3,), jnp.float32), 0.099609375, 1.8984375).astype(jnp.bfloat16),
    }


EPSILON = 1e-06

def block_rows(total):
    return math.gcd(total, 512)

def forward_head(queries, keys, values):
    temper = HEAD ** (-0.5)
    total = queries.shape[0]
    rows_block = block_rows(total)

    def one_block(query_rows):
        scores = jnp.dot(query_rows, keys.T, preferred_element_type=jnp.float32) * temper
        maxima = lax.optimization_barrier(jnp.max(scores, axis=-1, keepdims=True))
        weights = jnp.exp(scores - maxima)
        totals = lax.optimization_barrier(jnp.sum(weights, axis=-1, keepdims=True))
        mixed = jnp.dot(weights.astype(jnp.bfloat16), values, preferred_element_type=jnp.float32) / totals
        return (mixed.astype(jnp.bfloat16), (maxima + jnp.log(totals))[:, 0])
    outputs, log_totals = lax.map(one_block, queries.reshape(total // rows_block, rows_block, -1))
    return (outputs.reshape(total, -1), log_totals.reshape(total))

def backward_head(queries, keys, values, outputs, log_totals, out_cot):
    temper = HEAD ** (-0.5)
    total = queries.shape[0]
    rows_block = block_rows(total)
    blocks = total // rows_block
    delta_rows = lax.optimization_barrier(jnp.sum(out_cot.astype(jnp.float32) * outputs.astype(jnp.float32), axis=-1))

    def query_block(bundle):
        query_rows, cot_rows, lse_rows, delta_part = bundle
        scores = jnp.dot(query_rows, keys.T, preferred_element_type=jnp.float32) * temper
        weights = jnp.exp(scores - lse_rows[:, None])
        prob_cot = jnp.dot(cot_rows, values.T, preferred_element_type=jnp.float32)
        score_cot = (weights * (prob_cot - delta_part[:, None])).astype(jnp.bfloat16)
        return jnp.dot(score_cot, keys, preferred_element_type=jnp.float32) * temper
    query_cot = lax.map(query_block, (queries.reshape(blocks, rows_block, -1), out_cot.reshape(blocks, rows_block, -1), log_totals.reshape(blocks, rows_block), delta_rows.reshape(blocks, rows_block)))

    def key_block(bundle):
        key_rows, value_rows = bundle
        scores = jnp.dot(key_rows, queries.T, preferred_element_type=jnp.float32) * temper
        weights = jnp.exp(scores - log_totals[None, :])
        value_cot = jnp.dot(weights.astype(jnp.bfloat16), out_cot, preferred_element_type=jnp.float32)
        prob_cot = jnp.dot(value_rows, out_cot.T, preferred_element_type=jnp.float32)
        score_cot = (weights * (prob_cot - delta_rows[None, :])).astype(jnp.bfloat16)
        key_cot = jnp.dot(score_cot, queries, preferred_element_type=jnp.float32) * temper
        return (key_cot, value_cot)
    key_cot, value_cot = lax.map(key_block, (keys.reshape(blocks, rows_block, -1), values.reshape(blocks, rows_block, -1)))
    return (query_cot.reshape(total, -1), key_cot.reshape(total, -1), value_cot.reshape(total, -1))

def reference(fine_tiles, out_grad, down_proj, qkv_proj, out_proj, norm_gain):
    height, breadth, channels = fine_tiles.shape
    coarse_h = height // 2
    coarse_w = breadth // 2
    tokens_all = coarse_h * coarse_w
    merged = fine_tiles.reshape(coarse_h, 2, coarse_w, 2, channels).transpose(0, 2, 1, 3, 4).reshape(tokens_all, 4 * channels)
    coarse = jnp.dot(merged, down_proj, preferred_element_type=jnp.float32).astype(jnp.bfloat16)
    model_width = down_proj.shape[1]
    heads_all = model_width // HEAD
    coarse_f = coarse.astype(jnp.float32)
    inverse = lax.rsqrt(lax.optimization_barrier(jnp.mean(coarse_f * coarse_f, axis=-1, keepdims=True)) + EPSILON)
    gain_f = norm_gain.astype(jnp.float32)
    normed = (coarse_f * inverse * gain_f).astype(jnp.bfloat16)
    flat_proj = qkv_proj.reshape(model_width, 3 * model_width)
    projected = jnp.dot(normed, flat_proj, preferred_element_type=jnp.float32).astype(jnp.bfloat16)
    per_head = projected.reshape(tokens_all, 3, heads_all, HEAD).transpose(1, 2, 0, 3)
    outputs, log_totals = lax.map(lambda triple: forward_head(triple[0], triple[1], triple[2]), (per_head[0], per_head[1], per_head[2]))
    attended = outputs.transpose(1, 0, 2).reshape(tokens_all, model_width)
    mixed = jnp.dot(attended, out_proj, preferred_element_type=jnp.float32)
    coarse_out = (coarse_f + mixed).astype(jnp.bfloat16)
    grad_rows = out_grad.reshape(tokens_all, model_width)
    out_proj_grad = jnp.dot(attended.T, grad_rows, preferred_element_type=jnp.float32)
    attended_cot = jnp.dot(grad_rows, out_proj.T, preferred_element_type=jnp.float32).astype(jnp.bfloat16)
    cot_heads = attended_cot.reshape(tokens_all, heads_all, HEAD).transpose(1, 0, 2)
    query_cot, key_cot, value_cot = lax.map(lambda group: backward_head(group[0], group[1], group[2], group[3], group[4], group[5]), (per_head[0], per_head[1], per_head[2], outputs, log_totals, cot_heads))
    projected_cot = jnp.stack([query_cot, key_cot, value_cot], axis=0).astype(jnp.bfloat16)
    projected_cot = projected_cot.transpose(2, 0, 1, 3).reshape(tokens_all, 3 * model_width)
    qkv_grad = jnp.dot(normed.T, projected_cot, preferred_element_type=jnp.float32).reshape(model_width, 3, model_width)
    normed_cot = jnp.dot(projected_cot, flat_proj.T, preferred_element_type=jnp.float32)
    gain_grad = lax.optimization_barrier(jnp.sum(normed_cot * coarse_f * inverse, axis=0))
    scaled = normed_cot * gain_f
    coarse_cot = grad_rows.astype(jnp.float32) + inverse * scaled - coarse_f * inverse ** 3 * lax.optimization_barrier(jnp.mean(scaled * coarse_f, axis=-1, keepdims=True))
    coarse_cot = coarse_cot.astype(jnp.bfloat16)
    down_grad = jnp.dot(merged.T, coarse_cot, preferred_element_type=jnp.float32)
    merged_grad = jnp.dot(coarse_cot, down_proj.T, preferred_element_type=jnp.float32).astype(jnp.bfloat16)
    return (coarse_out.reshape(coarse_h, coarse_w, model_width), merged_grad.reshape(coarse_h, coarse_w, 4 * channels), down_grad, qkv_grad, out_proj_grad, gain_grad)
```

```python
import functools

import jax
import jax.numpy as jnp
from jax import lax
from jax.experimental import pallas as pl
from jax.experimental.pallas import tpu as pltpu
from jax.sharding import PartitionSpec as P

HEAD = 64
EPSILON = 1e-06
BF = jnp.bfloat16
F32 = jnp.float32


def mm(x, y):
    return jnp.dot(x, y, preferred_element_type=F32)


def mm_nt(x, y):
    return lax.dot_general(x, y, (((1,), (1,)), ((), ())), preferred_element_type=F32)


def flip(x):
    return x.astype(F32).T


def kernel(R, C, A, *refs):
    (fine, og, down, qkv, outp, gain,
     co_o, mg_o, dg_o, qg_o, opg_o, gg_o,
     fine_f, a2a_s, mrecv, merged, rs1_s, rs1_r, coarse_s, inv_s, normed,
     dO_s, w_t, kv, qd, kv_t, qd_t, k_m, v_m, q_m, d_m,
     m_s, l_s, acc_s, o_s, o_r, lse_s, lse_r, st, att_t,
     rs2_s, rs2_r, dkv_acc, dkv_s, dkv_r, dq_acc, dq_s, dq_r,
     rs3_s, rs3_r, g_t, g_s, g_r, cc, gn_s, gn_r, gt_s, gt_r, gsum, dp_s, dp_r,
     s_col, r_col, s_row, r_row) = refs
    B = R // A
    T, D = og.shape
    tb = T // C
    r = lax.axis_index("row")
    c = lax.axis_index("col")
    a = lax.rem(r, A)
    b = lax.div(r, A)

    def peer_col(i):
        return lax.rem(c + i, C)

    def at_row(i):
        return lax.rem(r + i, R)

    def rcopy(src, dst, ssem, rsem, dev):
        return pltpu.make_async_remote_copy(
            src_ref=src, dst_ref=dst, send_sem=ssem, recv_sem=rsem,
            device_id=dev, device_id_type=pl.DeviceIdType.MESH)

    def rows(ref, j):
        return ref.at[pl.ds(pl.multiple_of(j * tb, tb), tb)]

    def loop(n, fn):
        lax.fori_loop(1, n, lambda i, z: (fn(i), z)[1], 0)

    def col_send(k, src, dst):
        def one(i):
            j = peer_col(i)
            rcopy(src(j), dst(c), s_col.at[k, j], r_col.at[k, c], (r, j)).start()
        loop(C, one)

    def col_wait(k, dst, i):
        s = lax.rem(c + C - i, C)
        rcopy(dst(s), dst(s), s_col.at[k, s], r_col.at[k, s], (r, s)).wait_recv()
        return s

    def col_done(k, src):
        def one(i):
            j = peer_col(i)
            rcopy(src(j), src(j), s_col.at[k, j], r_col.at[k, j], (r, j)).wait_send()
        loop(C, one)

    def row_send(k, src, dst):
        def one(i):
            j = at_row(i)
            rcopy(src(j), dst(r), s_row.at[k, j], r_row.at[k, r], (j, c)).start()
        loop(R, one)

    def row_wait(k, dst, i):
        s = lax.rem(r + R - i, R)
        rcopy(dst(s), dst(s), s_row.at[k, s], r_row.at[k, s], (s, c)).wait_recv()
        return s

    def row_done(k, src):
        def one(i):
            j = at_row(i)
            rcopy(src(j), src(j), s_row.at[k, j], r_row.at[k, j], (j, c)).wait_send()
        loop(R, one)

    def a_dev(j):
        return (b * A + j, c)

    def b_dev(j):
        return (j * A + a, c)

    def grp(n, me, dev):
        def send_one(k, src, dst, j):
            rcopy(src, dst(me), s_row.at[k, j], r_row.at[k, me], dev(j)).start()

        def send(k, src, dst):
            loop(n, lambda i: send_one(k, src(lax.rem(me + i, n)), dst, lax.rem(me + i, n)))

        def wait(k, dst, i):
            s = lax.rem(me + n - i, n)
            rcopy(dst(s), dst(s), s_row.at[k, s], r_row.at[k, s], dev(s)).wait_recv()
            return s

        def done(k, src):
            def one(i):
                j = lax.rem(me + i, n)
                rcopy(src(j), src(j), s_row.at[k, j], r_row.at[k, j], dev(j)).wait_send()
            loop(n, one)
        return send_one, send, wait, done

    a_one, a_send, a_wait, a_done = grp(A, a, a_dev)
    b_one, b_send, b_wait, b_done = grp(B, b, b_dev)

    barrier = pltpu.get_barrier_semaphore()
    loop(C, lambda i: pl.semaphore_signal(
        barrier, inc=1, device_id=(r, peer_col(i)), device_id_type=pl.DeviceIdType.MESH))
    loop(R, lambda i: pl.semaphore_signal(
        barrier, inc=1, device_id=(at_row(i), c), device_id_type=pl.DeviceIdType.MESH))

    H8, W16, D2 = fine.shape
    n_cb = D2 // 128
    for cb in range(n_cb):
        fine_f[cb] = fine[:, :, cb * 128:(cb + 1) * 128].astype(F32)
    for aa in range(2):
        for bb in range(2):
            for cb in range(n_cb):
                parts = [fine_f[cb, 2 * h + aa, pl.ds(bb, W16 // 2, stride=2), :]
                         for h in range(H8 // 2)]
                a2a_s[(aa * 2 + bb) * n_cb + cb] = jnp.concatenate(parts, axis=0).astype(BF)
    mrecv[c] = a2a_s[c]
    pl.semaphore_wait(barrier, C + R - 2)
    col_send(0, lambda j: a2a_s.at[j], lambda j: mrecv.at[j])

    dO_s[...] = mm_nt(og[...], outp[...]).astype(BF)
    w_t[...] = flip(qkv[...]).astype(BF)

    loop(C, lambda i: col_wait(0, lambda s: mrecv.at[s], i))
    mr = mrecv[...].astype(F32).reshape(C, H8 // 2, W16 // 2, 128)
    merged[...] = jnp.swapaxes(mr, 0, 1).reshape(T, 128).astype(BF)

    rs1_s[...] = mm(merged[...], down[...]).astype(BF)
    col_send(1, lambda j: rows(rs1_s, j), lambda j: rs1_r.at[j])

    def reduce_col(k, s_ref, r_ref):
        def one(i, acc):
            s = col_wait(k, lambda q: r_ref.at[q], i)
            return acc + r_ref[s].astype(F32)
        return lax.fori_loop(1, C, one, rows(s_ref, c)[...].astype(F32))

    coarse = reduce_col(1, rs1_s, rs1_r).astype(BF).astype(F32)
    coarse_s[...] = coarse
    inv = lax.rsqrt(jnp.mean(coarse * coarse, axis=-1, keepdims=True) + EPSILON)
    inv_s[...] = jnp.broadcast_to(inv, inv_s.shape)
    gain_f = gain[...].astype(F32)
    rows(normed, c)[...] = (coarse * inv * gain_f).astype(BF)
    col_send(2, lambda j: rows(normed, c), lambda j: rows(normed, j))
    loop(C, lambda i: col_wait(2, lambda s: rows(normed, s), i))

    temper = HEAD ** (-0.5)
    proj = mm(normed[...], qkv[...]).astype(BF)
    kv[b] = proj[:, HEAD:]
    b_send(0, lambda j: kv.at[b], lambda j: kv.at[j])
    q_own = (proj[:, :HEAD].astype(F32) * temper).astype(BF)
    qd[a] = jnp.concatenate([q_own, dO_s[...]], axis=1)
    a_send(1, lambda j: qd.at[a], lambda j: qd.at[j])

    lane = lax.broadcasted_iota(jnp.int32, (T, 128), 1)
    zero = jnp.zeros((T, 128), BF)

    def prep_kv(s):
        x = kv[s]
        kv_t[s] = flip(x).astype(BF)
        k_m[s] = jnp.where(lane < HEAD, x, zero)
        v_m[s] = jnp.where(lane >= HEAD, x, zero)

    def prep_qd(s):
        x = qd[s]
        qd_t[s] = flip(x).astype(BF)
        q_m[s] = jnp.where(lane < HEAD, x, zero)
        d_m[s] = jnp.where(lane >= HEAD, x, zero)

    prep_kv(b)
    prep_qd(a)
    loop(B, lambda i: prep_kv(b_wait(0, lambda s: kv.at[s], i)))
    loop(A, lambda i: prep_qd(a_wait(1, lambda s: qd.at[s], i)))

    QS = min(256, T)

    def fwd_q(qi):
        m_s[...] = jnp.full(m_s.shape, -jnp.inf, F32)
        l_s[...] = jnp.zeros(l_s.shape, F32)
        acc_s[...] = jnp.zeros(acc_s.shape, F32)

        def fwd_k(kj, z):
            km = k_m[kj]
            vt = kv_t[kj, HEAD:, :]
            for t in range(T // QS):
                sl = slice(t * QS, (t + 1) * QS)
                s_t = mm(km, qd_t[qi, :, sl])
                old = m_s[:, sl]
                new = jnp.maximum(old, jnp.max(s_t, axis=0, keepdims=True))
                p = jnp.exp(s_t - new)
                shrink = jnp.exp(old - new)
                m_s[:, sl] = new
                l_s[:, sl] = l_s[:, sl] * shrink + jnp.sum(p, axis=0, keepdims=True)
                acc_s[:, sl] = acc_s[:, sl] * shrink + mm(vt, p.astype(BF))
            return z
        lax.fori_loop(0, B, fwd_k, 0)
        o_s[qi] = (acc_s[...] / l_s[...]).astype(BF)
        lse_s[qi] = jnp.broadcast_to(m_s[...] + jnp.log(l_s[...]), lse_s.shape[1:])

    def fwd_one(i):
        qi = lax.rem(a + i, A)
        fwd_q(qi)
        a_one(2, o_s.at[qi], lambda j: o_r.at[j], qi)
        a_one(3, lse_s.at[qi], lambda j: lse_r.at[j], qi)
    loop(A, fwd_one)
    fwd_q(a)
    o_r[a] = o_s[a]
    lse_r[a] = lse_s[a]
    loop(A, lambda i: (a_wait(2, lambda s: o_r.at[s], i), a_wait(3, lambda s: lse_r.at[s], i)))

    lses = [lse_r[s, 0:1, :] for s in range(A)]
    top = functools.reduce(jnp.maximum, lses)
    lse = top + jnp.log(sum(jnp.exp(x - top) for x in lses))
    o_t = sum(jnp.exp(x - lse) * o_r[s].astype(F32) for s, x in enumerate(lses)).astype(BF)
    att_t[...] = o_t
    d_own = qd_t[a, HEAD:, :].astype(F32)
    delta = jnp.sum(d_own * o_t.astype(F32), axis=0, keepdims=True)
    st[a] = jnp.concatenate([lse, delta, jnp.zeros((6, T), F32)], axis=0)
    a_send(4, lambda j: st.at[a], lambda j: st.at[j])

    att = flip(o_t).astype(BF)
    rs2_s[...] = mm(att, outp[...]).astype(BF)
    col_send(3, lambda j: rows(rs2_s, j), lambda j: rs2_r.at[j])
    g_t[3 * HEAD:, :] = mm(o_t, og[...])
    dkv_acc[...] = jnp.zeros(dkv_acc.shape, F32)
    dq_acc[...] = jnp.zeros(dq_acc.shape, F32)
    loop(A, lambda i: a_wait(4, lambda s: st.at[s], i))

    def bwd_k(kj):
        def bwd_q(i, z):
            qi = lax.rem(a + 1 + i, A)
            kt = kv_t[kj, :HEAD, :]
            for t in range(T // QS):
                sl = slice(t * QS, (t + 1) * QS)
                qs = qd_t[qi, :, sl]
                s_t = mm(k_m[kj], qs)
                p = jnp.exp(s_t - st[qi, 0:1, sl])
                dp = mm(v_m[kj], qs)
                ds = (p * (dp - st[qi, 1:2, sl])).astype(BF)
                dkv_acc[kj] += mm(ds, q_m[qi, sl, :]) + mm(p.astype(BF), d_m[qi, sl, :])
                dq_acc[qi, :, sl] += mm(kt, ds)
            return z
        lax.fori_loop(0, A, bwd_q, 0)

    def bwd_one(i):
        kj = lax.rem(b + i, B)
        bwd_k(kj)
        dkv_s[kj] = dkv_acc[kj].astype(BF)
        b_one(5, dkv_s.at[kj], lambda j: dkv_r.at[j], kj)
    loop(B, bwd_one)
    bwd_k(b)

    def dq_one(i):
        qi = lax.rem(a + i, A)
        dq_s[qi] = dq_acc[qi].astype(BF)
        a_one(6, dq_s.at[qi], lambda j: dq_r.at[j], qi)
    loop(A, dq_one)

    def dkv_sum(i, acc):
        s = b_wait(5, lambda q: dkv_r.at[q], i)
        return acc + dkv_r[s].astype(F32)
    dkv = lax.fori_loop(1, B, dkv_sum, dkv_acc[b]).astype(BF)

    def dq_sum(i, acc):
        s = a_wait(6, lambda q: dq_r.at[q], i)
        return acc + dq_r[s].astype(F32)
    dq_t = (lax.fori_loop(1, A, dq_sum, dq_acc[a]) * temper).astype(BF)

    dq = flip(dq_t).astype(BF)
    rs3_s[...] = (mm(dq, w_t[:HEAD, :]) + mm(dkv, w_t[HEAD:, :])).astype(BF)
    col_send(4, lambda j: rows(rs3_s, j), lambda j: rs3_r.at[j])

    g_t[:HEAD, :] = mm(dq_t, normed[...])
    g_t[HEAD:3 * HEAD, :] = mm(flip(dkv).astype(BF), normed[...])
    g_s[...] = g_t[...].T.astype(BF)
    gb = D // R

    def g_rows(j):
        return g_s.at[pl.ds(pl.multiple_of(j * gb, gb), gb)]
    row_send(7, g_rows, lambda j: g_r.at[j])

    mixed = reduce_col(3, rs2_s, rs2_r)
    rows(co_o, c)[...] = (coarse_s[...] + mixed).astype(BF)

    ncot = reduce_col(4, rs3_s, rs3_r)
    coarse = coarse_s[...]
    inv = inv_s[:, :1]
    gpart = jnp.sum(ncot * coarse * inv, axis=0, keepdims=True)
    scaled = ncot * gain_f
    ogr = rows(og, c)[...].astype(F32)
    ccot = ogr + inv * scaled - coarse * (inv * inv * inv) * jnp.mean(
        scaled * coarse, axis=-1, keepdims=True)
    rows(cc, c)[...] = ccot.astype(BF)
    col_send(5, lambda j: rows(cc, c), lambda j: rows(cc, j))
    gp = jnp.concatenate([gpart[:, i * 128:(i + 1) * 128] for i in range(D // 128)], axis=0)
    gn_s[...] = gp
    gn_r[c] = gp
    col_send(6, lambda j: gn_s, lambda j: gn_r.at[j])
    col_send(7, lambda j: rows(co_o, c), lambda j: rows(co_o, j))

    def g_sum(i, acc):
        s = row_wait(7, lambda q: g_r.at[q], i)
        return acc + g_r[s].astype(F32)
    g_all = lax.fori_loop(1, R, g_sum, g_rows(r)[...].astype(F32))
    qg_o[...] = g_all[:, :3 * HEAD]
    opg_o[...] = g_all[:, 3 * HEAD:].T

    loop(C, lambda i: col_wait(5, lambda s: rows(cc, s), i))
    dpt = flip(merged[...]).astype(BF)
    dp_s[...] = mm(dpt, cc[...]).T.astype(BF)

    def d_rows(j):
        return dp_s.at[pl.ds(pl.multiple_of(j * gb, gb), gb)]
    row_send(8, d_rows, lambda j: dp_r.at[j])

    loop(C, lambda i: col_wait(6, lambda s: gn_r.at[s], i))
    gt = jnp.sum(gn_r[...], axis=0)
    gt_s[...] = gt
    gt_r[r] = gt
    row_send(9, lambda j: gt_s, lambda j: gt_r.at[j])
    mg_o[...] = mm_nt(cc[...], down[...]).astype(BF)

    def d_sum(i, acc):
        s = row_wait(8, lambda q: dp_r.at[q], i)
        return acc + dp_r[s].astype(F32)
    dg_o[...] = lax.fori_loop(1, R, d_sum, d_rows(r)[...].astype(F32)).T

    loop(R, lambda i: row_wait(9, lambda s: gt_r.at[s], i))
    gsum[...] = jnp.sum(gt_r[...], axis=0)
    g_row = gsum[pl.ds(lax.div(r, 2), 1), :]
    gg_o[...] = jnp.where(lax.rem(r, 2) == 0, g_row[:, :64], g_row[:, 64:])

    loop(C, lambda i: col_wait(7, lambda s: rows(co_o, s), i))

    col_done(0, lambda j: a2a_s.at[j])
    col_done(1, lambda j: rows(rs1_s, j))
    col_done(2, lambda j: rows(normed, c))
    col_done(3, lambda j: rows(rs2_s, j))
    col_done(4, lambda j: rows(rs3_s, j))
    col_done(5, lambda j: rows(cc, c))
    col_done(6, lambda j: gn_s)
    col_done(7, lambda j: rows(co_o, c))
    b_done(0, lambda j: kv.at[b])
    a_done(1, lambda j: qd.at[a])
    a_done(2, lambda j: o_s.at[j])
    a_done(3, lambda j: lse_s.at[j])
    a_done(4, lambda j: st.at[a])
    b_done(5, lambda j: dkv_s.at[j])
    a_done(6, lambda j: dq_s.at[j])
    row_done(7, g_rows)
    row_done(8, d_rows)
    row_done(9, lambda j: gt_s)


def body(R, C, fine_tiles, out_grad, down_proj, qkv_proj, out_proj, norm_gain):
    A = 2 ** ((R.bit_length() - 1) // 2)
    B = R // A
    D = out_grad.shape[-1]
    th, tw = out_grad.shape[0], out_grad.shape[1]
    T = th * tw
    tb = T // C
    H8, W16, D2 = fine_tiles.shape
    ch = down_proj.shape[0]
    gb = D // R
    V = pltpu.VMEM
    scratch = [
        V((D2 // 128, H8, W16, 128), F32), V((C, tb, 128), BF), V((C, tb, 128), BF),
        V((T, 128), BF), V((T, D), BF), V((C, tb, D), BF), V((tb, D), F32), V((tb, 128), F32),
        V((T, D), BF),
        V((T, HEAD), BF), V((3 * HEAD, D), BF), V((B, T, 128), BF), V((A, T, 128), BF),
        V((B, 128, T), BF), V((A, 128, T), BF), V((B, T, 128), BF), V((B, T, 128), BF),
        V((A, T, 128), BF), V((A, T, 128), BF),
        V((1, T), F32), V((1, T), F32), V((HEAD, T), F32),
        V((A, HEAD, T), BF), V((A, HEAD, T), BF), V((A, 8, T), F32), V((A, 8, T), F32),
        V((A, 8, T), F32), V((HEAD, T), BF),
        V((T, D), BF), V((C, tb, D), BF),
        V((B, T, 128), F32), V((B, T, 128), BF), V((B, T, 128), BF),
        V((A, HEAD, T), F32), V((A, HEAD, T), BF), V((A, HEAD, T), BF),
        V((T, D), BF), V((C, tb, D), BF),
        V((4 * HEAD, D), F32), V((D, 4 * HEAD), BF), V((R, gb, 4 * HEAD), BF),
        V((T, D), BF), V((D // 128, 128), F32), V((C, D // 128, 128), F32),
        V((D // 128, 128), F32), V((R, D // 128, 128), F32), V((D // 128, 128), F32),
        V((D, ch), BF), V((R, gb, ch), BF),
        pltpu.SemaphoreType.DMA((8, C)), pltpu.SemaphoreType.DMA((8, C)),
        pltpu.SemaphoreType.DMA((10, R)), pltpu.SemaphoreType.DMA((10, R)),
    ]
    vm = pl.BlockSpec(memory_space=pltpu.VMEM)
    outs = pl.pallas_call(
        functools.partial(kernel, R, C, A),
        out_shape=(
            jax.ShapeDtypeStruct((T, D), BF),
            jax.ShapeDtypeStruct((T, ch), BF),
            jax.ShapeDtypeStruct((ch, gb), F32),
            jax.ShapeDtypeStruct((gb, 3 * HEAD), F32),
            jax.ShapeDtypeStruct((HEAD, gb), F32),
            jax.ShapeDtypeStruct((1, gb), F32),
        ),
        in_specs=[vm] * 6,
        out_specs=(vm,) * 6,
        scratch_shapes=scratch,
        compiler_params=pltpu.CompilerParams(
            collective_id=0, has_side_effects=True, vmem_limit_bytes=56 * 1024 * 1024),
        name="block",
    )(fine_tiles, out_grad.reshape(T, D), down_proj, qkv_proj.reshape(D, 3 * HEAD), out_proj,
      norm_gain.reshape(1, D))
    co, mg, dg, qg, opg, gg = outs
    return (co.reshape(th, tw, D), mg.reshape(th, tw, ch), dg, qg.reshape(gb, 3, HEAD), opg,
            gg.reshape(gb))


def solution(mesh):
    R, C = mesh.shape["row"], mesh.shape["col"]
    return jax.shard_map(
        functools.partial(body, R, C),
        mesh=mesh,
        in_specs=(P("row", "col", None), P("row", None, None), P("col", None),
                  P(None, None, "col"), P("col", None), P()),
        out_specs=(P("row", None, None), P("row", None, "col"), P("col", "row"),
                   P("row", None, "col"), P("col", "row"), P("row")),
        check_vma=False,
    )
```

```python
import functools

import jax
import jax.numpy as jnp
from jax import lax
from jax.experimental import pallas as pl
from jax.experimental.pallas import tpu as pltpu
from jax.sharding import PartitionSpec as P

HEAD = 64
EPSILON = 1e-06
BF = jnp.bfloat16
F32 = jnp.float32


def mm(x, y):
    return jnp.dot(x, y, preferred_element_type=F32)


def mm_nt(x, y):
    return lax.dot_general(x, y, (((1,), (1,)), ((), ())), preferred_element_type=F32)


def flip(x):
    return x.astype(F32).T


def kernel(R, C, A, *refs):
    (fine, og, down, qkv, outp, gain,
     co_o, mg_o, dg_o, qg_o, opg_o, gg_o,
     fine_f, a2a_s, mrecv, merged, down_p, w_s, w_t, out_p,
     rs1_s, rs1_r, coarse_s, inv_s, normed, px_kv, px_q, q_x,
     kv, qd, kv_t, qd_t, k_m, v_m, q_m, d_m,
     m_s, l_s, acc_s, o_s, o_r, lse_s, lse_r, st, att_s, att_r,
     rs2_s, rs2_r, dkv_acc, dkv_s, dkv_r, dq_acc, dq_s, dq_r, dp_s, dp_r,
     rs3_s, rs3_r, g_t, g_s, g_r, cc, gn_s, gn_r, gt_s, gt_r, gsum, mg_s, dn_s, dn_r,
     s_col, r_col, s_z, r_z, s_p, r_p, s_row, r_row, s_d, r_d) = refs
    B = R // A
    Z = C // 2
    T, D = og.shape
    tp = T // 2
    tb = tp // Z
    r = lax.axis_index("row")
    c = lax.axis_index("col")
    a = lax.rem(r, A)
    b = lax.div(r, A)
    z = lax.div(c, 2)
    x = lax.rem(c, 2)
    y = 1 - x
    pc = z * 2 + y

    def rcopy(src, dst, ssem, rsem, dev):
        return pltpu.make_async_remote_copy(
            src_ref=src, dst_ref=dst, send_sem=ssem, recv_sem=rsem,
            device_id=dev, device_id_type=pl.DeviceIdType.MESH)

    def blk(ref, j, n):
        return ref.at[pl.ds(pl.multiple_of(j * n, n), n)]

    def zrow(ref, j):
        return blk(ref, j, tb)

    def own(ref):
        return ref.at[pl.ds(pl.multiple_of(x * tp + z * tb, tb), tb)]

    def plane(ref, p):
        return blk(ref, p, tp)

    def loop(n, fn):
        lax.fori_loop(1, n, lambda i, t: (fn(i), t)[1], 0)

    def ring(n, me, dev, near):
        def off(i):
            odd = lax.rem(i, 2)
            return odd * lax.div(i + 1, 2) + (1 - odd) * (n - lax.div(i, 2)) if near else i

        def send_one(sem, src, dst, j):
            rcopy(src, dst(me), sem[0].at[j], sem[1].at[me], dev(j)).start()

        def send(sem, src, dst):
            def one(i):
                j = lax.rem(me + off(i), n)
                send_one(sem, src(j), dst, j)
            loop(n, one)

        def wait(sem, dst, i):
            s = lax.rem(me + n - off(i), n)
            rcopy(dst(s), dst(s), sem[0].at[s], sem[1].at[s], dev(s)).wait_recv()
            return s

        def done(sem, src):
            def one(i):
                j = lax.rem(me + i, n)
                rcopy(src(j), src(j), sem[0].at[j], sem[1].at[j], dev(j)).wait_send()
            loop(n, one)
        return send_one, send, wait, done

    _, col_send, col_wait, col_done = ring(C, c, lambda j: (r, j), False)
    _, z_send, z_wait, z_done = ring(Z, z, lambda j: (r, j * 2 + x), True)
    _, row_send, row_wait, row_done = ring(R, r, lambda j: (j, c), False)
    a_one, a_send, a_wait, a_done = ring(A, a, lambda j: (b * A + j, c), False)
    b_one, b_send, b_wait, b_done = ring(B, b, lambda j: (j * A + a, c), False)
    _, d_send, d_wait, d_done = ring(
        2 * R, r * 2 + x, lambda j: (lax.div(j, 2), z * 2 + lax.rem(j, 2)), False)

    def sc(k):
        return s_col.at[k], r_col.at[k]

    def sz(k):
        return s_z.at[k], r_z.at[k]

    def sr(k):
        return s_row.at[k], r_row.at[k]

    def pair(k, src, dst):
        return rcopy(src, dst, s_p.at[k], r_p.at[k], (r, pc))

    barrier = pltpu.get_barrier_semaphore()

    def greet(dev):
        pl.semaphore_signal(barrier, inc=1, device_id=dev, device_id_type=pl.DeviceIdType.MESH)
    loop(C, lambda i: greet((r, lax.rem(c + i, C))))
    loop(R, lambda i: greet((lax.rem(r + i, R), c)))
    loop(R, lambda i: greet((lax.rem(r + i, R), pc)))

    H8, W16, D2 = fine.shape
    n_cb = D2 // 128
    for cb in range(n_cb):
        fine_f[cb] = fine[:, :, cb * 128:(cb + 1) * 128].astype(F32)
    for aa in range(2):
        for bb in range(2):
            for cb in range(n_cb):
                parts = [fine_f[cb, 2 * h + aa, pl.ds(bb, W16 // 2, stride=2), :]
                         for h in range(H8 // 2)]
                a2a_s[(aa * 2 + bb) * n_cb + cb] = jnp.concatenate(parts, axis=0).astype(BF)

    def a2a_src(j):
        return a2a_s.at[pl.ds(lax.div(j, 2) * 2, 2), pl.ds(pl.multiple_of(lax.rem(j, 2) * 16, 16), 16)]

    mrecv[c] = a2a_src(c)[...]
    blk(down_p, x, down.shape[0])[...] = down[...]
    w_t[x, :2 * HEAD, :] = qkv[HEAD:, :]
    w_t[x, 2 * HEAD:3 * HEAD, :] = qkv[:HEAD, :]
    for k in range(2):
        w_t[k, 3 * HEAD:, :] = jnp.zeros((HEAD, D), BF)
    blk(out_p, x, HEAD)[...] = outp[...]
    pl.semaphore_wait(barrier, C + 2 * R - 3)
    col_send(sc(0), a2a_src, lambda j: mrecv.at[j])
    p_down = pair(0, down, blk(down_p, x, down.shape[0]))
    p_down.start()
    p_w = pair(1, w_t.at[x, pl.ds(0, 3 * HEAD)], w_t.at[x, pl.ds(0, 3 * HEAD)])
    p_w.start()
    p_out = pair(2, outp, blk(out_p, x, HEAD))
    p_out.start()

    d_own = mm_nt(og[...], outp[...]).astype(BF)
    w_s[x] = flip(w_t[x]).astype(BF)

    loop(C, lambda i: col_wait(sc(0), lambda s: mrecv.at[s], i))
    for k in range(2):
        mr = mrecv[:, k].astype(F32).reshape(C, 2, W16 // 2, 128)
        merged[:, k * 128:(k + 1) * 128] = jnp.swapaxes(mr, 0, 1).reshape(tp, 128).astype(BF)
    p_down.wait_recv()

    rs1_s[...] = mm(merged[...], down_p[...]).astype(BF)
    z_send(sz(0), lambda j: zrow(rs1_s, j), lambda j: rs1_r.at[j])

    def reduce_z(k, s_ref, r_ref):
        def one(i, acc):
            s = z_wait(sz(k), lambda q: r_ref.at[q], i)
            return acc + r_ref[s].astype(F32)
        return lax.fori_loop(1, Z, one, zrow(s_ref, z)[...].astype(F32))

    coarse = reduce_z(0, rs1_s, rs1_r).astype(BF).astype(F32)
    coarse_s[...] = coarse
    inv = lax.rsqrt(jnp.mean(coarse * coarse, axis=-1, keepdims=True) + EPSILON)
    inv_s[...] = jnp.broadcast_to(inv, inv_s.shape)
    gain_f = gain[...].astype(F32)
    own(normed)[...] = (coarse * inv * gain_f).astype(BF)

    def own_at(ref):
        return lambda j: ref.at[pl.ds(pl.multiple_of(x * tp + j * tb, tb), tb)]
    z_send(sz(1), lambda j: own(normed), own_at(normed))
    p_w.wait_recv()
    w_s[y] = flip(w_t[y]).astype(BF)
    loop(Z, lambda i: z_wait(sz(1), own_at(normed), i))

    temper = HEAD ** (-0.5)
    n_pl = plane(normed, x)[...]
    proj = mm(n_pl, w_s[y]).astype(BF)
    px_kv[...] = proj[:, :128]
    px_q[...] = (proj[:, 128:].astype(F32) * temper).astype(BF)
    p_kv = pair(3, px_kv, kv.at[b, pl.ds(pl.multiple_of(x * tp, tp), tp)])
    p_kv.start()
    p_q = pair(4, px_q, plane(q_x, x))
    p_q.start()
    proj = mm(n_pl, w_s[x]).astype(BF)
    kv[b, pl.ds(pl.multiple_of(x * tp, tp), tp)] = proj[:, :128]
    plane(q_x, x)[...] = (proj[:, 128:].astype(F32) * temper).astype(BF)
    p_kv.wait_recv()
    b_send(sr(0), lambda j: kv.at[b], lambda j: kv.at[j])
    p_q.wait_recv()
    qd[a] = jnp.concatenate([q_x[:, :HEAD], d_own], axis=1)
    a_send(sr(1), lambda j: qd.at[a], lambda j: qd.at[j])

    lane = lax.broadcasted_iota(jnp.int32, (T, 128), 1)
    zero = jnp.zeros((T, 128), BF)

    def prep_kv(s):
        v = kv[s]
        kv_t[s] = flip(v).astype(BF)
        k_m[s] = jnp.where(lane < HEAD, v, zero)
        v_m[s] = jnp.where(lane >= HEAD, v, zero)

    def prep_qd(s):
        v = qd[s]
        qd_t[s] = flip(v).astype(BF)
        q_m[s] = jnp.where(lane < HEAD, v, zero)
        d_m[s] = jnp.where(lane >= HEAD, v, zero)

    prep_kv(b)
    prep_qd(a)
    loop(B, lambda i: prep_kv(b_wait(sr(0), lambda s: kv.at[s], i)))
    loop(A, lambda i: prep_qd(a_wait(sr(1), lambda s: qd.at[s], i)))

    QS = min(256, T)

    def fwd_q(qi):
        m_s[...] = jnp.full(m_s.shape, -jnp.inf, F32)
        l_s[...] = jnp.zeros(l_s.shape, F32)
        acc_s[...] = jnp.zeros(acc_s.shape, F32)

        def fwd_k(kj, t0):
            km = k_m[kj]
            vt = kv_t[kj, HEAD:, :]
            for t in range(T // QS):
                sl = slice(t * QS, (t + 1) * QS)
                s_t = mm(km, qd_t[qi, :, sl])
                old = m_s[:, sl]
                new = jnp.maximum(old, jnp.max(s_t, axis=0, keepdims=True))
                p = jnp.exp(s_t - new)
                shrink = jnp.exp(old - new)
                m_s[:, sl] = new
                l_s[:, sl] = l_s[:, sl] * shrink + jnp.sum(p, axis=0, keepdims=True)
                acc_s[:, sl] = acc_s[:, sl] * shrink + mm(vt, p.astype(BF))
            return t0
        lax.fori_loop(0, B, fwd_k, 0)
        o_s[qi] = (acc_s[...] / l_s[...]).astype(BF)
        lse_s[qi] = jnp.broadcast_to(m_s[...] + jnp.log(l_s[...]), lse_s.shape[1:])

    def fwd_one(i):
        qi = lax.rem(a + i, A)
        fwd_q(qi)
        a_one(sr(2), o_s.at[qi], lambda j: o_r.at[j], qi)
        a_one(sr(3), lse_s.at[qi], lambda j: lse_r.at[j], qi)
    loop(A, fwd_one)
    fwd_q(a)
    o_r[a] = o_s[a]
    lse_r[a] = lse_s[a]
    loop(A, lambda i: (a_wait(sr(2), lambda s: o_r.at[s], i),
                       a_wait(sr(3), lambda s: lse_r.at[s], i)))

    lses = [lse_r[s, 0:1, :] for s in range(A)]
    top = functools.reduce(jnp.maximum, lses)
    lse = top + jnp.log(sum(jnp.exp(v - top) for v in lses))
    o_t = sum(jnp.exp(v - lse) * o_r[s].astype(F32) for s, v in enumerate(lses)).astype(BF)
    delta = jnp.sum(qd_t[a, HEAD:, :].astype(F32) * o_t.astype(F32), axis=0, keepdims=True)
    st[a] = jnp.concatenate([lse, delta, jnp.zeros((6, T), F32)], axis=0)
    a_send(sr(4), lambda j: st.at[a], lambda j: st.at[j])

    att_s[:, :HEAD] = flip(o_t).astype(BF)
    att_s[:, HEAD:] = jnp.zeros((T, 128 - HEAD), BF)
    p_att = pair(5, plane(att_s, y), att_r)
    p_att.start()
    p_norm = pair(6, plane(normed, x), plane(normed, x))
    p_norm.start()
    g_t[3 * HEAD:, :] = mm(o_t, og[...])
    dkv_acc[...] = jnp.zeros(dkv_acc.shape, F32)
    dq_acc[...] = jnp.zeros(dq_acc.shape, F32)
    loop(A, lambda i: a_wait(sr(4), lambda s: st.at[s], i))

    def bwd_k(kj):
        def bwd_q(i, t0):
            qi = lax.rem(a + 1 + i, A)
            kt = kv_t[kj, :HEAD, :]
            for t in range(T // QS):
                sl = slice(t * QS, (t + 1) * QS)
                qs = qd_t[qi, :, sl]
                s_t = mm(k_m[kj], qs)
                p = jnp.exp(s_t - st[qi, 0:1, sl])
                dp = mm(v_m[kj], qs)
                ds = (p * (dp - st[qi, 1:2, sl])).astype(BF)
                dkv_acc[kj] += mm(ds, q_m[qi, sl, :]) + mm(p.astype(BF), d_m[qi, sl, :])
                dq_acc[qi, :, sl] += mm(kt, ds)
            return t0
        lax.fori_loop(0, A, bwd_q, 0)

    def bwd_one(i):
        kj = lax.rem(b + i, B)
        bwd_k(kj)
        dkv_s[kj] = dkv_acc[kj].astype(BF)
        b_one(sr(5), dkv_s.at[kj], lambda j: dkv_r.at[j], kj)

        @pl.when(i == 1)
        def _():
            p_att.wait_recv()
            p_out.wait_recv()
            rs2_s[...] = (mm(plane(att_s, x)[:, :HEAD], blk(out_p, x, HEAD)[...])
                          + mm(att_r[:, :HEAD], blk(out_p, y, HEAD)[...])).astype(BF)
            z_send(sz(2), lambda j: zrow(rs2_s, j), lambda j: rs2_r.at[j])

        @pl.when(i == B - 1)
        def _():
            mixed = reduce_z(2, rs2_s, rs2_r)
            own(co_o)[...] = (coarse_s[...] + mixed).astype(BF)
            z_send(sz(5), lambda j: own(co_o), own_at(co_o))
    loop(B, bwd_one)
    bwd_k(b)

    def dq_one(i):
        qi = lax.rem(a + i, A)
        dq_s[qi] = dq_acc[qi].astype(BF)
        a_one(sr(6), dq_s.at[qi], lambda j: dq_r.at[j], qi)
    loop(A, dq_one)

    def dkv_sum(i, acc):
        s = b_wait(sr(5), lambda q: dkv_r.at[q], i)
        return acc + dkv_r[s].astype(F32)
    dkv = lax.fori_loop(1, B, dkv_sum, dkv_acc[b]).astype(BF)

    def dq_sum(i, acc):
        s = a_wait(sr(6), lambda q: dq_r.at[q], i)
        return acc + dq_r[s].astype(F32)
    dq_t = (lax.fori_loop(1, A, dq_sum, dq_acc[a]) * temper).astype(BF)

    dp_s[:, :128] = dkv
    dp_s[:, 128:] = jnp.concatenate([flip(dq_t).astype(BF), jnp.zeros((T, HEAD), BF)], axis=1)
    p_dp = pair(7, plane(dp_s, y), dp_r)
    p_dp.start()
    part = mm(plane(dp_s, x)[...], w_t[x])
    p_dp.wait_recv()
    rs3_s[...] = (part + mm(dp_r[...], w_t[y])).astype(BF)
    z_send(sz(3), lambda j: zrow(rs3_s, j), lambda j: rs3_r.at[j])

    loop(Z, lambda i: z_wait(sz(5), own_at(co_o), i))
    p_co = pair(8, plane(co_o, x), plane(co_o, x))
    p_co.start()

    p_norm.wait_recv()
    g_t[:2 * HEAD, :] = mm(flip(dkv).astype(BF), normed[...])
    g_t[2 * HEAD:3 * HEAD, :] = mm(dq_t, normed[...])
    g_s[...] = g_t[...].T.astype(BF)
    gb = D // R

    def g_rows(j):
        return blk(g_s, j, gb)
    row_send(sr(7), g_rows, lambda j: g_r.at[j])

    ncot = reduce_z(3, rs3_s, rs3_r)
    coarse = coarse_s[...]
    inv = inv_s[:, :1]
    gpart = jnp.sum(ncot * coarse * inv, axis=0, keepdims=True)
    scaled = ncot * gain_f
    ccot = own(og)[...].astype(F32) + inv * scaled - coarse * (inv * inv * inv) * jnp.mean(
        scaled * coarse, axis=-1, keepdims=True)
    zrow(cc, z)[...] = ccot.astype(BF)
    z_send(sz(4), lambda j: zrow(cc, z), lambda j: zrow(cc, j))
    gp = jnp.concatenate([gpart[:, i * 128:(i + 1) * 128] for i in range(D // 128)], axis=0)
    gn_s[...] = gp
    gn_r[c] = gp
    col_send(sc(1), lambda j: gn_s, lambda j: gn_r.at[j])

    def g_sum(i, acc):
        s = row_wait(sr(7), lambda q: g_r.at[q], i)
        return acc + g_r[s].astype(F32)
    g_all = lax.fori_loop(1, R, g_sum, g_rows(r)[...].astype(F32))
    for k in range(3):
        qg_o[k] = g_all[:, (k + 2) % 3 * HEAD:(k + 2) % 3 * HEAD + HEAD]
    opg_o[...] = g_all[:, 3 * HEAD:].T

    m_t = [flip(merged[:, k * 128:(k + 1) * 128]).astype(BF) for k in range(2)]
    loop(Z, lambda i: z_wait(sz(4), lambda s: zrow(cc, s), i))
    for k in range(2):
        dn_s[k] = mm(m_t[k], cc[...]).T.astype(BF)

    def dn_src(j):
        return dn_s.at[lax.rem(j, 2), pl.ds(pl.multiple_of(lax.div(j, 2) * gb, gb), gb)]
    sd = (s_d, r_d)
    d_send(sd, dn_src, lambda j: dn_r.at[j])

    mg_s[...] = mm_nt(cc[...], blk(down_p, y, down.shape[0])[...]).astype(BF)
    p_mg = pair(9, mg_s, plane(mg_o, x))
    p_mg.start()
    loop(C, lambda i: col_wait(sc(1), lambda s: gn_r.at[s], i))
    gt = jnp.sum(gn_r[...], axis=0)
    gt_s[...] = gt
    gt_r[r] = gt
    row_send(sr(8), lambda j: gt_s, lambda j: gt_r.at[j])
    plane(mg_o, x)[...] = mm_nt(cc[...], blk(down_p, x, down.shape[0])[...]).astype(BF)

    def d_sum(i, acc):
        s = d_wait(sd, lambda q: dn_r.at[q], i)
        return acc + dn_r[s].astype(F32)
    dg_o[...] = lax.fori_loop(1, 2 * R, d_sum, dn_src(r * 2 + x)[...].astype(F32))

    loop(R, lambda i: row_wait(sr(8), lambda s: gt_r.at[s], i))
    gsum[...] = jnp.sum(gt_r[...], axis=0)
    g_row = gsum[pl.ds(lax.div(r, 2), 1), :]
    gg_o[...] = jnp.where(lax.rem(r, 2) == 0, g_row[:, :64], g_row[:, 64:])

    p_co.wait_recv()
    p_mg.wait_recv()
    for p in (p_down, p_w, p_out, p_kv, p_q, p_att, p_norm, p_dp, p_co, p_mg):
        p.wait_send()
    col_done(sc(0), a2a_src)
    col_done(sc(1), lambda j: gn_s)
    z_done(sz(0), lambda j: zrow(rs1_s, j))
    z_done(sz(1), lambda j: own(normed))
    z_done(sz(2), lambda j: zrow(rs2_s, j))
    z_done(sz(3), lambda j: zrow(rs3_s, j))
    z_done(sz(4), lambda j: zrow(cc, z))
    z_done(sz(5), lambda j: own(co_o))
    b_done(sr(0), lambda j: kv.at[b])
    a_done(sr(1), lambda j: qd.at[a])
    a_done(sr(2), lambda j: o_s.at[j])
    a_done(sr(3), lambda j: lse_s.at[j])
    a_done(sr(4), lambda j: st.at[a])
    b_done(sr(5), lambda j: dkv_s.at[j])
    a_done(sr(6), lambda j: dq_s.at[j])
    row_done(sr(7), g_rows)
    row_done(sr(8), lambda j: gt_s)
    d_done(sd, dn_src)


def body(R, C, fine_tiles, out_grad, down_proj, qkv_proj, out_proj, norm_gain):
    A = 2 ** ((R.bit_length() - 1) // 2)
    B = R // A
    D = out_grad.shape[-1]
    th, tw = out_grad.shape[0], out_grad.shape[1]
    T = th * tw
    Z = C // 2
    tp = T // 2
    tb = tp // Z
    H8, W16, D2 = fine_tiles.shape
    ch = down_proj.shape[0]
    gb = D // R
    V = pltpu.VMEM
    S = pltpu.SemaphoreType.DMA
    scratch = [
        V((D2 // 128, H8, W16, 128), F32), V((C, 32, 128), BF), V((C, 2, 16, 128), BF),
        V((tp, 2 * ch), BF), V((2 * ch, D), BF), V((2, D, 4 * HEAD), BF), V((2, 4 * HEAD, D), BF),
        V((2 * HEAD, D), BF),
        V((tp, D), BF), V((Z, tb, D), BF), V((tb, D), F32), V((tb, 128), F32),
        V((T, D), BF), V((tp, 128), BF), V((tp, 128), BF), V((T, 128), BF),
        V((B, T, 128), BF), V((A, T, 128), BF),
        V((B, 128, T), BF), V((A, 128, T), BF), V((B, T, 128), BF), V((B, T, 128), BF),
        V((A, T, 128), BF), V((A, T, 128), BF),
        V((1, T), F32), V((1, T), F32), V((HEAD, T), F32),
        V((A, HEAD, T), BF), V((A, HEAD, T), BF), V((A, 8, T), F32), V((A, 8, T), F32),
        V((A, 8, T), F32), V((T, 128), BF), V((tp, 128), BF),
        V((tp, D), BF), V((Z, tb, D), BF),
        V((B, T, 128), F32), V((B, T, 128), BF), V((B, T, 128), BF),
        V((A, HEAD, T), F32), V((A, HEAD, T), BF), V((A, HEAD, T), BF),
        V((T, 4 * HEAD), BF), V((tp, 4 * HEAD), BF),
        V((tp, D), BF), V((Z, tb, D), BF),
        V((4 * HEAD, D), F32), V((D, 4 * HEAD), BF), V((R, gb, 4 * HEAD), BF),
        V((tp, D), BF), V((D // 128, 128), F32), V((C, D // 128, 128), F32),
        V((D // 128, 128), F32), V((R, D // 128, 128), F32), V((D // 128, 128), F32),
        V((tp, ch), BF), V((2, D, ch), BF), V((2 * R, gb, ch), BF),
        S((2, C)), S((2, C)), S((6, Z)), S((6, Z)), S((10,)), S((10,)),
        S((9, R)), S((9, R)), S((2 * R,)), S((2 * R,)),
    ]
    vm = pl.BlockSpec(memory_space=pltpu.VMEM)
    outs = pl.pallas_call(
        functools.partial(kernel, R, C, A),
        out_shape=(
            jax.ShapeDtypeStruct((T, D), BF),
            jax.ShapeDtypeStruct((T, ch), BF),
            jax.ShapeDtypeStruct((gb, ch), F32),
            jax.ShapeDtypeStruct((3, gb, HEAD), F32),
            jax.ShapeDtypeStruct((HEAD, gb), F32),
            jax.ShapeDtypeStruct((1, gb), F32),
        ),
        in_specs=[vm] * 6,
        out_specs=(vm,) * 6,
        scratch_shapes=scratch,
        compiler_params=pltpu.CompilerParams(
            collective_id=0, has_side_effects=True, vmem_limit_bytes=56 * 1024 * 1024),
        name="block",
    )(fine_tiles, out_grad.reshape(T, D), down_proj, qkv_proj.transpose(1, 2, 0).reshape(3 * HEAD, D), out_proj,
      norm_gain.reshape(1, D))
    co, mg, dg, qg, opg, gg = outs
    return (co.reshape(th, tw, D), mg.reshape(th, tw, ch), dg.T, qg.transpose(1, 0, 2), opg,
            gg.reshape(gb))


def solution(mesh):
    R, C = mesh.shape["row"], mesh.shape["col"]
    return jax.shard_map(
        functools.partial(body, R, C),
        mesh=mesh,
        in_specs=(P("row", "col", None), P("row", None, None), P("col", None),
                  P(None, None, "col"), P("col", None), P()),
        out_specs=(P("row", None, None), P("row", None, "col"), P("col", "row"),
                   P("row", None, "col"), P("col", "row"), P("row")),
        check_vma=False,
    )
```

```python
import functools

import jax
import jax.numpy as jnp
from jax import lax
from jax.experimental import pallas as pl
from jax.experimental.pallas import tpu as pltpu
from jax.sharding import PartitionSpec as P

HEAD = 64
EPSILON = 1e-06
BF = jnp.bfloat16
F32 = jnp.float32


def mm(x, y):
    return jnp.dot(x, y, preferred_element_type=F32)


def mm_nt(x, y):
    return lax.dot_general(x, y, (((1,), (1,)), ((), ())), preferred_element_type=F32)


def flip(x):
    return x.astype(F32).T


def kernel(R, C, A, *refs):
    (fine, og, down, qkv, outp, gain,
     co_o, mg_o, dg_o, qg_o, opg_o, gg_o,
     fine_f, a2a_s, mrecv, merged, down_p, w_s, w_t, out_p,
     rs1_s, rs1_r, coarse_s, inv_s, normed, px_kv, px_q,
     kv, kv_t, qd_t, k_m, v_m, q_m, d_m,
     o_s, o_r, lse_s, lse_r, st, att_s, att_r,
     rs2_s, rs2_r, dkv_acc, dkv_s, dkv_r, dq_acc, dq_s, dq_r, dp_s, dp_r,
     rs3_s, rs3_r, g_t, g_s, g_r, cc, gn_s, gn_r, gt_s, gt_r, gsum, mg_s, dn_s, dn_r,
     s_col, r_col, s_z, r_z, s_p, r_p, s_row, r_row, s_d, r_d) = refs
    B = R // A
    Z = C // 2
    T, D = og.shape
    tp = T // 2
    tb = tp // Z
    r = lax.axis_index("row")
    c = lax.axis_index("col")
    a = lax.rem(r, A)
    b = lax.div(r, A)
    z = lax.div(c, 2)
    x = lax.rem(c, 2)
    y = 1 - x
    pc = z * 2 + y

    def rcopy(src, dst, ssem, rsem, dev):
        return pltpu.make_async_remote_copy(
            src_ref=src, dst_ref=dst, send_sem=ssem, recv_sem=rsem,
            device_id=dev, device_id_type=pl.DeviceIdType.MESH)

    def blk(ref, j, n):
        return ref.at[pl.ds(pl.multiple_of(j * n, n), n)]

    def zrow(ref, j):
        return blk(ref, j, tb)

    def own(ref):
        return ref.at[pl.ds(pl.multiple_of(x * tp + z * tb, tb), tb)]

    def plane(ref, p):
        return blk(ref, p, tp)

    def loop(n, fn):
        lax.fori_loop(1, n, lambda i, t: (fn(i), t)[1], 0)

    def ring(n, me, dev, near):
        def off(i):
            odd = lax.rem(i, 2)
            return odd * lax.div(i + 1, 2) + (1 - odd) * (n - lax.div(i, 2)) if near else i

        def send_one(sem, src, dst, j):
            rcopy(src, dst(me), sem[0].at[j], sem[1].at[me], dev(j)).start()

        def send(sem, src, dst):
            def one(i):
                j = lax.rem(me + off(i), n)
                send_one(sem, src(j), dst, j)
            loop(n, one)

        def wait(sem, dst, i):
            s = lax.rem(me + n - off(i), n)
            rcopy(dst(s), dst(s), sem[0].at[s], sem[1].at[s], dev(s)).wait_recv()
            return s

        def done(sem, src):
            def one(i):
                j = lax.rem(me + i, n)
                rcopy(src(j), src(j), sem[0].at[j], sem[1].at[j], dev(j)).wait_send()
            loop(n, one)
        return send_one, send, wait, done

    _, col_send, col_wait, col_done = ring(C, c, lambda j: (r, j), False)
    _, z_send, z_wait, z_done = ring(Z, z, lambda j: (r, j * 2 + x), True)
    _, row_send, row_wait, row_done = ring(R, r, lambda j: (j, c), False)
    a_one, a_send, a_wait, a_done = ring(A, a, lambda j: (b * A + j, c), False)
    b_one, b_send, b_wait, b_done = ring(B, b, lambda j: (j * A + a, c), False)
    _, d_send, d_wait, d_done = ring(
        2 * R, r * 2 + x, lambda j: (lax.div(j, 2), z * 2 + lax.rem(j, 2)), False)

    def sc(k):
        return s_col.at[k], r_col.at[k]

    def sz(k):
        return s_z.at[k], r_z.at[k]

    def sr(k):
        return s_row.at[k], r_row.at[k]

    def pair(k, src, dst):
        return rcopy(src, dst, s_p.at[k], r_p.at[k], (r, pc))

    barrier = pltpu.get_barrier_semaphore()

    def greet(dev):
        pl.semaphore_signal(barrier, inc=1, device_id=dev, device_id_type=pl.DeviceIdType.MESH)
    loop(C, lambda i: greet((r, lax.rem(c + i, C))))
    loop(R, lambda i: greet((lax.rem(r + i, R), c)))
    loop(R, lambda i: greet((lax.rem(r + i, R), pc)))

    H8, W16, D2 = fine.shape
    n_cb = D2 // 128
    for cb in range(n_cb):
        fine_f[cb] = fine[:, :, cb * 128:(cb + 1) * 128].astype(F32)
    for aa in range(2):
        for bb in range(2):
            for cb in range(n_cb):
                parts = [fine_f[cb, 2 * h + aa, pl.ds(bb, W16 // 2, stride=2), :]
                         for h in range(H8 // 2)]
                a2a_s[(aa * 2 + bb) * n_cb + cb] = jnp.concatenate(parts, axis=0).astype(BF)

    def a2a_src(j):
        return a2a_s.at[pl.ds(lax.div(j, 2) * 2, 2), pl.ds(pl.multiple_of(lax.rem(j, 2) * 16, 16), 16)]

    pl.semaphore_wait(barrier, C + 2 * R - 3)
    col_send(sc(0), a2a_src, lambda j: mrecv.at[j])
    p_down = pair(0, down, blk(down_p, x, down.shape[0]))
    p_down.start()

    mrecv[c] = a2a_src(c)[...]
    blk(down_p, x, down.shape[0])[...] = down[...]
    qd_t[a, HEAD:, :] = flip(mm_nt(og[...], outp[...])).astype(BF)

    def d_at(j):
        return qd_t.at[j, pl.ds(HEAD, HEAD)]
    a_send(sr(9), lambda j: d_at(a), d_at)
    w_t[x, :2 * HEAD, :] = qkv[HEAD:, :]
    w_t[x, 2 * HEAD:3 * HEAD, :] = qkv[:HEAD, :]
    for k in range(2):
        w_t[k, 3 * HEAD:, :] = jnp.zeros((HEAD, D), BF)
    blk(out_p, x, HEAD)[...] = outp[...]

    loop(C, lambda i: col_wait(sc(0), lambda s: mrecv.at[s], i))
    for k in range(2):
        mr = mrecv[:, k].astype(F32).reshape(C, 2, W16 // 2, 128)
        merged[:, k * 128:(k + 1) * 128] = jnp.swapaxes(mr, 0, 1).reshape(tp, 128).astype(BF)
    p_down.wait_recv()

    rs1_s[...] = mm(merged[...], down_p[...]).astype(BF)
    z_send(sz(0), lambda j: zrow(rs1_s, j), lambda j: rs1_r.at[j])
    p_w = pair(1, w_t.at[x, pl.ds(0, 3 * HEAD)], w_t.at[x, pl.ds(0, 3 * HEAD)])
    p_w.start()
    p_out = pair(2, outp, blk(out_p, x, HEAD))
    p_out.start()
    w_s[x] = flip(w_t[x]).astype(BF)
    dkv_acc[...] = jnp.zeros(dkv_acc.shape, F32)
    dq_acc[...] = jnp.zeros(dq_acc.shape, F32)

    def reduce_z(k, s_ref, r_ref):
        def one(i, acc):
            s = z_wait(sz(k), lambda q: r_ref.at[q], i)
            return acc + r_ref[s].astype(F32)
        return lax.fori_loop(1, Z, one, zrow(s_ref, z)[...].astype(F32))

    coarse = reduce_z(0, rs1_s, rs1_r).astype(BF).astype(F32)
    coarse_s[...] = coarse
    inv = lax.rsqrt(jnp.mean(coarse * coarse, axis=-1, keepdims=True) + EPSILON)
    inv_s[...] = jnp.broadcast_to(inv, inv_s.shape)
    gain_f = gain[...].astype(F32)
    own(normed)[...] = (coarse * inv * gain_f).astype(BF)

    def own_at(ref):
        return lambda j: ref.at[pl.ds(pl.multiple_of(x * tp + j * tb, tb), tb)]
    z_send(sz(1), lambda j: own(normed), own_at(normed))
    p_w.wait_recv()
    w_s[y] = flip(w_t[y]).astype(BF)
    loop(Z, lambda i: z_wait(sz(1), own_at(normed), i))

    temper = HEAD ** (-0.5)
    n_pl = plane(normed, x)[...]
    mine = pl.ds(pl.multiple_of(x * tp, tp), tp)

    def split(w):
        proj = mm(n_pl, w)
        return proj[:, :128].astype(BF), flip(proj[:, 128:].astype(BF).astype(F32) * temper)
    kv_y, q_y = split(w_s[y])
    px_kv[...] = kv_y
    p_kv = pair(3, px_kv, kv.at[b, mine])
    p_kv.start()
    px_q[...] = q_y[:HEAD].astype(BF)
    p_q = pair(4, px_q, qd_t.at[a, pl.ds(0, HEAD), mine])
    p_q.start()
    kv_x, q_x = split(w_s[x])
    kv[b, mine] = kv_x
    qd_t[a, :HEAD, mine] = q_x[:HEAD].astype(BF)

    def kv_at(p):
        return lambda j: kv.at[j, pl.ds(pl.multiple_of(p * tp, tp), tp)]
    b_send(sr(0), lambda j: kv_at(x)(b), kv_at(x))
    p_kv.wait_recv()
    b_send(sr(1), lambda j: kv_at(y)(b), kv_at(y))
    p_q.wait_recv()

    def q_at(j):
        return qd_t.at[j, pl.ds(0, HEAD)]
    a_send(sr(10), lambda j: q_at(a), q_at)

    lane = lax.broadcasted_iota(jnp.int32, (T, 128), 1)
    zero = jnp.zeros((T, 128), BF)

    def prep_kv(s):
        v = kv[s]
        kv_t[s] = flip(v).astype(BF)
        k_m[s] = jnp.where(lane < HEAD, v, zero)
        v_m[s] = jnp.where(lane >= HEAD, v, zero)

    def prep_qd(s):
        v = flip(qd_t[s]).astype(BF)
        q_m[s] = jnp.where(lane < HEAD, v, zero)
        d_m[s] = jnp.where(lane >= HEAD, v, zero)

    prep_kv(b)
    prep_qd(a)

    def kv_next(i):
        b_wait(sr(0), kv_at(x), i)
        prep_kv(b_wait(sr(1), kv_at(y), i))
    loop(B, kv_next)

    def qd_next(i):
        a_wait(sr(9), d_at, i)
        prep_qd(a_wait(sr(10), q_at, i))
    loop(A, qd_next)

    def fwd_q(qi):
        qs = qd_t[qi]
        ss = [mm(k_m[kj], qs) for kj in range(B)]
        top = functools.reduce(
            jnp.maximum, [jnp.max(v, axis=0, keepdims=True) for v in ss])
        ps = [jnp.exp(v - top) for v in ss]
        total = sum(jnp.sum(p, axis=0, keepdims=True) for p in ps)
        acc = sum(mm(kv_t[kj, HEAD:, :], p.astype(BF)) for kj, p in enumerate(ps))
        o_s[qi] = (acc / total).astype(BF)
        lse_s[qi] = jnp.broadcast_to(top + jnp.log(total), lse_s.shape[1:])

    def fwd_one(i):
        qi = lax.rem(a + i, A)
        fwd_q(qi)
        a_one(sr(2), o_s.at[qi], lambda j: o_r.at[j], qi)
        a_one(sr(3), lse_s.at[qi], lambda j: lse_r.at[j], qi)
    loop(A, fwd_one)
    fwd_q(a)
    o_r[a] = o_s[a]
    lse_r[a] = lse_s[a]
    loop(A, lambda i: (a_wait(sr(2), lambda s: o_r.at[s], i),
                       a_wait(sr(3), lambda s: lse_r.at[s], i)))

    lses = [lse_r[s, 0:1, :] for s in range(A)]
    top = functools.reduce(jnp.maximum, lses)
    lse = top + jnp.log(sum(jnp.exp(v - top) for v in lses))
    o_t = sum(jnp.exp(v - lse) * o_r[s].astype(F32) for s, v in enumerate(lses)).astype(BF)
    delta = jnp.sum(qd_t[a, HEAD:, :].astype(F32) * o_t.astype(F32), axis=0, keepdims=True)
    st[a] = jnp.concatenate([lse, delta, jnp.zeros((6, T), F32)], axis=0)
    a_send(sr(4), lambda j: st.at[a], lambda j: st.at[j])

    att_s[:, :HEAD] = flip(o_t).astype(BF)
    att_s[:, HEAD:] = jnp.zeros((T, 128 - HEAD), BF)
    p_att = pair(5, plane(att_s, y), att_r)
    p_att.start()
    g_t[3 * HEAD:, :] = mm(o_t, og[...])
    p_att.wait_recv()
    p_norm = pair(6, plane(normed, x), plane(normed, x))
    p_norm.start()
    p_out.wait_recv()
    rs2_s[...] = (mm(plane(att_s, x)[:, :HEAD], blk(out_p, x, HEAD)[...])
                  + mm(att_r[:, :HEAD], blk(out_p, y, HEAD)[...])).astype(BF)
    z_send(sz(2), lambda j: zrow(rs2_s, j), lambda j: rs2_r.at[j])
    loop(A, lambda i: a_wait(sr(4), lambda s: st.at[s], i))

    def tile(kj, qi):
        qs = qd_t[qi]
        p = jnp.exp(mm(k_m[kj], qs) - st[qi, 0:1, :])
        ds = (p * (mm(v_m[kj], qs) - st[qi, 1:2, :])).astype(BF)
        dkv_acc[kj] += mm(ds, q_m[qi]) + mm(p.astype(BF), d_m[qi])
        dq_acc[qi] += mm(kv_t[kj, :HEAD, :], ds)

    def bwd_one(i):
        kj = lax.rem(b + i, B)

        def two(h, t0):
            tile(kj, lax.rem(a + 2 * h, A))
            tile(kj, lax.rem(a + 2 * h + 1, A))
            return t0
        lax.fori_loop(0, A // 2, two, 0)
        dkv_s[kj] = dkv_acc[kj].astype(BF)
        b_one(sr(5), dkv_s.at[kj], lambda j: dkv_r.at[j], kj)
    loop(B, bwd_one)

    mixed = reduce_z(2, rs2_s, rs2_r)
    own(co_o)[...] = (coarse_s[...] + mixed).astype(BF)
    z_send(sz(5), lambda j: own(co_o), own_at(co_o))

    for i in range(1, A + 1):
        qi = lax.rem(a + i, A)
        tile(b, qi)
        if i < A:
            dq_s[qi] = dq_acc[qi].astype(BF)
            a_one(sr(6), dq_s.at[qi], lambda j: dq_r.at[j], qi)

    def dkv_sum(i, acc):
        s = b_wait(sr(5), lambda q: dkv_r.at[q], i)
        return acc + dkv_r[s].astype(F32)
    dkv = lax.fori_loop(1, B, dkv_sum, dkv_acc[b]).astype(BF)

    def dq_sum(i, acc):
        s = a_wait(sr(6), lambda q: dq_r.at[q], i)
        return acc + dq_r[s].astype(F32)
    dq_t = (lax.fori_loop(1, A, dq_sum, dq_acc[a]) * temper).astype(BF)

    dp_s[:, :128] = dkv
    dp_s[:, 128:] = jnp.concatenate([flip(dq_t).astype(BF), jnp.zeros((T, HEAD), BF)], axis=1)
    p_dp = pair(7, plane(dp_s, y), dp_r)
    p_dp.start()
    part = mm(plane(dp_s, x)[...], w_t[x])
    p_dp.wait_recv()
    rs3_s[...] = (part + mm(dp_r[...], w_t[y])).astype(BF)
    z_send(sz(3), lambda j: zrow(rs3_s, j), lambda j: rs3_r.at[j])

    loop(Z, lambda i: z_wait(sz(5), own_at(co_o), i))
    p_co = pair(8, plane(co_o, x), plane(co_o, x))
    p_co.start()

    p_norm.wait_recv()
    g_t[:2 * HEAD, :] = mm(flip(dkv).astype(BF), normed[...])
    g_t[2 * HEAD:3 * HEAD, :] = mm(dq_t, normed[...])
    g_s[...] = g_t[...].T.astype(BF)
    gb = D // R

    def g_rows(j):
        return blk(g_s, j, gb)
    row_send(sr(7), g_rows, lambda j: g_r.at[j])

    ncot = reduce_z(3, rs3_s, rs3_r)
    coarse = coarse_s[...]
    inv = inv_s[:, :1]
    gpart = jnp.sum(ncot * coarse * inv, axis=0, keepdims=True)
    scaled = ncot * gain_f
    ccot = own(og)[...].astype(F32) + inv * scaled - coarse * (inv * inv * inv) * jnp.mean(
        scaled * coarse, axis=-1, keepdims=True)
    zrow(cc, z)[...] = ccot.astype(BF)
    z_send(sz(4), lambda j: zrow(cc, z), lambda j: zrow(cc, j))
    gp = jnp.concatenate([gpart[:, i * 128:(i + 1) * 128] for i in range(D // 128)], axis=0)
    gn_s[...] = gp
    gn_r[c] = gp
    col_send(sc(1), lambda j: gn_s, lambda j: gn_r.at[j])

    def g_sum(i, acc):
        s = row_wait(sr(7), lambda q: g_r.at[q], i)
        return acc + g_r[s].astype(F32)
    g_all = lax.fori_loop(1, R, g_sum, g_rows(r)[...].astype(F32))
    for k in range(3):
        qg_o[k] = g_all[:, (k + 2) % 3 * HEAD:(k + 2) % 3 * HEAD + HEAD]
    opg_o[...] = g_all[:, 3 * HEAD:].T

    m_t = [flip(merged[:, k * 128:(k + 1) * 128]).astype(BF) for k in range(2)]
    loop(Z, lambda i: z_wait(sz(4), lambda s: zrow(cc, s), i))
    for k in range(2):
        dn_s[k] = mm(m_t[k], cc[...]).T.astype(BF)

    def dn_src(j):
        return dn_s.at[lax.rem(j, 2), pl.ds(pl.multiple_of(lax.div(j, 2) * gb, gb), gb)]
    sd = (s_d, r_d)
    d_send(sd, dn_src, lambda j: dn_r.at[j])

    mg_s[...] = mm_nt(cc[...], blk(down_p, y, down.shape[0])[...]).astype(BF)
    p_mg = pair(9, mg_s, plane(mg_o, x))
    p_mg.start()
    loop(C, lambda i: col_wait(sc(1), lambda s: gn_r.at[s], i))
    gt = jnp.sum(gn_r[...], axis=0)
    gt_s[...] = gt
    gt_r[r] = gt
    row_send(sr(8), lambda j: gt_s, lambda j: gt_r.at[j])
    plane(mg_o, x)[...] = mm_nt(cc[...], blk(down_p, x, down.shape[0])[...]).astype(BF)

    def d_sum(i, acc):
        s = d_wait(sd, lambda q: dn_r.at[q], i)
        return acc + dn_r[s].astype(F32)
    dg_o[...] = lax.fori_loop(1, 2 * R, d_sum, dn_src(r * 2 + x)[...].astype(F32))

    loop(R, lambda i: row_wait(sr(8), lambda s: gt_r.at[s], i))
    gsum[...] = jnp.sum(gt_r[...], axis=0)
    g_row = gsum[pl.ds(lax.div(r, 2), 1), :]
    gg_o[...] = jnp.where(lax.rem(r, 2) == 0, g_row[:, :64], g_row[:, 64:])

    p_co.wait_recv()
    p_mg.wait_recv()
    for p in (p_down, p_w, p_out, p_kv, p_q, p_att, p_norm, p_dp, p_co, p_mg):
        p.wait_send()
    col_done(sc(0), a2a_src)
    col_done(sc(1), lambda j: gn_s)
    z_done(sz(0), lambda j: zrow(rs1_s, j))
    z_done(sz(1), lambda j: own(normed))
    z_done(sz(2), lambda j: zrow(rs2_s, j))
    z_done(sz(3), lambda j: zrow(rs3_s, j))
    z_done(sz(4), lambda j: zrow(cc, z))
    z_done(sz(5), lambda j: own(co_o))
    b_done(sr(0), lambda j: kv_at(x)(b))
    b_done(sr(1), lambda j: kv_at(y)(b))
    a_done(sr(9), lambda j: d_at(a))
    a_done(sr(10), lambda j: q_at(a))
    a_done(sr(2), lambda j: o_s.at[j])
    a_done(sr(3), lambda j: lse_s.at[j])
    a_done(sr(4), lambda j: st.at[a])
    b_done(sr(5), lambda j: dkv_s.at[j])
    a_done(sr(6), lambda j: dq_s.at[j])
    row_done(sr(7), g_rows)
    row_done(sr(8), lambda j: gt_s)
    d_done(sd, dn_src)


def body(R, C, fine_tiles, out_grad, down_proj, qkv_proj, out_proj, norm_gain):
    A = 2 ** ((R.bit_length() - 1) // 2)
    B = R // A
    D = out_grad.shape[-1]
    th, tw = out_grad.shape[0], out_grad.shape[1]
    T = th * tw
    Z = C // 2
    tp = T // 2
    tb = tp // Z
    H8, W16, D2 = fine_tiles.shape
    ch = down_proj.shape[0]
    gb = D // R
    V = pltpu.VMEM
    S = pltpu.SemaphoreType.DMA
    scratch = [
        V((D2 // 128, H8, W16, 128), F32), V((C, 32, 128), BF), V((C, 2, 16, 128), BF),
        V((tp, 2 * ch), BF), V((2 * ch, D), BF), V((2, D, 4 * HEAD), BF), V((2, 4 * HEAD, D), BF),
        V((2 * HEAD, D), BF),
        V((tp, D), BF), V((Z, tb, D), BF), V((tb, D), F32), V((tb, 128), F32),
        V((T, D), BF), V((tp, 128), BF), V((HEAD, tp), BF),
        V((B, T, 128), BF),
        V((B, 128, T), BF), V((A, 128, T), BF), V((B, T, 128), BF), V((B, T, 128), BF),
        V((A, T, 128), BF), V((A, T, 128), BF),
        V((A, HEAD, T), BF), V((A, HEAD, T), BF), V((A, 8, T), F32), V((A, 8, T), F32),
        V((A, 8, T), F32), V((T, 128), BF), V((tp, 128), BF),
        V((tp, D), BF), V((Z, tb, D), BF),
        V((B, T, 128), F32), V((B, T, 128), BF), V((B, T, 128), BF),
        V((A, HEAD, T), F32), V((A, HEAD, T), BF), V((A, HEAD, T), BF),
        V((T, 4 * HEAD), BF), V((tp, 4 * HEAD), BF),
        V((tp, D), BF), V((Z, tb, D), BF),
        V((4 * HEAD, D), F32), V((D, 4 * HEAD), BF), V((R, gb, 4 * HEAD), BF),
        V((tp, D), BF), V((D // 128, 128), F32), V((C, D // 128, 128), F32),
        V((D // 128, 128), F32), V((R, D // 128, 128), F32), V((D // 128, 128), F32),
        V((tp, ch), BF), V((2, D, ch), BF), V((2 * R, gb, ch), BF),
        S((2, C)), S((2, C)), S((6, Z)), S((6, Z)), S((10,)), S((10,)),
        S((11, R)), S((11, R)), S((2 * R,)), S((2 * R,)),
    ]
    vm = pl.BlockSpec(memory_space=pltpu.VMEM)
    outs = pl.pallas_call(
        functools.partial(kernel, R, C, A),
        out_shape=(
            jax.ShapeDtypeStruct((T, D), BF),
            jax.ShapeDtypeStruct((T, ch), BF),
            jax.ShapeDtypeStruct((gb, ch), F32),
            jax.ShapeDtypeStruct((3, gb, HEAD), F32),
            jax.ShapeDtypeStruct((HEAD, gb), F32),
            jax.ShapeDtypeStruct((1, gb), F32),
        ),
        in_specs=[vm] * 6,
        out_specs=(vm,) * 6,
        scratch_shapes=scratch,
        compiler_params=pltpu.CompilerParams(
            collective_id=0, has_side_effects=True, vmem_limit_bytes=56 * 1024 * 1024),
        name="block",
    )(fine_tiles, out_grad.reshape(T, D), down_proj, qkv_proj.transpose(1, 2, 0).reshape(3 * HEAD, D), out_proj,
      norm_gain.reshape(1, D))
    co, mg, dg, qg, opg, gg = outs
    return (co.reshape(th, tw, D), mg.reshape(th, tw, ch), dg.T, qg.transpose(1, 0, 2), opg,
            gg.reshape(gb))


def solution(mesh):
    R, C = mesh.shape["row"], mesh.shape["col"]
    return jax.shard_map(
        functools.partial(body, R, C),
        mesh=mesh,
        in_specs=(P("row", "col", None), P("row", None, None), P("col", None),
                  P(None, None, "col"), P("col", None), P()),
        out_specs=(P("row", None, None), P("row", None, "col"), P("col", "row"),
                   P("row", None, "col"), P("col", "row"), P("row")),
        check_vma=False,
    )
```

```python
import functools

import jax
import jax.numpy as jnp
from jax import lax
from jax.experimental import pallas as pl
from jax.experimental.pallas import tpu as pltpu
from jax.sharding import PartitionSpec as P

HEAD = 64
EPSILON = 1e-06
BF = jnp.bfloat16
F32 = jnp.float32


def mm(x, y):
    return jnp.dot(x, y, preferred_element_type=F32)


def mm_nt(x, y):
    return lax.dot_general(x, y, (((1,), (1,)), ((), ())), preferred_element_type=F32)


def flip(x):
    return x.astype(F32).T


def kernel(R, C, A, *refs):
    (fine, og_h, down_h, qkv_h, outp_h, gain,
     co_h, mg_o, dg_o, qg_o, opg_o, gg_o,
     og, co_o, fine_f, a2a_s, mrecv, merged, down_p, w_s, w_t, out_p,
     rs1_s, rs1_r, rs1_m, coarse_s, inv_s, normed, px_kv, px_q,
     kv, kv_t, qd_t, k_m, v_m, q_m, d_m,
     o_s, o_r, lse_s, lse_r, st, att_s, att_r,
     rs2_s, rs2_r, rs2_m, dkv_acc, dkv_s, dkv_r, dq_acc, dq_s, dq_r, dp_s, dp_r,
     rs3_s, rs3_r, rs3_m, g_t, g_s, g_r, cc, gn_s, gn_r, gt_s, gt_r, gsum, mg_s, dn_s, dn_r,
     s_col, r_col, s_z, r_z, s_p, r_p, s_row, r_row, s_d, r_d, s_in) = refs
    B = R // A
    Z = C // 2
    T, D = og.shape
    core = lax.rem(lax.axis_index("row"), 2)
    tp = T // 2
    tb = tp // Z
    r = lax.axis_index("row")
    c = lax.axis_index("col")
    a = lax.rem(r, A)
    b = lax.div(r, A)
    z = lax.div(c, 2)
    x = lax.rem(c, 2)
    y = 1 - x
    pc = z * 2 + y

    def rcopy(src, dst, ssem, rsem, dev):
        return pltpu.make_async_remote_copy(
            src_ref=src, dst_ref=dst, send_sem=ssem, recv_sem=rsem,
            device_id=dev, device_id_type=pl.DeviceIdType.MESH)

    def blk(ref, j, n):
        return ref.at[pl.ds(pl.multiple_of(j * n, n), n)]

    def zrow(ref, j):
        return blk(ref, j, tb)

    def own(ref):
        return ref.at[pl.ds(pl.multiple_of(x * tp + z * tb, tb), tb)]

    def plane(ref, p):
        return blk(ref, p, tp)

    def loop(n, fn):
        lax.fori_loop(1, n, lambda i, t: (fn(i), t)[1], 0)

    def ring(n, me, dev, near):
        def off(i):
            odd = lax.rem(i, 2)
            return odd * lax.div(i + 1, 2) + (1 - odd) * (n - lax.div(i, 2)) if near else i

        def send_one(sem, src, dst, j):
            rcopy(src, dst(me), sem[0].at[j], sem[1].at[me], dev(j)).start()

        def send(sem, src, dst):
            def one(i):
                j = lax.rem(me + off(i), n)
                send_one(sem, src(j), dst, j)
            loop(n, one)

        def wait(sem, dst, i):
            s = lax.rem(me + n - off(i), n)
            rcopy(dst(s), dst(s), sem[0].at[s], sem[1].at[s], dev(s)).wait_recv()
            return s

        def done(sem, src):
            def one(i):
                j = lax.rem(me + i, n)
                rcopy(src(j), src(j), sem[0].at[j], sem[1].at[j], dev(j)).wait_send()
            loop(n, one)
        return send_one, send, wait, done

    _, col_send, col_wait, col_done = ring(C, c, lambda j: (r, j), False)
    _, z_send, z_wait, z_done = ring(Z, z, lambda j: (r, j * 2 + x), True)
    _, row_send, row_wait, row_done = ring(R, r, lambda j: (j, c), False)
    a_one, a_send, a_wait, a_done = ring(A, a, lambda j: (b * A + j, c), False)
    b_one, b_send, b_wait, b_done = ring(B, b, lambda j: (j * A + a, c), False)
    _, d_send, d_wait, d_done = ring(
        2 * R, r * 2 + x, lambda j: (lax.div(j, 2), z * 2 + lax.rem(j, 2)), False)

    def sc(k):
        return s_col.at[k], r_col.at[k]

    def sz(k):
        return s_z.at[k], r_z.at[k]

    def zd(d):
        return lax.rem(z + 8 + d, 8)

    def rs_copy(k, src, r_ref, q, d):
        return rcopy(src, r_ref.at[q], s_z.at[k, q], r_z.at[k, q], (r, zd(d) * 2 + x))

    def rs_start(k, s_ref, r_ref):
        if Z != 8:
            z_send(sz(k), lambda j: zrow(s_ref, j), lambda j: r_ref.at[j])
            return
        rs_copy(k, zrow(s_ref, zd(4)), r_ref, 2, 4 * core - 2).start()
        rs_copy(k, zrow(s_ref, zd(-3)), r_ref, 0, -1).start()
        rs_copy(k, zrow(s_ref, zd(3)), r_ref, 1, 1).start()
        rs_copy(k, zrow(s_ref, zd(-1)), r_ref, 3, -1).start()
        rs_copy(k, zrow(s_ref, zd(1)), r_ref, 4, 1).start()

    def rs_wait(k, r_ref, qs):
        for q in qs:
            rs_copy(k, r_ref.at[q], r_ref, q, 1).wait_recv()

    def rs_mid(k, s_ref, r_ref, m_ref):
        if Z != 8:
            return
        rs_wait(k, r_ref, (0, 1, 2))
        far = r_ref[2].astype(F32)
        none = jnp.zeros_like(far)
        m_ref[0] = (zrow(s_ref, zd(-2))[...].astype(F32) + r_ref[0].astype(F32)
                    + jnp.where(core == 0, far, none)).astype(BF)
        rs_copy(k, m_ref.at[0], r_ref, 5, -2).start()
        m_ref[1] = (zrow(s_ref, zd(2))[...].astype(F32) + r_ref[1].astype(F32)
                    + jnp.where(core == 0, none, far)).astype(BF)
        rs_copy(k, m_ref.at[1], r_ref, 6, 2).start()

    def rs_done(k, s_ref, r_ref):
        if Z != 8:
            z_done(sz(k), lambda j: zrow(s_ref, j))
            return
        for q in range(7):
            rs_copy(k, r_ref.at[q], r_ref, q, 1).wait_send()

    def ag_copy(k, at, s, q, d):
        return rcopy(at(s), at(s), s_z.at[k, q], r_z.at[k, s], (r, zd(d) * 2 + x))

    def ag_start(k, at):
        if Z != 8:
            z_send(sz(k), lambda j: at(z), at)
            return
        for q, d in enumerate((2, -2, 1, -1)):
            ag_copy(k, at, z, q, d).start()

    def ag_wait(k, at, ds):
        for d in ds:
            ag_copy(k, at, zd(d), 0, 1).wait_recv()

    def ag_mid(k, at):
        if Z != 8:
            return
        ag_wait(k, at, (-2,))
        ag_copy(k, at, zd(-2), 4, 1).start()
        ag_wait(k, at, (2,))
        ag_copy(k, at, zd(2), 5, -1).start()
        ag_copy(k, at, zd(4 * core - 2), 6, 2 - 4 * core).start()

    def ag_end(k, at):
        if Z != 8:
            loop(Z, lambda i: z_wait(sz(k), at, i))
            return
        ag_wait(k, at, (-1, 1, -3, 3, 4))

    def ag_done(k, at):
        if Z != 8:
            z_done(sz(k), lambda j: at(z))
            return
        for q in range(7):
            ag_copy(k, at, z, q, 1).wait_send()

    def sr(k):
        return s_row.at[k], r_row.at[k]

    def pair(k, src, dst):
        return rcopy(src, dst, s_p.at[k], r_p.at[k], (r, pc))

    ch = down_h.shape[0]
    my_down = blk(down_p, x, ch)
    my_out = blk(out_p, x, HEAD)
    loads = [
        pltpu.make_async_copy(down_h, my_down, s_in.at[0]),
        pltpu.make_async_copy(outp_h, my_out, s_in.at[1]),
        pltpu.make_async_copy(og_h, og, s_in.at[2]),
        pltpu.make_async_copy(
            qkv_h.at[pl.ds(HEAD, 2 * HEAD)], w_t.at[x, pl.ds(0, 2 * HEAD)], s_in.at[3]),
        pltpu.make_async_copy(
            qkv_h.at[pl.ds(0, HEAD)], w_t.at[x, pl.ds(2 * HEAD, HEAD)], s_in.at[4]),
    ]
    for load in loads:
        load.start()

    barrier = pltpu.get_barrier_semaphore()

    def greet(dev):
        pl.semaphore_signal(barrier, inc=1, device_id=dev, device_id_type=pl.DeviceIdType.MESH)
    loop(C, lambda i: greet((r, lax.rem(c + i, C))))
    loop(R, lambda i: greet((lax.rem(r + i, R), c)))
    loop(R, lambda i: greet((lax.rem(r + i, R), pc)))

    H8, W16, D2 = fine.shape
    n_cb = D2 // 128
    for cb in range(n_cb):
        fine_f[cb] = fine[:, :, cb * 128:(cb + 1) * 128].astype(F32)
    for aa in range(2):
        for bb in range(2):
            for cb in range(n_cb):
                parts = [fine_f[cb, 2 * h + aa, pl.ds(bb, W16 // 2, stride=2), :]
                         for h in range(H8 // 2)]
                a2a_s[(aa * 2 + bb) * n_cb + cb] = jnp.concatenate(parts, axis=0).astype(BF)

    def a2a_src(j):
        return a2a_s.at[pl.ds(lax.div(j, 2) * 2, 2), pl.ds(pl.multiple_of(lax.rem(j, 2) * 16, 16), 16)]

    pl.semaphore_wait(barrier, C + 2 * R - 3)
    col_send(sc(0), a2a_src, lambda j: mrecv.at[j])
    loads[0].wait()
    p_down = pair(0, my_down, my_down)
    p_down.start()

    mrecv[c] = a2a_src(c)[...]
    loads[1].wait()
    loads[2].wait()
    qd_t[a, HEAD:, :] = mm_nt(my_out[...], og[...]).astype(BF)

    def d_at(j):
        return qd_t.at[j, pl.ds(HEAD, HEAD)]
    a_send(sr(9), lambda j: d_at(a), d_at)
    for k in range(2):
        w_t[k, 3 * HEAD:, :] = jnp.zeros((HEAD, D), BF)
    loads[3].wait()
    loads[4].wait()

    loop(C, lambda i: col_wait(sc(0), lambda s: mrecv.at[s], i))
    for k in range(2):
        mr = mrecv[:, k].astype(F32).reshape(C, 2, W16 // 2, 128)
        merged[:, k * 128:(k + 1) * 128] = jnp.swapaxes(mr, 0, 1).reshape(tp, 128).astype(BF)
    p_down.wait_recv()

    rs1_s[...] = mm(merged[...], down_p[...]).astype(BF)
    rs_start(0, rs1_s, rs1_r)
    p_w = pair(1, w_t.at[x, pl.ds(0, 3 * HEAD)], w_t.at[x, pl.ds(0, 3 * HEAD)])
    p_w.start()
    p_out = pair(2, my_out, my_out)
    p_out.start()
    w_s[x] = flip(w_t[x]).astype(BF)
    rs_mid(0, rs1_s, rs1_r, rs1_m)
    dkv_acc[...] = jnp.zeros(dkv_acc.shape, F32)
    dq_acc[...] = jnp.zeros(dq_acc.shape, F32)

    def reduce_z(k, s_ref, r_ref):
        if Z == 8:
            rs_wait(k, r_ref, (3, 4, 5, 6))
            acc = zrow(s_ref, z)[...].astype(F32)
            for q in (3, 4, 5, 6):
                acc = acc + r_ref[q].astype(F32)
            return acc

        def one(i, acc):
            s = z_wait(sz(k), lambda q: r_ref.at[q], i)
            return acc + r_ref[s].astype(F32)
        return lax.fori_loop(1, Z, one, zrow(s_ref, z)[...].astype(F32))

    coarse = reduce_z(0, rs1_s, rs1_r).astype(BF).astype(F32)
    coarse_s[...] = coarse
    inv = lax.rsqrt(jnp.mean(coarse * coarse, axis=-1, keepdims=True) + EPSILON)
    inv_s[...] = jnp.broadcast_to(inv, inv_s.shape)
    gain_f = gain[...].astype(F32)
    own(normed)[...] = (coarse * inv * gain_f).astype(BF)

    def own_at(ref):
        return lambda j: ref.at[pl.ds(pl.multiple_of(x * tp + j * tb, tb), tb)]
    ag_start(1, own_at(normed))
    ag_mid(1, own_at(normed))
    p_w.wait_recv()
    w_s[y] = flip(w_t[y]).astype(BF)
    ag_end(1, own_at(normed))

    temper = HEAD ** (-0.5)
    n_pl = plane(normed, x)[...]
    mine = pl.ds(pl.multiple_of(x * tp, tp), tp)

    def split(w):
        proj = mm(n_pl, w)
        return proj[:, :128].astype(BF), flip(proj[:, 128:].astype(BF).astype(F32) * temper)
    kv_y, q_y = split(w_s[y])
    px_kv[...] = kv_y
    p_kv = pair(3, px_kv, kv.at[b, mine])
    p_kv.start()
    px_q[...] = q_y[:HEAD].astype(BF)
    p_q = pair(4, px_q, qd_t.at[a, pl.ds(0, HEAD), mine])
    p_q.start()
    kv_x, q_x = split(w_s[x])
    kv[b, mine] = kv_x
    qd_t[a, :HEAD, mine] = q_x[:HEAD].astype(BF)

    def kv_at(p):
        return lambda j: kv.at[j, pl.ds(pl.multiple_of(p * tp, tp), tp)]
    b_send(sr(0), lambda j: kv_at(x)(b), kv_at(x))
    p_kv.wait_recv()
    b_send(sr(1), lambda j: kv_at(y)(b), kv_at(y))
    p_q.wait_recv()

    def q_at(j):
        return qd_t.at[j, pl.ds(0, HEAD)]
    a_send(sr(10), lambda j: q_at(a), q_at)

    lane = lax.broadcasted_iota(jnp.int32, (T, 128), 1)
    zero = jnp.zeros((T, 128), BF)

    def prep_kv(s):
        v = kv[s]
        kv_t[s] = flip(v).astype(BF)
        k_m[s] = jnp.where(lane < HEAD, v, zero)
        v_m[s] = jnp.where(lane >= HEAD, v, zero)

    def prep_qd(s):
        v = flip(qd_t[s]).astype(BF)
        q_m[s] = jnp.where(lane < HEAD, v, zero)
        d_m[s] = jnp.where(lane >= HEAD, v, zero)

    prep_kv(b)
    prep_qd(a)

    def kv_next(i):
        b_wait(sr(0), kv_at(x), i)
        prep_kv(b_wait(sr(1), kv_at(y), i))
    loop(B, kv_next)

    def qd_next(i):
        a_wait(sr(9), d_at, i)
        prep_qd(a_wait(sr(10), q_at, i))
    loop(A, qd_next)

    def fwd_q(qi):
        qs = qd_t[qi]
        ss = [mm(k_m[kj], qs) for kj in range(B)]
        top = functools.reduce(
            jnp.maximum, [jnp.max(v, axis=0, keepdims=True) for v in ss])
        ps = [jnp.exp(v - top) for v in ss]
        total = sum(jnp.sum(p, axis=0, keepdims=True) for p in ps)
        acc = sum(mm(kv_t[kj, HEAD:, :], p.astype(BF)) for kj, p in enumerate(ps))
        o_s[qi] = (acc / total).astype(BF)
        lse_s[qi] = jnp.broadcast_to(top + jnp.log(total), lse_s.shape[1:])

    def fwd_one(i):
        qi = lax.rem(a + i, A)
        fwd_q(qi)
        a_one(sr(2), o_s.at[qi], lambda j: o_r.at[j], qi)
        a_one(sr(3), lse_s.at[qi], lambda j: lse_r.at[j], qi)
    loop(A, fwd_one)
    fwd_q(a)
    o_r[a] = o_s[a]
    lse_r[a] = lse_s[a]
    loop(A, lambda i: (a_wait(sr(2), lambda s: o_r.at[s], i),
                       a_wait(sr(3), lambda s: lse_r.at[s], i)))

    lses = [lse_r[s, 0:1, :] for s in range(A)]
    top = functools.reduce(jnp.maximum, lses)
    lse = top + jnp.log(sum(jnp.exp(v - top) for v in lses))
    o_t = sum(jnp.exp(v - lse) * o_r[s].astype(F32) for s, v in enumerate(lses)).astype(BF)
    delta = jnp.sum(qd_t[a, HEAD:, :].astype(F32) * o_t.astype(F32), axis=0, keepdims=True)
    st[a] = jnp.concatenate([lse, delta, jnp.zeros((6, T), F32)], axis=0)
    a_send(sr(4), lambda j: st.at[a], lambda j: st.at[j])

    att_s[:, :HEAD] = flip(o_t).astype(BF)
    att_s[:, HEAD:] = jnp.zeros((T, 128 - HEAD), BF)
    p_att = pair(5, plane(att_s, y), att_r)
    p_att.start()
    g_t[3 * HEAD:, :] = mm(o_t, og[...])
    loop(A, lambda i: a_wait(sr(4), lambda s: st.at[s], i))

    def tile(kj, qi):
        qs = qd_t[qi]
        p = jnp.exp(mm(k_m[kj], qs) - st[qi, 0:1, :])
        ds = (p * (mm(v_m[kj], qs) - st[qi, 1:2, :])).astype(BF)
        dkv_acc[kj] += mm(ds, q_m[qi]) + mm(p.astype(BF), d_m[qi])
        dq_acc[qi] += mm(kv_t[kj, :HEAD, :], ds)

    def bwd_one(i):
        kj = lax.rem(b + i, B)

        def two(h, t0):
            tile(kj, lax.rem(a + 2 * h, A))
            tile(kj, lax.rem(a + 2 * h + 1, A))
            return t0
        lax.fori_loop(0, A // 2, two, 0)
        dkv_s[kj] = dkv_acc[kj].astype(BF)
        b_one(sr(5), dkv_s.at[kj], lambda j: dkv_r.at[j], kj)

        @pl.when(i == 1)
        def _():
            p_att.wait_recv()
            p_norm.start()
            p_out.wait_recv()
            rs2_s[...] = (mm(plane(att_s, x)[:, :HEAD], my_out[...])
                          + mm(att_r[:, :HEAD], blk(out_p, y, HEAD)[...])).astype(BF)
            rs_start(2, rs2_s, rs2_r)

        @pl.when(i == min(2, B - 1))
        def _():
            rs_mid(2, rs2_s, rs2_r, rs2_m)
    p_norm = pair(6, plane(normed, x), plane(normed, x))
    loop(B, bwd_one)

    mixed = reduce_z(2, rs2_s, rs2_r)
    own(co_o)[...] = (coarse_s[...] + mixed).astype(BF)
    ag_start(5, own_at(co_o))

    for i in range(1, A + 1):
        qi = lax.rem(a + i, A)
        tile(b, qi)
        if i < A:
            dq_s[qi] = dq_acc[qi].astype(BF)
            a_one(sr(6), dq_s.at[qi], lambda j: dq_r.at[j], qi)

    ag_mid(5, own_at(co_o))

    def dkv_sum(i, acc):
        s = b_wait(sr(5), lambda q: dkv_r.at[q], i)
        return acc + dkv_r[s].astype(F32)
    dkv = lax.fori_loop(1, B, dkv_sum, dkv_acc[b]).astype(BF)

    def dq_sum(i, acc):
        s = a_wait(sr(6), lambda q: dq_r.at[q], i)
        return acc + dq_r[s].astype(F32)
    dq_t = (lax.fori_loop(1, A, dq_sum, dq_acc[a]) * temper).astype(BF)

    dp_s[:, :128] = dkv
    dp_s[:, 128:] = jnp.concatenate([flip(dq_t).astype(BF), jnp.zeros((T, HEAD), BF)], axis=1)
    p_dp = pair(7, plane(dp_s, y), dp_r)
    p_dp.start()
    part = mm(plane(dp_s, x)[...], w_t[x])
    p_dp.wait_recv()
    rs3_s[...] = (part + mm(dp_r[...], w_t[y])).astype(BF)
    rs_start(3, rs3_s, rs3_r)

    ag_end(5, own_at(co_o))
    p_co = pair(8, plane(co_o, x), plane(co_o, x))
    p_co.start()

    p_norm.wait_recv()
    rs_mid(3, rs3_s, rs3_r, rs3_m)
    g_t[:2 * HEAD, :] = mm(flip(dkv).astype(BF), normed[...])
    g_t[2 * HEAD:3 * HEAD, :] = mm(dq_t, normed[...])
    g_s[...] = g_t[...].T.astype(BF)
    gb = D // R

    def g_rows(j):
        return blk(g_s, j, gb)
    row_send(sr(7), g_rows, lambda j: g_r.at[j])

    ncot = reduce_z(3, rs3_s, rs3_r)
    coarse = coarse_s[...]
    inv = inv_s[:, :1]
    gpart = jnp.sum(ncot * coarse * inv, axis=0, keepdims=True)
    scaled = ncot * gain_f
    ccot = own(og)[...].astype(F32) + inv * scaled - coarse * (inv * inv * inv) * jnp.mean(
        scaled * coarse, axis=-1, keepdims=True)
    zrow(cc, z)[...] = ccot.astype(BF)

    def cc_at(j):
        return zrow(cc, j)
    ag_start(4, cc_at)
    gp = jnp.concatenate([gpart[:, i * 128:(i + 1) * 128] for i in range(D // 128)], axis=0)
    gn_s[...] = gp
    gn_r[c] = gp
    col_send(sc(1), lambda j: gn_s, lambda j: gn_r.at[j])

    ag_mid(4, cc_at)

    def g_sum(i, acc):
        s = row_wait(sr(7), lambda q: g_r.at[q], i)
        return acc + g_r[s].astype(F32)
    g_all = lax.fori_loop(1, R, g_sum, g_rows(r)[...].astype(F32))
    for k in range(3):
        qg_o[k] = g_all[:, (k + 2) % 3 * HEAD:(k + 2) % 3 * HEAD + HEAD]
    opg_o[...] = g_all[:, 3 * HEAD:].T

    m_t = [flip(merged[:, k * 128:(k + 1) * 128]).astype(BF) for k in range(2)]
    p_co.wait_recv()
    co_out = pltpu.make_async_copy(co_o, co_h, s_in.at[5])
    co_out.start()
    ag_end(4, cc_at)
    for k in range(2):
        dn_s[k] = mm(m_t[k], cc[...]).T.astype(BF)

    def dn_src(j):
        return dn_s.at[lax.rem(j, 2), pl.ds(pl.multiple_of(lax.div(j, 2) * gb, gb), gb)]
    sd = (s_d, r_d)
    d_send(sd, dn_src, lambda j: dn_r.at[j])

    mg_s[...] = mm_nt(cc[...], blk(down_p, y, ch)[...]).astype(BF)
    p_mg = pair(9, mg_s, plane(mg_o, x))
    p_mg.start()
    loop(C, lambda i: col_wait(sc(1), lambda s: gn_r.at[s], i))
    gt = jnp.sum(gn_r[...], axis=0)
    gt_s[...] = gt
    gt_r[r] = gt
    row_send(sr(8), lambda j: gt_s, lambda j: gt_r.at[j])
    plane(mg_o, x)[...] = mm_nt(cc[...], my_down[...]).astype(BF)

    def d_sum(i, acc):
        s = d_wait(sd, lambda q: dn_r.at[q], i)
        return acc + dn_r[s].astype(F32)
    dg_o[...] = lax.fori_loop(1, 2 * R, d_sum, dn_src(r * 2 + x)[...].astype(F32))

    loop(R, lambda i: row_wait(sr(8), lambda s: gt_r.at[s], i))
    gsum[...] = jnp.sum(gt_r[...], axis=0)
    g_row = gsum[pl.ds(lax.div(r, 2), 1), :]
    gg_o[...] = jnp.where(lax.rem(r, 2) == 0, g_row[:, :64], g_row[:, 64:])

    p_mg.wait_recv()
    co_out.wait()
    for p in (p_down, p_w, p_out, p_kv, p_q, p_att, p_norm, p_dp, p_co, p_mg):
        p.wait_send()
    col_done(sc(0), a2a_src)
    col_done(sc(1), lambda j: gn_s)
    rs_done(0, rs1_s, rs1_r)
    rs_done(2, rs2_s, rs2_r)
    rs_done(3, rs3_s, rs3_r)
    ag_done(1, own_at(normed))
    ag_done(4, cc_at)
    ag_done(5, own_at(co_o))
    b_done(sr(0), lambda j: kv_at(x)(b))
    b_done(sr(1), lambda j: kv_at(y)(b))
    a_done(sr(9), lambda j: d_at(a))
    a_done(sr(10), lambda j: q_at(a))
    a_done(sr(2), lambda j: o_s.at[j])
    a_done(sr(3), lambda j: lse_s.at[j])
    a_done(sr(4), lambda j: st.at[a])
    b_done(sr(5), lambda j: dkv_s.at[j])
    a_done(sr(6), lambda j: dq_s.at[j])
    row_done(sr(7), g_rows)
    row_done(sr(8), lambda j: gt_s)
    d_done(sd, dn_src)


def body(R, C, fine_tiles, out_grad, down_proj, qkv_proj, out_proj, norm_gain):
    A = 2 ** ((R.bit_length() - 1) // 2)
    B = R // A
    D = out_grad.shape[-1]
    th, tw = out_grad.shape[0], out_grad.shape[1]
    T = th * tw
    Z = C // 2
    tp = T // 2
    tb = tp // Z
    H8, W16, D2 = fine_tiles.shape
    ch = down_proj.shape[0]
    gb = D // R
    V = pltpu.VMEM
    S = pltpu.SemaphoreType.DMA
    scratch = [
        V((T, D), BF), V((T, D), BF),
        V((D2 // 128, H8, W16, 128), F32), V((C, 32, 128), BF), V((C, 2, 16, 128), BF),
        V((tp, 2 * ch), BF), V((2 * ch, D), BF), V((2, D, 4 * HEAD), BF), V((2, 4 * HEAD, D), BF),
        V((2 * HEAD, D), BF),
        V((tp, D), BF), V((Z, tb, D), BF), V((2, tb, D), BF), V((tb, D), F32), V((tb, 128), F32),
        V((T, D), BF), V((tp, 128), BF), V((HEAD, tp), BF),
        V((B, T, 128), BF),
        V((B, 128, T), BF), V((A, 128, T), BF), V((B, T, 128), BF), V((B, T, 128), BF),
        V((A, T, 128), BF), V((A, T, 128), BF),
        V((A, HEAD, T), BF), V((A, HEAD, T), BF), V((A, 8, T), F32), V((A, 8, T), F32),
        V((A, 8, T), F32), V((T, 128), BF), V((tp, 128), BF),
        V((tp, D), BF), V((Z, tb, D), BF), V((2, tb, D), BF),
        V((B, T, 128), F32), V((B, T, 128), BF), V((B, T, 128), BF),
        V((A, HEAD, T), F32), V((A, HEAD, T), BF), V((A, HEAD, T), BF),
        V((T, 4 * HEAD), BF), V((tp, 4 * HEAD), BF),
        V((tp, D), BF), V((Z, tb, D), BF), V((2, tb, D), BF),
        V((4 * HEAD, D), F32), V((D, 4 * HEAD), BF), V((R, gb, 4 * HEAD), BF),
        V((tp, D), BF), V((D // 128, 128), F32), V((C, D // 128, 128), F32),
        V((D // 128, 128), F32), V((R, D // 128, 128), F32), V((D // 128, 128), F32),
        V((tp, ch), BF), V((2, D, ch), BF), V((2 * R, gb, ch), BF),
        S((2, C)), S((2, C)), S((6, Z)), S((6, Z)), S((10,)), S((10,)),
        S((11, R)), S((11, R)), S((2 * R,)), S((2 * R,)), S((6,)),
    ]
    vm = pl.BlockSpec(memory_space=pltpu.VMEM)
    hb = pl.BlockSpec(memory_space=pl.ANY)
    outs = pl.pallas_call(
        functools.partial(kernel, R, C, A),
        out_shape=(
            jax.ShapeDtypeStruct((T, D), BF),
            jax.ShapeDtypeStruct((T, ch), BF),
            jax.ShapeDtypeStruct((gb, ch), F32),
            jax.ShapeDtypeStruct((3, gb, HEAD), F32),
            jax.ShapeDtypeStruct((HEAD, gb), F32),
            jax.ShapeDtypeStruct((1, gb), F32),
        ),
        in_specs=[vm, hb, hb, hb, hb, vm],
        out_specs=(hb,) + (vm,) * 5,
        scratch_shapes=scratch,
        compiler_params=pltpu.CompilerParams(
            collective_id=0, has_side_effects=True, vmem_limit_bytes=56 * 1024 * 1024),
        name="block",
    )(fine_tiles, out_grad.reshape(T, D), down_proj, qkv_proj.transpose(1, 2, 0).reshape(3 * HEAD, D), out_proj,
      norm_gain.reshape(1, D))
    co, mg, dg, qg, opg, gg = outs
    return (co.reshape(th, tw, D), mg.reshape(th, tw, ch), dg.T, qg.transpose(1, 0, 2), opg,
            gg.reshape(gb))


def solution(mesh):
    R, C = mesh.shape["row"], mesh.shape["col"]
    return jax.shard_map(
        functools.partial(body, R, C),
        mesh=mesh,
        in_specs=(P("row", "col", None), P("row", None, None), P("col", None),
                  P(None, None, "col"), P("col", None), P()),
        out_specs=(P("row", None, None), P("row", None, "col"), P("col", "row"),
                   P("row", None, "col"), P("col", "row"), P("row")),
        check_vma=False,
    )
```

```python
import functools

import jax
import jax.numpy as jnp
from jax import lax
from jax.experimental import pallas as pl
from jax.experimental.pallas import tpu as pltpu
from jax.sharding import PartitionSpec as P

HEAD = 64
EPSILON = 1e-06
BF = jnp.bfloat16
F32 = jnp.float32


def mm(x, y):
    return jnp.dot(x, y, preferred_element_type=F32)


def mm_nt(x, y):
    return lax.dot_general(x, y, (((1,), (1,)), ((), ())), preferred_element_type=F32)


def flip(x):
    return x.astype(F32).T


def kernel(R, C, A, *refs):
    (fine, og_h, down_h, qkv_h, outp_h, gain,
     co_h, mg_o, dg_o, qg_o, opg_o, gg_o,
     og, co_o, fine_f, a2a_s, mrecv, merged, down_p, w_s, w_t, out_p,
     rs1_s, rs1_r, rs1_m, coarse_s, inv_s, normed, px_kv, px_q,
     kv, kv_t, qd_t, k_m, v_m, q_m, d_m,
     o_s, o_r, lse_s, lse_r, st, att_s, att_r,
     rs2_s, rs2_r, rs2_m, dkv_acc, dkv_s, dkv_r, dq_acc, dq_s, dq_r, dp_s, dp_r,
     rs3_s, rs3_r, rs3_m, g_t, g_s, g_r, cc, gn_s, gn_r, gt_s, gt_r, gsum, mg_s, dn_s, dn_r,
     s_one, r_one, r_z, s_p, r_p, r_ab, s_in) = refs
    B = R // A
    Z = C // 2
    T, D = og.shape
    core = lax.rem(lax.axis_index("row"), 2)
    tp = T // 2
    tb = tp // Z
    r = lax.axis_index("row")
    c = lax.axis_index("col")
    a = lax.rem(r, A)
    b = lax.div(r, A)
    z = lax.div(c, 2)
    x = lax.rem(c, 2)
    y = 1 - x
    pc = z * 2 + y

    def rcopy(src, dst, ssem, rsem, dev):
        return pltpu.make_async_remote_copy(
            src_ref=src, dst_ref=dst, send_sem=ssem, recv_sem=rsem,
            device_id=dev, device_id_type=pl.DeviceIdType.MESH)

    def blk(ref, j, n):
        return ref.at[pl.ds(pl.multiple_of(j * n, n), n)]

    def zrow(ref, j):
        return blk(ref, j, tb)

    def own(ref):
        return ref.at[pl.ds(pl.multiple_of(x * tp + z * tb, tb), tb)]

    def plane(ref, p):
        return blk(ref, p, tp)

    def loop(n, fn):
        lax.fori_loop(1, n, lambda i, t: (fn(i), t)[1], 0)

    def ring(n, me, dev, near):
        def off(i):
            odd = lax.rem(i, 2)
            return odd * lax.div(i + 1, 2) + (1 - odd) * (n - lax.div(i, 2)) if near else i

        def send_one(sem, src, dst, j):
            rcopy(src, dst(me), sem[0], sem[1](me), dev(j)).start()

        def send(sem, src, dst):
            def one(i):
                j = lax.rem(me + off(i), n)
                send_one(sem, src(j), dst, j)
            loop(n, one)

        def wait(sem, dst, i):
            s = lax.rem(me + n - off(i), n)
            rcopy(dst(s), dst(s), sem[0], sem[1](s), dev(s)).wait_recv()
            return s
        return send_one, send, wait

    def all_sent(sem, size):
        rcopy(size, size, sem[0], sem[1](0), (r, pc)).wait_send()

    def all_here(sem, size):
        rcopy(size, size, sem[0], sem[1](0), (r, pc)).wait_recv()

    _, col_send, _ = ring(C, c, lambda j: (r, j), False)
    _, z_send, z_wait = ring(Z, z, lambda j: (r, j * 2 + x), True)
    _, row_send, _ = ring(R, r, lambda j: (j, c), False)
    a_one, a_send, a_wait = ring(A, a, lambda j: (b * A + j, c), False)
    b_one, b_send, b_wait = ring(B, b, lambda j: (j * A + a, c), False)

    def one(k):
        return s_one.at[k], lambda j: r_one.at[k]

    def sz(k):
        return s_one.at[5 + k], lambda j: r_z.at[k, j]

    def sr(k):
        return s_one.at[12 + k], lambda j: r_ab.at[k, j]

    def zd(d):
        return lax.rem(z + 8 + d, 8)

    def rs_copy(k, src, r_ref, q, d):
        return rcopy(src, r_ref.at[q], s_one.at[5 + k], r_z.at[k, q], (r, zd(d) * 2 + x))

    def rs_start(k, s_ref, r_ref):
        if Z != 8:
            z_send(sz(k), lambda j: zrow(s_ref, j), lambda j: r_ref.at[j])
            return
        rs_copy(k, zrow(s_ref, zd(4)), r_ref, 2, 4 * core - 2).start()
        rs_copy(k, zrow(s_ref, zd(-3)), r_ref, 0, -1).start()
        rs_copy(k, zrow(s_ref, zd(3)), r_ref, 1, 1).start()
        rs_copy(k, zrow(s_ref, zd(-1)), r_ref, 3, -1).start()
        rs_copy(k, zrow(s_ref, zd(1)), r_ref, 4, 1).start()

    def rs_wait(k, r_ref, qs):
        for q in qs:
            rs_copy(k, r_ref.at[q], r_ref, q, 1).wait_recv()

    def rs_mid(k, s_ref, r_ref, m_ref):
        if Z != 8:
            return
        rs_wait(k, r_ref, (0, 1, 2))
        far = r_ref[2].astype(F32)
        none = jnp.zeros_like(far)
        m_ref[0] = (zrow(s_ref, zd(-2))[...].astype(F32) + r_ref[0].astype(F32)
                    + jnp.where(core == 0, far, none)).astype(BF)
        rs_copy(k, m_ref.at[0], r_ref, 5, -2).start()
        m_ref[1] = (zrow(s_ref, zd(2))[...].astype(F32) + r_ref[1].astype(F32)
                    + jnp.where(core == 0, none, far)).astype(BF)
        rs_copy(k, m_ref.at[1], r_ref, 6, 2).start()

    def ag_copy(k, at, s, d):
        return rcopy(at(s), at(s), s_one.at[5 + k], r_z.at[k, s], (r, zd(d) * 2 + x))

    def ag_start(k, at):
        if Z != 8:
            z_send(sz(k), lambda j: at(z), at)
            return
        for d in (2, -2, 1, -1):
            ag_copy(k, at, z, d).start()

    def ag_wait(k, at, ds):
        for d in ds:
            ag_copy(k, at, zd(d), 1).wait_recv()

    def ag_mid(k, at):
        if Z != 8:
            return
        ag_wait(k, at, (-2,))
        ag_copy(k, at, zd(-2), 1).start()
        ag_wait(k, at, (2,))
        ag_copy(k, at, zd(2), -1).start()
        ag_copy(k, at, zd(4 * core - 2), 2 - 4 * core).start()

    def ag_end(k, at):
        if Z != 8:
            loop(Z, lambda i: z_wait(sz(k), at, i))
            return
        ag_wait(k, at, (-1, 1, -3, 3, 4))

    def pair(k, src, dst):
        return rcopy(src, dst, s_p.at[k], r_p.at[k], (r, pc))

    ch = down_h.shape[0]
    my_down = blk(down_p, x, ch)
    my_out = blk(out_p, x, HEAD)
    loads = [
        pltpu.make_async_copy(down_h, my_down, s_in.at[0]),
        pltpu.make_async_copy(outp_h, my_out, s_in.at[1]),
        pltpu.make_async_copy(og_h, og, s_in.at[2]),
        pltpu.make_async_copy(
            qkv_h.at[pl.ds(HEAD, 2 * HEAD)], w_t.at[x, pl.ds(0, 2 * HEAD)], s_in.at[3]),
        pltpu.make_async_copy(
            qkv_h.at[pl.ds(0, HEAD)], w_t.at[x, pl.ds(2 * HEAD, HEAD)], s_in.at[4]),
    ]
    for load in loads:
        load.start()

    barrier = pltpu.get_barrier_semaphore()

    def greet(dev):
        pl.semaphore_signal(barrier, inc=1, device_id=dev, device_id_type=pl.DeviceIdType.MESH)
    loop(C, lambda i: greet((r, lax.rem(c + i, C))))
    loop(R, lambda i: greet((lax.rem(r + i, R), c)))
    loop(R, lambda i: greet((lax.rem(r + i, R), pc)))

    H8, W16, D2 = fine.shape
    n_cb = D2 // 128
    for cb in range(n_cb):
        fine_f[cb] = fine[:, :, cb * 128:(cb + 1) * 128].astype(F32)
    for aa in range(2):
        for bb in range(2):
            for cb in range(n_cb):
                parts = [fine_f[cb, 2 * h + aa, pl.ds(bb, W16 // 2, stride=2), :]
                         for h in range(H8 // 2)]
                a2a_s[(aa * 2 + bb) * n_cb + cb] = jnp.concatenate(parts, axis=0).astype(BF)

    def a2a_src(j):
        return a2a_s.at[pl.ds(lax.div(j, 2) * 2, 2), pl.ds(pl.multiple_of(lax.rem(j, 2) * 16, 16), 16)]

    pl.semaphore_wait(barrier, C + 2 * R - 3)
    col_send(one(0), a2a_src, lambda j: mrecv.at[j])
    loads[0].wait()
    p_down = pair(0, my_down, my_down)
    p_down.start()

    mrecv[c] = a2a_src(c)[...]
    loads[1].wait()
    loads[2].wait()
    qd_t[a, HEAD:, :] = mm_nt(my_out[...], og[...]).astype(BF)

    def d_at(j):
        return qd_t.at[j, pl.ds(HEAD, HEAD)]
    a_send(sr(7), lambda j: d_at(a), d_at)
    for k in range(2):
        w_t[k, 3 * HEAD:, :] = jnp.zeros((HEAD, D), BF)
    loads[3].wait()
    loads[4].wait()

    all_here(one(0), mrecv.at[pl.ds(0, C - 1)])
    for k in range(2):
        mr = mrecv[:, k].astype(F32).reshape(C, 2, W16 // 2, 128)
        merged[:, k * 128:(k + 1) * 128] = jnp.swapaxes(mr, 0, 1).reshape(tp, 128).astype(BF)
    p_down.wait_recv()

    rs1_s[...] = mm(merged[...], down_p[...]).astype(BF)
    rs_start(0, rs1_s, rs1_r)
    p_w = pair(1, w_t.at[x, pl.ds(0, 3 * HEAD)], w_t.at[x, pl.ds(0, 3 * HEAD)])
    p_w.start()
    p_out = pair(2, my_out, my_out)
    p_out.start()
    w_s[x] = flip(w_t[x]).astype(BF)
    rs_mid(0, rs1_s, rs1_r, rs1_m)
    dkv_acc[...] = jnp.zeros(dkv_acc.shape, F32)
    dq_acc[...] = jnp.zeros(dq_acc.shape, F32)

    def reduce_z(k, s_ref, r_ref):
        if Z == 8:
            rs_wait(k, r_ref, (3, 4, 5, 6))
            acc = zrow(s_ref, z)[...].astype(F32)
            for q in (3, 4, 5, 6):
                acc = acc + r_ref[q].astype(F32)
            return acc

        def one(i, acc):
            s = z_wait(sz(k), lambda q: r_ref.at[q], i)
            return acc + r_ref[s].astype(F32)
        return lax.fori_loop(1, Z, one, zrow(s_ref, z)[...].astype(F32))

    coarse = reduce_z(0, rs1_s, rs1_r).astype(BF).astype(F32)
    coarse_s[...] = coarse
    inv = lax.rsqrt(jnp.mean(coarse * coarse, axis=-1, keepdims=True) + EPSILON)
    inv_s[...] = jnp.broadcast_to(inv, inv_s.shape)
    gain_f = gain[...].astype(F32)
    own(normed)[...] = (coarse * inv * gain_f).astype(BF)

    def own_at(ref):
        return lambda j: ref.at[pl.ds(pl.multiple_of(x * tp + j * tb, tb), tb)]
    ag_start(1, own_at(normed))
    ag_mid(1, own_at(normed))
    p_w.wait_recv()
    w_s[y] = flip(w_t[y]).astype(BF)
    ag_end(1, own_at(normed))

    temper = HEAD ** (-0.5)
    n_pl = plane(normed, x)[...]
    mine = pl.ds(pl.multiple_of(x * tp, tp), tp)

    def split(w):
        proj = mm(n_pl, w)
        return proj[:, :128].astype(BF), flip(proj[:, 128:].astype(BF).astype(F32) * temper)
    kv_y, q_y = split(w_s[y])
    px_kv[...] = kv_y
    p_kv = pair(3, px_kv, kv.at[b, mine])
    p_kv.start()
    px_q[...] = q_y[:HEAD].astype(BF)
    p_q = pair(4, px_q, qd_t.at[a, pl.ds(0, HEAD), mine])
    p_q.start()
    kv_x, q_x = split(w_s[x])
    kv[b, mine] = kv_x
    qd_t[a, :HEAD, mine] = q_x[:HEAD].astype(BF)

    def kv_at(p):
        return lambda j: kv.at[j, pl.ds(pl.multiple_of(p * tp, tp), tp)]
    b_send(sr(0), lambda j: kv_at(x)(b), kv_at(x))
    p_kv.wait_recv()
    b_send(sr(1), lambda j: kv_at(y)(b), kv_at(y))
    p_q.wait_recv()

    def q_at(j):
        return qd_t.at[j, pl.ds(0, HEAD)]
    a_send(sr(8), lambda j: q_at(a), q_at)

    lane = lax.broadcasted_iota(jnp.int32, (T, 128), 1)
    zero = jnp.zeros((T, 128), BF)

    def prep_kv(s):
        v = kv[s]
        kv_t[s] = flip(v).astype(BF)
        k_m[s] = jnp.where(lane < HEAD, v, zero)
        v_m[s] = jnp.where(lane >= HEAD, v, zero)

    def prep_qd(s):
        v = flip(qd_t[s]).astype(BF)
        q_m[s] = jnp.where(lane < HEAD, v, zero)
        d_m[s] = jnp.where(lane >= HEAD, v, zero)

    prep_kv(b)
    prep_qd(a)

    def kv_next(i):
        b_wait(sr(0), kv_at(x), i)
        prep_kv(b_wait(sr(1), kv_at(y), i))
    loop(B, kv_next)

    def qd_next(i):
        a_wait(sr(7), d_at, i)
        prep_qd(a_wait(sr(8), q_at, i))
    loop(A, qd_next)

    def fwd_q(qi):
        qs = qd_t[qi]
        ss = [mm(k_m[kj], qs) for kj in range(B)]
        top = functools.reduce(
            jnp.maximum, [jnp.max(v, axis=0, keepdims=True) for v in ss])
        ps = [jnp.exp(v - top) for v in ss]
        total = sum(jnp.sum(p, axis=0, keepdims=True) for p in ps)
        acc = sum(mm(kv_t[kj, HEAD:, :], p.astype(BF)) for kj, p in enumerate(ps))
        o_s[qi] = (acc / total).astype(BF)
        lse_s[qi] = jnp.broadcast_to(top + jnp.log(total), lse_s.shape[1:])

    def fwd_one(i):
        qi = lax.rem(a + i, A)
        fwd_q(qi)
        a_one(sr(2), o_s.at[qi], lambda j: o_r.at[j], qi)
        a_one(sr(3), lse_s.at[qi], lambda j: lse_r.at[j], qi)
    loop(A, fwd_one)
    fwd_q(a)
    o_r[a] = o_s[a]
    lse_r[a] = lse_s[a]
    loop(A, lambda i: (a_wait(sr(2), lambda s: o_r.at[s], i),
                       a_wait(sr(3), lambda s: lse_r.at[s], i)))

    lses = [lse_r[s, 0:1, :] for s in range(A)]
    top = functools.reduce(jnp.maximum, lses)
    lse = top + jnp.log(sum(jnp.exp(v - top) for v in lses))
    o_t = sum(jnp.exp(v - lse) * o_r[s].astype(F32) for s, v in enumerate(lses)).astype(BF)
    delta = jnp.sum(qd_t[a, HEAD:, :].astype(F32) * o_t.astype(F32), axis=0, keepdims=True)
    st[a] = jnp.concatenate([lse, delta, jnp.zeros((6, T), F32)], axis=0)
    a_send(sr(4), lambda j: st.at[a], lambda j: st.at[j])

    att_s[:, :HEAD] = flip(o_t).astype(BF)
    att_s[:, HEAD:] = jnp.zeros((T, 128 - HEAD), BF)
    p_att = pair(5, plane(att_s, y), att_r)
    p_att.start()
    g_t[3 * HEAD:, :] = mm(o_t, og[...])
    loop(A, lambda i: a_wait(sr(4), lambda s: st.at[s], i))

    def tile(kj, qi):
        qs = qd_t[qi]
        p = jnp.exp(mm(k_m[kj], qs) - st[qi, 0:1, :])
        ds = (p * (mm(v_m[kj], qs) - st[qi, 1:2, :])).astype(BF)
        dkv_acc[kj] += mm(ds, q_m[qi]) + mm(p.astype(BF), d_m[qi])
        dq_acc[qi] += mm(kv_t[kj, :HEAD, :], ds)

    def bwd_one(i):
        kj = lax.rem(b + i, B)

        def two(h, t0):
            tile(kj, lax.rem(a + 2 * h, A))
            tile(kj, lax.rem(a + 2 * h + 1, A))
            return t0
        lax.fori_loop(0, A // 2, two, 0)
        dkv_s[kj] = dkv_acc[kj].astype(BF)
        b_one(sr(5), dkv_s.at[kj], lambda j: dkv_r.at[j], kj)

        @pl.when(i == 1)
        def _():
            p_att.wait_recv()
            p_norm.start()
            p_out.wait_recv()
            rs2_s[...] = (mm(plane(att_s, x)[:, :HEAD], my_out[...])
                          + mm(att_r[:, :HEAD], blk(out_p, y, HEAD)[...])).astype(BF)
            rs_start(2, rs2_s, rs2_r)

        @pl.when(i == min(2, B - 1))
        def _():
            rs_mid(2, rs2_s, rs2_r, rs2_m)
    p_norm = pair(6, plane(normed, x), plane(normed, x))
    loop(B, bwd_one)

    mixed = reduce_z(2, rs2_s, rs2_r)
    own(co_o)[...] = (coarse_s[...] + mixed).astype(BF)
    ag_start(5, own_at(co_o))

    for i in range(1, A + 1):
        qi = lax.rem(a + i, A)
        tile(b, qi)
        if i < A:
            dq_s[qi] = dq_acc[qi].astype(BF)
            a_one(sr(6), dq_s.at[qi], lambda j: dq_r.at[j], qi)

    ag_mid(5, own_at(co_o))

    def dkv_sum(i, acc):
        s = b_wait(sr(5), lambda q: dkv_r.at[q], i)
        return acc + dkv_r[s].astype(F32)
    dkv = lax.fori_loop(1, B, dkv_sum, dkv_acc[b]).astype(BF)

    def dq_sum(i, acc):
        s = a_wait(sr(6), lambda q: dq_r.at[q], i)
        return acc + dq_r[s].astype(F32)
    dq_t = (lax.fori_loop(1, A, dq_sum, dq_acc[a]) * temper).astype(BF)

    dp_s[:, :128] = dkv
    dp_s[:, 128:] = jnp.concatenate([flip(dq_t).astype(BF), jnp.zeros((T, HEAD), BF)], axis=1)
    p_dp = pair(7, plane(dp_s, y), dp_r)
    p_dp.start()
    part = mm(plane(dp_s, x)[...], w_t[x])
    p_dp.wait_recv()
    rs3_s[...] = (part + mm(dp_r[...], w_t[y])).astype(BF)
    rs_start(3, rs3_s, rs3_r)

    ag_end(5, own_at(co_o))
    p_co = pair(8, plane(co_o, x), plane(co_o, x))
    p_co.start()

    p_norm.wait_recv()
    rs_mid(3, rs3_s, rs3_r, rs3_m)
    g_t[:2 * HEAD, :] = mm(flip(dkv).astype(BF), normed[...])
    g_t[2 * HEAD:3 * HEAD, :] = mm(dq_t, normed[...])
    g_s[...] = g_t[...].T.astype(BF)
    gb = D // R

    def g_rows(j):
        return blk(g_s, j, gb)
    row_send(one(2), g_rows, lambda j: g_r.at[j])

    ncot = reduce_z(3, rs3_s, rs3_r)
    coarse = coarse_s[...]
    inv = inv_s[:, :1]
    gpart = jnp.sum(ncot * coarse * inv, axis=0, keepdims=True)
    scaled = ncot * gain_f
    ccot = own(og)[...].astype(F32) + inv * scaled - coarse * (inv * inv * inv) * jnp.mean(
        scaled * coarse, axis=-1, keepdims=True)
    zrow(cc, z)[...] = ccot.astype(BF)
    hw = D // 2

    def cc_at(h):
        return lambda j: cc.at[pl.ds(pl.multiple_of(j * tb, tb), tb), pl.ds(h * hw, hw)]
    ag_start(4, cc_at(0))
    ag_mid(4, cc_at(0))
    ag_start(6, cc_at(1))
    gp = jnp.concatenate([gpart[:, i * 128:(i + 1) * 128] for i in range(D // 128)], axis=0)
    gn_s[...] = gp
    gn_r[c] = gp
    col_send(one(1), lambda j: gn_s, lambda j: gn_r.at[j])

    ag_mid(6, cc_at(1))

    def g_sum(i, acc):
        return acc + g_r[lax.rem(r + i, R)].astype(F32)
    all_here(one(2), g_r.at[pl.ds(0, R - 1)])
    g_all = lax.fori_loop(1, R, g_sum, g_rows(r)[...].astype(F32))
    for k in range(3):
        qg_o[k] = g_all[:, (k + 2) % 3 * HEAD:(k + 2) % 3 * HEAD + HEAD]
    opg_o[...] = g_all[:, 3 * HEAD:].T

    m_t = [flip(merged[:, k * 128:(k + 1) * 128]).astype(BF) for k in range(2)]
    p_co.wait_recv()
    co_out = pltpu.make_async_copy(co_o, co_h, s_in.at[5])
    co_out.start()
    me = r * 2 + x

    def dn_src(j):
        return dn_s.at[lax.rem(j, 2), pl.ds(pl.multiple_of(lax.div(j, 2) * gb, gb), gb)]
    for h in range(2):
        ag_end(4 + 2 * h, cc_at(h))
        for k in range(2):
            dn_s[k, h * hw:(h + 1) * hw, :] = mm(
                m_t[k], cc[:, h * hw:(h + 1) * hw]).T.astype(BF)

        def dn_one(i, t0):
            j = h * R + lax.rem(i + me, R)

            @pl.when(j != me)
            def _():
                rcopy(dn_src(j), dn_r.at[me], s_one.at[4], r_one.at[4],
                      (lax.div(j, 2), z * 2 + lax.rem(j, 2))).start()
            return t0
        lax.fori_loop(0, R, dn_one, 0)

    mg_s[...] = mm_nt(cc[...], blk(down_p, y, ch)[...]).astype(BF)
    p_mg = pair(9, mg_s, plane(mg_o, x))
    p_mg.start()
    all_here(one(1), gn_r.at[pl.ds(0, C - 1)])
    gt = jnp.sum(gn_r[...], axis=0)
    gt_s[...] = gt
    gt_r[r] = gt
    row_send(one(3), lambda j: gt_s, lambda j: gt_r.at[j])
    plane(mg_o, x)[...] = mm_nt(cc[...], my_down[...]).astype(BF)

    def d_sum(i, acc):
        return acc + dn_r[lax.rem(me + i, 2 * R)].astype(F32)
    all_here(one(4), dn_r.at[pl.ds(0, 2 * R - 1)])
    dg_o[...] = lax.fori_loop(1, 2 * R, d_sum, dn_src(me)[...].astype(F32))

    all_here(one(3), gt_r.at[pl.ds(0, R - 1)])
    gsum[...] = jnp.sum(gt_r[...], axis=0)
    g_row = gsum[pl.ds(lax.div(r, 2), 1), :]
    gg_o[...] = jnp.where(lax.rem(r, 2) == 0, g_row[:, :64], g_row[:, 64:])

    p_mg.wait_recv()
    co_out.wait()
    for p in (p_down, p_w, p_out, p_kv, p_q, p_att, p_norm, p_dp, p_co, p_mg):
        p.wait_send()
    all_sent(one(0), mrecv.at[pl.ds(0, C - 1)])
    all_sent(one(1), gn_r.at[pl.ds(0, C - 1)])
    all_sent(one(2), g_r.at[pl.ds(0, R - 1)])
    all_sent(one(3), gt_r.at[pl.ds(0, R - 1)])
    all_sent(one(4), dn_r.at[pl.ds(0, 2 * R - 1)])
    for k in (0, 1, 2, 3, 5):
        all_sent(sz(k), rs1_r.at[pl.ds(0, Z - 1)])
    for k in (4, 6):
        all_sent(sz(k), rs1_r.at[pl.ds(0, Z - 1), :, pl.ds(0, hw)])
    for k in (0, 1):
        all_sent(sr(k), kv.at[pl.ds(0, B - 1), pl.ds(0, tp)])
    for k in (7, 8, 2, 6):
        all_sent(sr(k), o_s.at[pl.ds(0, A - 1)])
    for k in (3, 4):
        all_sent(sr(k), st.at[pl.ds(0, A - 1)])
    all_sent(sr(5), dkv_s.at[pl.ds(0, B - 1)])


def body(R, C, fine_tiles, out_grad, down_proj, qkv_proj, out_proj, norm_gain):
    A = 2 ** ((R.bit_length() - 1) // 2)
    B = R // A
    D = out_grad.shape[-1]
    th, tw = out_grad.shape[0], out_grad.shape[1]
    T = th * tw
    Z = C // 2
    tp = T // 2
    tb = tp // Z
    H8, W16, D2 = fine_tiles.shape
    ch = down_proj.shape[0]
    gb = D // R
    V = pltpu.VMEM
    S = pltpu.SemaphoreType.DMA
    scratch = [
        V((T, D), BF), V((T, D), BF),
        V((D2 // 128, H8, W16, 128), F32), V((C, 32, 128), BF), V((C, 2, 16, 128), BF),
        V((tp, 2 * ch), BF), V((2 * ch, D), BF), V((2, D, 4 * HEAD), BF), V((2, 4 * HEAD, D), BF),
        V((2 * HEAD, D), BF),
        V((tp, D), BF), V((Z, tb, D), BF), V((2, tb, D), BF), V((tb, D), F32), V((tb, 128), F32),
        V((T, D), BF), V((tp, 128), BF), V((HEAD, tp), BF),
        V((B, T, 128), BF),
        V((B, 128, T), BF), V((A, 128, T), BF), V((B, T, 128), BF), V((B, T, 128), BF),
        V((A, T, 128), BF), V((A, T, 128), BF),
        V((A, HEAD, T), BF), V((A, HEAD, T), BF), V((A, 8, T), F32), V((A, 8, T), F32),
        V((A, 8, T), F32), V((T, 128), BF), V((tp, 128), BF),
        V((tp, D), BF), V((Z, tb, D), BF), V((2, tb, D), BF),
        V((B, T, 128), F32), V((B, T, 128), BF), V((B, T, 128), BF),
        V((A, HEAD, T), F32), V((A, HEAD, T), BF), V((A, HEAD, T), BF),
        V((T, 4 * HEAD), BF), V((tp, 4 * HEAD), BF),
        V((tp, D), BF), V((Z, tb, D), BF), V((2, tb, D), BF),
        V((4 * HEAD, D), F32), V((D, 4 * HEAD), BF), V((R, gb, 4 * HEAD), BF),
        V((tp, D), BF), V((D // 128, 128), F32), V((C, D // 128, 128), F32),
        V((D // 128, 128), F32), V((R, D // 128, 128), F32), V((D // 128, 128), F32),
        V((tp, ch), BF), V((2, D, ch), BF), V((2 * R, gb, ch), BF),
        S((21,)), S((5,)), S((7, Z)), S((10,)), S((10,)), S((9, max(A, B))), S((6,)),
    ]
    vm = pl.BlockSpec(memory_space=pltpu.VMEM)
    hb = pl.BlockSpec(memory_space=pl.ANY)
    outs = pl.pallas_call(
        functools.partial(kernel, R, C, A),
        out_shape=(
            jax.ShapeDtypeStruct((T, D), BF),
            jax.ShapeDtypeStruct((T, ch), BF),
            jax.ShapeDtypeStruct((gb, ch), F32),
            jax.ShapeDtypeStruct((3, gb, HEAD), F32),
            jax.ShapeDtypeStruct((HEAD, gb), F32),
            jax.ShapeDtypeStruct((1, gb), F32),
        ),
        in_specs=[vm, hb, hb, hb, hb, vm],
        out_specs=(hb,) + (vm,) * 5,
        scratch_shapes=scratch,
        compiler_params=pltpu.CompilerParams(
            collective_id=0, has_side_effects=True, vmem_limit_bytes=56 * 1024 * 1024),
        name="block",
    )(fine_tiles, out_grad.reshape(T, D), down_proj, qkv_proj.transpose(1, 2, 0).reshape(3 * HEAD, D), out_proj,
      norm_gain.reshape(1, D))
    co, mg, dg, qg, opg, gg = outs
    return (co.reshape(th, tw, D), mg.reshape(th, tw, ch), dg.T, qg.transpose(1, 0, 2), opg,
            gg.reshape(gb))


def solution(mesh):
    R, C = mesh.shape["row"], mesh.shape["col"]
    return jax.shard_map(
        functools.partial(body, R, C),
        mesh=mesh,
        in_specs=(P("row", "col", None), P("row", None, None), P("col", None),
                  P(None, None, "col"), P("col", None), P()),
        out_specs=(P("row", None, None), P("row", None, "col"), P("col", "row"),
                   P("row", None, "col"), P("col", "row"), P("row")),
        check_vma=False,
    )
```

```python
import functools

import jax
import jax.numpy as jnp
from jax import lax
from jax.experimental import pallas as pl
from jax.experimental.pallas import tpu as pltpu
from jax.sharding import PartitionSpec as P

HEAD = 64
EPSILON = 1e-06
BF = jnp.bfloat16
F32 = jnp.float32


def mm(x, y):
    return jnp.dot(x, y, preferred_element_type=F32)


def mm_nt(x, y):
    return lax.dot_general(x, y, (((1,), (1,)), ((), ())), preferred_element_type=F32)


def flip(x):
    return x.astype(F32).T


def kernel(R, C, A, *refs):
    (fine, og_h, down_h, qkv_h, outp_h, gain,
     co_h, mg_o, dg_o, qg_o, opg_o, gg_o,
     og, co_o, fine_f, a2a_s, mrecv, merged, down_p, w_s, w_t, out_p,
     rs1_s, rs1_r, rs1_m, coarse_s, inv_s, normed, px_kv, px_q,
     kv, kv_t, qd_t, k_m, v_m, q_m, d_m,
     o_s, o_r, lse_s, lse_r, st, att_s, att_r,
     rs2_s, rs2_r, rs2_m, dkv_acc, dkv_s, dkv_r, dq_acc, dq_s, dq_r, dpk_s, dpk_r, dpq_s, dpq_r,
     rs3_s, rs3_r, rs3_m, g_t, g_s, g_r, cc, gn_s, gn_r, gt_s, gt_r, gsum, mg_s, dn_s, dn_r,
     s_one, r_one, r_z, s_p, r_p, r_ab, s_in) = refs
    B = R // A
    Z = C // 2
    T, D = og.shape
    core = lax.rem(lax.axis_index("row"), 2)
    tp = T // 2
    tb = tp // Z
    r = lax.axis_index("row")
    c = lax.axis_index("col")
    a = lax.rem(r, A)
    b = lax.div(r, A)
    z = lax.div(c, 2)
    x = lax.rem(c, 2)
    y = 1 - x
    pc = z * 2 + y

    def rcopy(src, dst, ssem, rsem, dev):
        return pltpu.make_async_remote_copy(
            src_ref=src, dst_ref=dst, send_sem=ssem, recv_sem=rsem,
            device_id=dev, device_id_type=pl.DeviceIdType.MESH)

    def blk(ref, j, n):
        return ref.at[pl.ds(pl.multiple_of(j * n, n), n)]

    def zrow(ref, j):
        return blk(ref, j, tb)

    def own(ref):
        return ref.at[pl.ds(pl.multiple_of(x * tp + z * tb, tb), tb)]

    def plane(ref, p):
        return blk(ref, p, tp)

    def loop(n, fn):
        lax.fori_loop(1, n, lambda i, t: (fn(i), t)[1], 0)

    def ring(n, me, dev, near):
        def off(i):
            odd = lax.rem(i, 2)
            return odd * lax.div(i + 1, 2) + (1 - odd) * (n - lax.div(i, 2)) if near else i

        def send_one(sem, src, dst, j):
            rcopy(src, dst(me), sem[0], sem[1](me), dev(j)).start()

        def send(sem, src, dst):
            def one(i):
                j = lax.rem(me + off(i), n)
                send_one(sem, src(j), dst, j)
            loop(n, one)

        def wait(sem, dst, i):
            s = lax.rem(me + n - off(i), n)
            rcopy(dst(s), dst(s), sem[0], sem[1](s), dev(s)).wait_recv()
            return s
        return send_one, send, wait

    def all_sent(sem, size):
        rcopy(size, size, sem[0], sem[1](0), (r, pc)).wait_send()

    def all_here(sem, size):
        rcopy(size, size, sem[0], sem[1](0), (r, pc)).wait_recv()

    _, col_send, _ = ring(C, c, lambda j: (r, j), False)
    _, z_send, z_wait = ring(Z, z, lambda j: (r, j * 2 + x), True)
    _, row_send, _ = ring(R, r, lambda j: (j, c), False)
    a_one, a_send, a_wait = ring(A, a, lambda j: (b * A + j, c), False)
    b_one, b_send, b_wait = ring(B, b, lambda j: (j * A + a, c), False)

    def one(k):
        return s_one.at[k], lambda j: r_one.at[k]

    def sz(k):
        return s_one.at[5 + k], lambda j: r_z.at[k, j]

    def sr(k):
        return s_one.at[12 + k], lambda j: r_ab.at[k, j]

    def zd(d):
        return lax.rem(z + 8 + d, 8)

    def rs_copy(k, src, r_ref, q, d):
        return rcopy(src, r_ref.at[q], s_one.at[5 + k], r_z.at[k, q], (r, zd(d) * 2 + x))

    def rs_start(k, s_ref, r_ref):
        if Z != 8:
            z_send(sz(k), lambda j: zrow(s_ref, j), lambda j: r_ref.at[j])
            return
        rs_copy(k, zrow(s_ref, zd(4)), r_ref, 2, 4 * core - 2).start()
        rs_copy(k, zrow(s_ref, zd(-3)), r_ref, 0, -1).start()
        rs_copy(k, zrow(s_ref, zd(3)), r_ref, 1, 1).start()
        rs_copy(k, zrow(s_ref, zd(-1)), r_ref, 3, -1).start()
        rs_copy(k, zrow(s_ref, zd(1)), r_ref, 4, 1).start()

    def rs_wait(k, r_ref, qs):
        for q in qs:
            rs_copy(k, r_ref.at[q], r_ref, q, 1).wait_recv()

    def rs_mid(k, s_ref, r_ref, m_ref):
        if Z != 8:
            return
        rs_wait(k, r_ref, (0, 1, 2))
        far = r_ref[2].astype(F32)
        none = jnp.zeros_like(far)
        m_ref[0] = (zrow(s_ref, zd(-2))[...].astype(F32) + r_ref[0].astype(F32)
                    + jnp.where(core == 0, far, none)).astype(BF)
        rs_copy(k, m_ref.at[0], r_ref, 5, -2).start()
        m_ref[1] = (zrow(s_ref, zd(2))[...].astype(F32) + r_ref[1].astype(F32)
                    + jnp.where(core == 0, none, far)).astype(BF)
        rs_copy(k, m_ref.at[1], r_ref, 6, 2).start()

    def ag_copy(k, at, s, d):
        return rcopy(at(s), at(s), s_one.at[5 + k], r_z.at[k, s], (r, zd(d) * 2 + x))

    def ag_start(k, at):
        if Z != 8:
            z_send(sz(k), lambda j: at(z), at)
            return
        for d in (2, -2, 1, -1):
            ag_copy(k, at, z, d).start()

    def ag_wait(k, at, ds):
        for d in ds:
            ag_copy(k, at, zd(d), 1).wait_recv()

    def ag_mid(k, at):
        if Z != 8:
            return
        ag_wait(k, at, (-2,))
        ag_copy(k, at, zd(-2), 1).start()
        ag_wait(k, at, (2,))
        ag_copy(k, at, zd(2), -1).start()
        ag_copy(k, at, zd(4 * core - 2), 2 - 4 * core).start()

    def ag_end(k, at):
        if Z != 8:
            loop(Z, lambda i: z_wait(sz(k), at, i))
            return
        ag_wait(k, at, (-1, 1, -3, 3, 4))

    def pair(k, src, dst):
        return rcopy(src, dst, s_p.at[k], r_p.at[k], (r, pc))

    ch = down_h.shape[0]
    my_down = blk(down_p, x, ch)
    my_out = blk(out_p, x, HEAD)
    loads = [
        pltpu.make_async_copy(down_h, my_down, s_in.at[0]),
        pltpu.make_async_copy(outp_h, my_out, s_in.at[1]),
        pltpu.make_async_copy(og_h, og, s_in.at[2]),
        pltpu.make_async_copy(
            qkv_h.at[pl.ds(HEAD, 2 * HEAD)], w_t.at[x, pl.ds(0, 2 * HEAD)], s_in.at[3]),
        pltpu.make_async_copy(
            qkv_h.at[pl.ds(0, HEAD)], w_t.at[x, pl.ds(2 * HEAD, HEAD)], s_in.at[4]),
    ]
    for load in loads:
        load.start()

    barrier = pltpu.get_barrier_semaphore()

    def greet(dev):
        pl.semaphore_signal(barrier, inc=1, device_id=dev, device_id_type=pl.DeviceIdType.MESH)
    loop(C, lambda i: greet((r, lax.rem(c + i, C))))
    loop(R, lambda i: greet((lax.rem(r + i, R), c)))
    loop(R, lambda i: greet((lax.rem(r + i, R), pc)))

    H8, W16, D2 = fine.shape
    n_cb = D2 // 128
    for cb in range(n_cb):
        fine_f[cb] = fine[:, :, cb * 128:(cb + 1) * 128].astype(F32)
    for aa in range(2):
        for bb in range(2):
            for cb in range(n_cb):
                parts = [fine_f[cb, 2 * h + aa, pl.ds(bb, W16 // 2, stride=2), :]
                         for h in range(H8 // 2)]
                a2a_s[(aa * 2 + bb) * n_cb + cb] = jnp.concatenate(parts, axis=0).astype(BF)

    def a2a_src(j):
        return a2a_s.at[pl.ds(lax.div(j, 2) * 2, 2), pl.ds(pl.multiple_of(lax.rem(j, 2) * 16, 16), 16)]

    pl.semaphore_wait(barrier, C + 2 * R - 3)
    col_send(one(0), a2a_src, lambda j: mrecv.at[j])
    loads[0].wait()
    p_down = pair(0, my_down, my_down)
    p_down.start()

    mrecv[c] = a2a_src(c)[...]
    loads[1].wait()
    loads[2].wait()
    qd_t[a, HEAD:, :] = mm_nt(my_out[...], og[...]).astype(BF)

    def d_at(j):
        return qd_t.at[j, pl.ds(HEAD, HEAD)]
    a_send(sr(7), lambda j: d_at(a), d_at)
    for k in range(2):
        w_t[k, 3 * HEAD:, :] = jnp.zeros((HEAD, D), BF)
    loads[3].wait()
    loads[4].wait()

    all_here(one(0), mrecv.at[pl.ds(0, C - 1)])
    for k in range(2):
        mr = mrecv[:, k].astype(F32).reshape(C, 2, W16 // 2, 128)
        merged[:, k * 128:(k + 1) * 128] = jnp.swapaxes(mr, 0, 1).reshape(tp, 128).astype(BF)
    p_down.wait_recv()

    rs1_s[...] = mm(merged[...], down_p[...]).astype(BF)
    rs_start(0, rs1_s, rs1_r)
    p_w = pair(1, w_t.at[x, pl.ds(0, 3 * HEAD)], w_t.at[x, pl.ds(0, 3 * HEAD)])
    p_w.start()
    p_out = pair(2, my_out, my_out)
    p_out.start()
    w_s[x] = flip(w_t[x]).astype(BF)
    rs_mid(0, rs1_s, rs1_r, rs1_m)
    dkv_acc[...] = jnp.zeros(dkv_acc.shape, F32)
    dq_acc[...] = jnp.zeros(dq_acc.shape, F32)

    def reduce_z(k, s_ref, r_ref):
        if Z == 8:
            rs_wait(k, r_ref, (3, 4, 5, 6))
            acc = zrow(s_ref, z)[...].astype(F32)
            for q in (3, 4, 5, 6):
                acc = acc + r_ref[q].astype(F32)
            return acc

        def one(i, acc):
            s = z_wait(sz(k), lambda q: r_ref.at[q], i)
            return acc + r_ref[s].astype(F32)
        return lax.fori_loop(1, Z, one, zrow(s_ref, z)[...].astype(F32))

    coarse = reduce_z(0, rs1_s, rs1_r).astype(BF).astype(F32)
    coarse_s[...] = coarse
    inv = lax.rsqrt(jnp.mean(coarse * coarse, axis=-1, keepdims=True) + EPSILON)
    inv_s[...] = jnp.broadcast_to(inv, inv_s.shape)
    gain_f = gain[...].astype(F32).reshape(1, D)
    own(normed)[...] = (coarse * inv * gain_f).astype(BF)

    def own_at(ref):
        return lambda j: ref.at[pl.ds(pl.multiple_of(x * tp + j * tb, tb), tb)]
    ag_start(1, own_at(normed))
    ag_mid(1, own_at(normed))
    p_w.wait_recv()
    w_s[y] = flip(w_t[y]).astype(BF)
    ag_end(1, own_at(normed))

    temper = HEAD ** (-0.5)
    n_pl = plane(normed, x)[...]
    mine = pl.ds(pl.multiple_of(x * tp, tp), tp)

    def split(w):
        proj = mm(n_pl, w)
        return proj[:, :128].astype(BF), flip(proj[:, 128:].astype(BF).astype(F32) * temper)
    kv_y, q_y = split(w_s[y])
    px_kv[...] = kv_y
    p_kv = pair(3, px_kv, kv.at[b, mine])
    p_kv.start()
    px_q[...] = q_y[:HEAD].astype(BF)
    p_q = pair(4, px_q, qd_t.at[a, pl.ds(0, HEAD), mine])
    p_q.start()
    kv_x, q_x = split(w_s[x])
    kv[b, mine] = kv_x
    qd_t[a, :HEAD, mine] = q_x[:HEAD].astype(BF)

    def kv_at(p):
        return lambda j: kv.at[j, pl.ds(pl.multiple_of(p * tp, tp), tp)]
    b_send(sr(0), lambda j: kv_at(x)(b), kv_at(x))
    p_kv.wait_recv()
    b_send(sr(1), lambda j: kv_at(y)(b), kv_at(y))
    p_q.wait_recv()

    def q_at(j):
        return qd_t.at[j, pl.ds(0, HEAD)]
    a_send(sr(8), lambda j: q_at(a), q_at)

    lane = lax.broadcasted_iota(jnp.int32, (T, 128), 1)
    zero = jnp.zeros((T, 128), BF)

    def prep_kv(s):
        v = kv[s]
        kv_t[s] = flip(v).astype(BF)
        k_m[s] = jnp.where(lane < HEAD, v, zero)
        v_m[s] = jnp.where(lane >= HEAD, v, zero)

    def prep_qd(s):
        v = flip(qd_t[s]).astype(BF)
        q_m[s] = jnp.where(lane < HEAD, v, zero)
        d_m[s] = jnp.where(lane >= HEAD, v, zero)

    prep_kv(b)
    prep_qd(a)

    def kv_next(i):
        b_wait(sr(0), kv_at(x), i)
        prep_kv(b_wait(sr(1), kv_at(y), i))
    loop(B, kv_next)

    def qd_next(i):
        a_wait(sr(7), d_at, i)
        prep_qd(a_wait(sr(8), q_at, i))
    loop(A, qd_next)

    def fwd_q(qi):
        qs = qd_t[qi]
        ss = [mm(k_m[kj], qs) for kj in range(B)]
        top = functools.reduce(
            jnp.maximum, [jnp.max(v, axis=0, keepdims=True) for v in ss])
        ps = [jnp.exp(v - top) for v in ss]
        total = sum(jnp.sum(p, axis=0, keepdims=True) for p in ps)
        acc = sum(mm(kv_t[kj, HEAD:, :], p.astype(BF)) for kj, p in enumerate(ps))
        o_s[qi] = (acc / total).astype(BF)
        lse_s[qi] = jnp.broadcast_to(top + jnp.log(total), lse_s.shape[1:])

    def fwd_one(i):
        qi = lax.rem(a + i, A)
        fwd_q(qi)
        a_one(sr(2), o_s.at[qi], lambda j: o_r.at[j], qi)
        a_one(sr(3), lse_s.at[qi], lambda j: lse_r.at[j], qi)
    loop(A, fwd_one)
    fwd_q(a)
    o_r[a] = o_s[a]
    lse_r[a] = lse_s[a]
    loop(A, lambda i: (a_wait(sr(2), lambda s: o_r.at[s], i),
                       a_wait(sr(3), lambda s: lse_r.at[s], i)))

    lses = [lse_r[s, 0:1, :] for s in range(A)]
    top = functools.reduce(jnp.maximum, lses)
    lse = top + jnp.log(sum(jnp.exp(v - top) for v in lses))
    o_t = sum(jnp.exp(v - lse) * o_r[s].astype(F32) for s, v in enumerate(lses)).astype(BF)
    delta = jnp.sum(qd_t[a, HEAD:, :].astype(F32) * o_t.astype(F32), axis=0, keepdims=True)
    st[a] = jnp.concatenate([lse, delta, jnp.zeros((6, T), F32)], axis=0)
    a_send(sr(4), lambda j: st.at[a], lambda j: st.at[j])

    att_s[:, :HEAD] = flip(o_t).astype(BF)
    att_s[:, HEAD:] = jnp.zeros((T, 128 - HEAD), BF)
    p_att = pair(5, plane(att_s, y), att_r)
    p_att.start()
    g_t[3 * HEAD:, :] = mm(o_t, og[...])
    loop(A, lambda i: a_wait(sr(4), lambda s: st.at[s], i))

    def tile(kj, qi):
        qs = qd_t[qi]
        p = jnp.exp(mm(k_m[kj], qs) - st[qi, 0:1, :])
        ds = (p * (mm(v_m[kj], qs) - st[qi, 1:2, :])).astype(BF)
        dkv_acc[kj] += mm(ds, q_m[qi]) + mm(p.astype(BF), d_m[qi])
        dq_acc[qi] += mm(kv_t[kj, :HEAD, :], ds)

    def bwd_one(i):
        kj = lax.rem(b + i, B)

        def two(h, t0):
            tile(kj, lax.rem(a + 2 * h, A))
            tile(kj, lax.rem(a + 2 * h + 1, A))
            return t0
        lax.fori_loop(0, A // 2, two, 0)
        dkv_s[kj] = dkv_acc[kj].astype(BF)
        b_one(sr(5), dkv_s.at[kj], lambda j: dkv_r.at[j], kj)

        @pl.when(i == 1)
        def _():
            p_att.wait_recv()
            p_norm.start()
            p_out.wait_recv()
            rs2_s[...] = (mm(plane(att_s, x)[:, :HEAD], my_out[...])
                          + mm(att_r[:, :HEAD], blk(out_p, y, HEAD)[...])).astype(BF)
            rs_start(2, rs2_s, rs2_r)

        @pl.when(i == min(2, B - 1))
        def _():
            rs_mid(2, rs2_s, rs2_r, rs2_m)
    p_norm = pair(6, plane(normed, x), plane(normed, x))
    loop(B, bwd_one)

    mixed = reduce_z(2, rs2_s, rs2_r)
    own(co_o)[...] = (coarse_s[...] + mixed).astype(BF)
    ag_start(5, own_at(co_o))

    for i in range(1, A + 1):
        qi = lax.rem(a + i, A)
        tile(b, qi)
        if i < A:
            dq_s[qi] = dq_acc[qi].astype(BF)
            a_one(sr(6), dq_s.at[qi], lambda j: dq_r.at[j], qi)

    ag_mid(5, own_at(co_o))

    def dkv_sum(i, acc):
        s = b_wait(sr(5), lambda q: dkv_r.at[q], i)
        return acc + dkv_r[s].astype(F32)
    dkv = lax.fori_loop(1, B, dkv_sum, dkv_acc[b]).astype(BF)

    dpk_s[...] = dkv
    p_dpk = pair(7, plane(dpk_s, y), dpk_r)
    p_dpk.start()
    part = mm(plane(dpk_s, x)[...], w_t[x, :2 * HEAD, :])

    def dq_sum(i, acc):
        s = a_wait(sr(6), lambda q: dq_r.at[q], i)
        return acc + dq_r[s].astype(F32)
    dq_t = (lax.fori_loop(1, A, dq_sum, dq_acc[a]) * temper).astype(BF)
    dpq_s[...] = dq_t
    other = pl.ds(pl.multiple_of(y * tp, tp), tp)
    p_dpq = pair(10, dpq_s.at[:, other], dpq_r)
    p_dpq.start()
    part += mm(flip(dpq_s[:, mine]).astype(BF), w_t[x, 2 * HEAD:3 * HEAD, :])
    p_dpk.wait_recv()
    part += mm(dpk_r[...], w_t[y, :2 * HEAD, :])
    p_dpq.wait_recv()
    rs3_s[...] = (part + mm(flip(dpq_r[...]).astype(BF), w_t[y, 2 * HEAD:3 * HEAD, :])).astype(BF)
    rs_start(3, rs3_s, rs3_r)

    ag_end(5, own_at(co_o))
    p_co = pair(8, plane(co_o, x), plane(co_o, x))
    p_co.start()

    p_norm.wait_recv()
    rs_mid(3, rs3_s, rs3_r, rs3_m)
    g_t[:2 * HEAD, :] = mm(flip(dkv).astype(BF), normed[...])
    g_t[2 * HEAD:3 * HEAD, :] = mm(dq_t, normed[...])
    g_s[...] = g_t[...].T.astype(BF)
    gb = D // R

    def g_rows(j):
        return blk(g_s, j, gb)
    row_send(one(2), g_rows, lambda j: g_r.at[j])

    ncot = reduce_z(3, rs3_s, rs3_r)
    coarse = coarse_s[...]
    inv = inv_s[:, :1]
    gpart = jnp.sum(ncot * coarse * inv, axis=0, keepdims=True)
    scaled = ncot * gain_f
    ccot = own(og)[...].astype(F32) + inv * scaled - coarse * (inv * inv * inv) * jnp.mean(
        scaled * coarse, axis=-1, keepdims=True)
    zrow(cc, z)[...] = ccot.astype(BF)
    hw = D // 2

    def cc_at(h):
        return lambda j: cc.at[pl.ds(pl.multiple_of(j * tb, tb), tb), pl.ds(h * hw, hw)]
    ag_start(4, cc_at(0))
    ag_mid(4, cc_at(0))
    ag_start(6, cc_at(1))
    gp = jnp.concatenate([gpart[:, i * 128:(i + 1) * 128] for i in range(D // 128)], axis=0)
    gn_s[...] = gp
    gn_r[c] = gp
    col_send(one(1), lambda j: gn_s, lambda j: gn_r.at[j])

    ag_mid(6, cc_at(1))

    def g_sum(i, acc):
        return acc + g_r[lax.rem(r + i, R)].astype(F32)
    all_here(one(2), g_r.at[pl.ds(0, R - 1)])
    g_all = lax.fori_loop(1, R, g_sum, g_rows(r)[...].astype(F32))
    for k in range(3):
        qg_o[k] = g_all[:, (k + 2) % 3 * HEAD:(k + 2) % 3 * HEAD + HEAD]
    opg_o[...] = g_all[:, 3 * HEAD:].T

    m_t = [flip(merged[:, k * 128:(k + 1) * 128]).astype(BF) for k in range(2)]
    p_co.wait_recv()
    co_out = pltpu.make_async_copy(co_o, co_h, s_in.at[5])
    co_out.start()
    me = r * 2 + x

    def dn_src(j):
        return dn_s.at[lax.rem(j, 2), pl.ds(pl.multiple_of(lax.div(j, 2) * gb, gb), gb)]
    for h in range(2):
        ag_end(4 + 2 * h, cc_at(h))
        for k in range(2):
            dn_s[k, h * hw:(h + 1) * hw, :] = mm(
                m_t[k], cc[:, h * hw:(h + 1) * hw]).T.astype(BF)

        def dn_one(i, t0):
            j = h * R + lax.rem(i + me, R)

            @pl.when(j != me)
            def _():
                rcopy(dn_src(j), dn_r.at[me], s_one.at[4], r_one.at[4],
                      (lax.div(j, 2), z * 2 + lax.rem(j, 2))).start()
            return t0
        lax.fori_loop(0, R, dn_one, 0)

    mg_s[...] = mm_nt(cc[...], blk(down_p, y, ch)[...]).astype(BF)
    p_mg = pair(9, mg_s, plane(mg_o, x))
    p_mg.start()
    all_here(one(1), gn_r.at[pl.ds(0, C - 1)])
    gt = jnp.sum(gn_r[...], axis=0)
    gt_s[...] = gt
    gt_r[r] = gt
    row_send(one(3), lambda j: gt_s, lambda j: gt_r.at[j])
    plane(mg_o, x)[...] = mm_nt(cc[...], my_down[...]).astype(BF)

    def d_sum(i, acc):
        return acc + dn_r[lax.rem(me + i, 2 * R)].astype(F32)
    all_here(one(4), dn_r.at[pl.ds(0, 2 * R - 1)])
    dg_o[...] = lax.fori_loop(1, 2 * R, d_sum, dn_src(me)[...].astype(F32))

    all_here(one(3), gt_r.at[pl.ds(0, R - 1)])
    gsum[...] = jnp.sum(gt_r[...], axis=0)
    g_row = gsum[pl.ds(lax.div(r, 2), 1), :]
    gg_o[...] = jnp.where(lax.rem(r, 2) == 0, g_row[:, :64], g_row[:, 64:])

    p_mg.wait_recv()
    co_out.wait()
    for p in (p_down, p_w, p_out, p_kv, p_q, p_att, p_norm, p_dpk, p_dpq, p_co, p_mg):
        p.wait_send()
    all_sent(one(0), mrecv.at[pl.ds(0, C - 1)])
    all_sent(one(1), gn_r.at[pl.ds(0, C - 1)])
    all_sent(one(2), g_r.at[pl.ds(0, R - 1)])
    all_sent(one(3), gt_r.at[pl.ds(0, R - 1)])
    all_sent(one(4), dn_r.at[pl.ds(0, 2 * R - 1)])
    for k in (0, 1, 2, 3, 5):
        all_sent(sz(k), rs1_r.at[pl.ds(0, Z - 1)])
    for k in (4, 6):
        all_sent(sz(k), rs1_r.at[pl.ds(0, Z - 1), :, pl.ds(0, hw)])
    for k in (0, 1):
        all_sent(sr(k), kv.at[pl.ds(0, B - 1), pl.ds(0, tp)])
    for k in (7, 8, 2, 6):
        all_sent(sr(k), o_s.at[pl.ds(0, A - 1)])
    for k in (3, 4):
        all_sent(sr(k), st.at[pl.ds(0, A - 1)])
    all_sent(sr(5), dkv_s.at[pl.ds(0, B - 1)])


def hand_over(parts, *refs):
    ins, outs, bufs, s_in, s_out = refs[:6], refs[6:12], refs[12:18], refs[18], refs[19]
    loads, stores = [], []
    for src, dst, buf, n in zip(ins, outs, bufs, parts):
        rows = src.shape[0] // n
        for k in range(n):
            at, q = pl.ds(k * rows, rows), len(loads)
            loads.append(pltpu.make_async_copy(src.at[at], buf.at[at], s_in.at[q]))
            stores.append(pltpu.make_async_copy(buf.at[at], dst.at[at], s_out.at[q]))
    for load in loads:
        load.start()
    for load, store in zip(loads, stores):
        load.wait()
        store.start()
    for store in stores:
        store.wait()


def body(R, C, fine_tiles, out_grad, down_proj, qkv_proj, out_proj, norm_gain):
    A = 2 ** ((R.bit_length() - 1) // 2)
    B = R // A
    D = out_grad.shape[-1]
    th, tw = out_grad.shape[0], out_grad.shape[1]
    T = th * tw
    Z = C // 2
    tp = T // 2
    tb = tp // Z
    H8, W16, D2 = fine_tiles.shape
    ch = down_proj.shape[0]
    gb = D // R
    V = pltpu.VMEM
    S = pltpu.SemaphoreType.DMA
    scratch = [
        V((T, D), BF), V((T, D), BF),
        V((D2 // 128, H8, W16, 128), F32), V((C, 32, 128), BF), V((C, 2, 16, 128), BF),
        V((tp, 2 * ch), BF), V((2 * ch, D), BF), V((2, D, 4 * HEAD), BF), V((2, 4 * HEAD, D), BF),
        V((2 * HEAD, D), BF),
        V((tp, D), BF), V((Z, tb, D), BF), V((2, tb, D), BF), V((tb, D), F32), V((tb, 128), F32),
        V((T, D), BF), V((tp, 128), BF), V((HEAD, tp), BF),
        V((B, T, 128), BF),
        V((B, 128, T), BF), V((A, 128, T), BF), V((B, T, 128), BF), V((B, T, 128), BF),
        V((A, T, 128), BF), V((A, T, 128), BF),
        V((A, HEAD, T), BF), V((A, HEAD, T), BF), V((A, 8, T), F32), V((A, 8, T), F32),
        V((A, 8, T), F32), V((T, 128), BF), V((tp, 128), BF),
        V((tp, D), BF), V((Z, tb, D), BF), V((2, tb, D), BF),
        V((B, T, 128), F32), V((B, T, 128), BF), V((B, T, 128), BF),
        V((A, HEAD, T), F32), V((A, HEAD, T), BF), V((A, HEAD, T), BF),
        V((T, 128), BF), V((tp, 128), BF), V((HEAD, T), BF), V((HEAD, tp), BF),
        V((tp, D), BF), V((Z, tb, D), BF), V((2, tb, D), BF),
        V((4 * HEAD, D), F32), V((D, 4 * HEAD), BF), V((R, gb, 4 * HEAD), BF),
        V((tp, D), BF), V((D // 128, 128), F32), V((C, D // 128, 128), F32),
        V((D // 128, 128), F32), V((R, D // 128, 128), F32), V((D // 128, 128), F32),
        V((tp, ch), BF), V((2, D, ch), BF), V((2 * R, gb, ch), BF),
        S((21,)), S((5,)), S((7, Z)), S((11,)), S((11,)), S((9, max(A, B))), S((6,)),
    ]
    vm = pl.BlockSpec(memory_space=pltpu.VMEM)
    hb = pl.BlockSpec(memory_space=pl.ANY)
    outs = pl.pallas_call(
        functools.partial(kernel, R, C, A),
        out_shape=(
            jax.ShapeDtypeStruct((T, D), BF),
            jax.ShapeDtypeStruct((T, ch), BF),
            jax.ShapeDtypeStruct((gb, ch), F32),
            jax.ShapeDtypeStruct((3, gb, HEAD), F32),
            jax.ShapeDtypeStruct((HEAD, gb), F32),
            jax.ShapeDtypeStruct((1, gb), F32),
        ),
        in_specs=[vm, hb, hb, hb, hb, vm],
        out_specs=(hb,) + (vm,) * 5,
        scratch_shapes=scratch,
        compiler_params=pltpu.CompilerParams(
            collective_id=0, has_side_effects=True, vmem_limit_bytes=56 * 1024 * 1024),
        name="block",
    )(fine_tiles, out_grad.reshape(T, D), down_proj, qkv_proj.transpose(1, 2, 0).reshape(3 * HEAD, D), out_proj,
      norm_gain)
    parts = [8, 1, 1, 1, 1, 1]
    co, mg, dg, qg, opg, gg = pl.pallas_call(
        functools.partial(hand_over, parts),
        out_shape=[jax.ShapeDtypeStruct(o.shape, o.dtype) for o in outs],
        in_specs=[hb] * 6,
        out_specs=[hb] * 6,
        scratch_shapes=[V(o.shape, o.dtype) for o in outs] + [S((sum(parts),))] * 2,
        name="hand_over",
    )(*outs)
    return (co.reshape(th, tw, D), mg.reshape(th, tw, ch), dg.T, qg.transpose(1, 0, 2), opg,
            gg.reshape(gb))


def solution(mesh):
    R, C = mesh.shape["row"], mesh.shape["col"]
    return jax.shard_map(
        functools.partial(body, R, C),
        mesh=mesh,
        in_specs=(P("row", "col", None), P("row", None, None), P("col", None),
                  P(None, None, "col"), P("col", None), P()),
        out_specs=(P("row", None, None), P("row", None, "col"), P("col", "row"),
                   P("row", None, "col"), P("col", "row"), P("row")),
        check_vma=False,
    )
```

```python
import functools

import jax
import jax.numpy as jnp
from jax import lax
from jax.experimental import pallas as pl
from jax.experimental.pallas import tpu as pltpu
from jax.sharding import PartitionSpec as P

HEAD = 64
EPSILON = 1e-06
BF = jnp.bfloat16
F32 = jnp.float32


def mm(x, y):
    return jnp.dot(x, y, preferred_element_type=F32)


def mm_nt(x, y):
    return lax.dot_general(x, y, (((1,), (1,)), ((), ())), preferred_element_type=F32)


def flip(x):
    return x.astype(F32).T


def kernel(R, C, A, *refs):
    (fine, og_h, down_h, qkv_h, outp_h, gain,
     co_h, mg_o, dg_o, qg_o, opg_o, gg_o,
     og, co_o, fine_f, a2a_s, mrecv, merged, down_p, w_s, w_t, out_p,
     rs1_s, rs1_r, rs1_m, coarse_s, inv_s, normed, px_kv, px_q,
     kv, kv_t, qd_t, k_m, v_m, q_m, d_m,
     o_s, o_r, lse_s, lse_r, st, att_s, att_r,
     rs2_s, rs2_r, rs2_m, dkv_acc, dkv_s, dkv_r, dq_acc, dq_s, dq_r, dpk_s, dpk_r, dpq_s, dpq_r,
     rs3_s, rs3_r, rs3_m, g_t, g_s, g_r, cc, gn_s, gn_r, gt_s, gt_r, gsum, mg_s, dn_s, dn_r,
     s_one, r_one, r_z, s_p, r_p, r_ab, s_in) = refs
    B = R // A
    Z = C // 2
    T, D = og.shape
    core = lax.rem(lax.axis_index("row"), 2)
    tp = T // 2
    tb = tp // Z
    r = lax.axis_index("row")
    c = lax.axis_index("col")
    a = lax.rem(r, A)
    b = lax.div(r, A)
    z = lax.div(c, 2)
    x = lax.rem(c, 2)
    y = 1 - x
    pc = z * 2 + y

    def rcopy(src, dst, ssem, rsem, dev):
        return pltpu.make_async_remote_copy(
            src_ref=src, dst_ref=dst, send_sem=ssem, recv_sem=rsem,
            device_id=dev, device_id_type=pl.DeviceIdType.MESH)

    def blk(ref, j, n):
        return ref.at[pl.ds(pl.multiple_of(j * n, n), n)]

    def zrow(ref, j):
        return blk(ref, j, tb)

    def own(ref):
        return ref.at[pl.ds(pl.multiple_of(x * tp + z * tb, tb), tb)]

    def plane(ref, p):
        return blk(ref, p, tp)

    def loop(n, fn):
        lax.fori_loop(1, n, lambda i, t: (fn(i), t)[1], 0)

    def ring(n, me, dev, near):
        def off(i):
            odd = lax.rem(i, 2)
            return odd * lax.div(i + 1, 2) + (1 - odd) * (n - lax.div(i, 2)) if near else i

        def send_one(sem, src, dst, j):
            rcopy(src, dst(me), sem[0], sem[1](me), dev(j)).start()

        def send(sem, src, dst):
            def one(i):
                j = lax.rem(me + off(i), n)
                send_one(sem, src(j), dst, j)
            loop(n, one)

        def wait(sem, dst, i):
            s = lax.rem(me + n - off(i), n)
            rcopy(dst(s), dst(s), sem[0], sem[1](s), dev(s)).wait_recv()
            return s
        return send_one, send, wait

    def all_sent(sem, size):
        rcopy(size, size, sem[0], sem[1](0), (r, pc)).wait_send()

    def all_here(sem, size):
        rcopy(size, size, sem[0], sem[1](0), (r, pc)).wait_recv()

    _, col_send, _ = ring(C, c, lambda j: (r, j), False)
    _, z_send, z_wait = ring(Z, z, lambda j: (r, j * 2 + x), True)
    _, row_send, _ = ring(R, r, lambda j: (j, c), False)
    a_one, a_send, a_wait = ring(A, a, lambda j: (b * A + j, c), False)
    b_one, b_send, b_wait = ring(B, b, lambda j: (j * A + a, c), False)

    def one(k):
        return s_one.at[k], lambda j: r_one.at[k]

    def sz(k):
        return s_one.at[5 + k], lambda j: r_z.at[k, j]

    def sr(k):
        return s_one.at[15 + k], lambda j: r_ab.at[k, j]

    def zd(d):
        return lax.rem(z + 8 + d, 8)

    def rs_copy(k, src, r_ref, q, d):
        return rcopy(src, r_ref.at[q], s_one.at[5 + k], r_z.at[k, q], (r, zd(d) * 2 + x))

    def rs_start(k, s_ref, r_ref):
        if Z != 8:
            z_send(sz(k), lambda j: zrow(s_ref, j), lambda j: r_ref.at[j])
            return
        rs_copy(k, zrow(s_ref, zd(4)), r_ref, 2, 4 * core - 2).start()
        rs_copy(k, zrow(s_ref, zd(-3)), r_ref, 0, -1).start()
        rs_copy(k, zrow(s_ref, zd(3)), r_ref, 1, 1).start()
        rs_copy(k, zrow(s_ref, zd(-1)), r_ref, 3, -1).start()
        rs_copy(k, zrow(s_ref, zd(1)), r_ref, 4, 1).start()

    def rs_wait(k, r_ref, qs):
        for q in qs:
            rs_copy(k, r_ref.at[q], r_ref, q, 1).wait_recv()

    def rs_mid(k, s_ref, r_ref, m_ref):
        if Z != 8:
            return
        rs_wait(k, r_ref, (0, 1, 2))
        far = r_ref[2].astype(F32)
        none = jnp.zeros_like(far)
        m_ref[0] = (zrow(s_ref, zd(-2))[...].astype(F32) + r_ref[0].astype(F32)
                    + jnp.where(core == 0, far, none)).astype(BF)
        rs_copy(k, m_ref.at[0], r_ref, 5, -2).start()
        m_ref[1] = (zrow(s_ref, zd(2))[...].astype(F32) + r_ref[1].astype(F32)
                    + jnp.where(core == 0, none, far)).astype(BF)
        rs_copy(k, m_ref.at[1], r_ref, 6, 2).start()

    def ag_copy(k, at, s, d):
        return rcopy(at(s), at(s), s_one.at[5 + k], r_z.at[k, s], (r, zd(d) * 2 + x))

    def ag_start(k, at):
        if Z != 8:
            z_send(sz(k), lambda j: at(z), at)
            return
        for d in (2, -2, 1, -1):
            ag_copy(k, at, z, d).start()

    def ag_wait(k, at, ds):
        for d in ds:
            ag_copy(k, at, zd(d), 1).wait_recv()

    def ag_mid(k, at):
        if Z != 8:
            return
        ag_wait(k, at, (-2,))
        ag_copy(k, at, zd(-2), 1).start()
        ag_wait(k, at, (2,))
        ag_copy(k, at, zd(2), -1).start()
        ag_copy(k, at, zd(4 * core - 2), 2 - 4 * core).start()

    def ag_end(k, at):
        if Z != 8:
            loop(Z, lambda i: z_wait(sz(k), at, i))
            return
        ag_wait(k, at, (-1, 1, -3, 3, 4))

    def pair(k, src, dst):
        return rcopy(src, dst, s_p.at[k], r_p.at[k], (r, pc))

    ch = down_h.shape[0]
    my_down = blk(down_p, x, ch)
    my_out = blk(out_p, x, HEAD)
    loads = [
        pltpu.make_async_copy(down_h, my_down, s_in.at[0]),
        pltpu.make_async_copy(outp_h, my_out, s_in.at[1]),
        pltpu.make_async_copy(og_h, og, s_in.at[2]),
        pltpu.make_async_copy(
            qkv_h.at[pl.ds(HEAD, 2 * HEAD)], w_t.at[x, pl.ds(0, 2 * HEAD)], s_in.at[3]),
        pltpu.make_async_copy(
            qkv_h.at[pl.ds(0, HEAD)], w_t.at[x, pl.ds(2 * HEAD, HEAD)], s_in.at[4]),
    ]
    for load in loads:
        load.start()

    barrier = pltpu.get_barrier_semaphore()

    def greet(dev):
        pl.semaphore_signal(barrier, inc=1, device_id=dev, device_id_type=pl.DeviceIdType.MESH)
    loop(C, lambda i: greet((r, lax.rem(c + i, C))))
    loop(R, lambda i: greet((lax.rem(r + i, R), c)))
    loop(R, lambda i: greet((lax.rem(r + i, R), pc)))

    H8, W16, D2 = fine.shape
    n_cb = D2 // 128
    for cb in range(n_cb):
        fine_f[cb] = fine[:, :, cb * 128:(cb + 1) * 128].astype(F32)
    for aa in range(2):
        for bb in range(2):
            for cb in range(n_cb):
                parts = [fine_f[cb, 2 * h + aa, pl.ds(bb, W16 // 2, stride=2), :]
                         for h in range(H8 // 2)]
                a2a_s[(aa * 2 + bb) * n_cb + cb] = jnp.concatenate(parts, axis=0).astype(BF)

    def a2a_src(j):
        return a2a_s.at[pl.ds(lax.div(j, 2) * 2, 2), pl.ds(pl.multiple_of(lax.rem(j, 2) * 16, 16), 16)]

    pl.semaphore_wait(barrier, C + 2 * R - 3)
    col_send(one(0), a2a_src, lambda j: mrecv.at[j])
    loads[0].wait()
    hw = D // 2

    def cols(h):
        return pl.ds(h * hw, hw)

    def halves(h, s_ref, r_ref, m_ref):
        return s_ref.at[:, cols(h)], r_ref.at[:, :, cols(h)], m_ref.at[:, :, cols(h)]
    p_down = [pair(k, my_down.at[:, cols(h)], my_down.at[:, cols(h)])
              for h, k in enumerate((0, 11))]
    for p in p_down:
        p.start()

    mrecv[c] = a2a_src(c)[...]
    loads[1].wait()
    loads[2].wait()
    qd_t[a, HEAD:, :] = mm_nt(my_out[...], og[...]).astype(BF)

    def d_at(j):
        return qd_t.at[j, pl.ds(HEAD, HEAD)]
    a_send(sr(7), lambda j: d_at(a), d_at)
    for k in range(2):
        w_t[k, 3 * HEAD:, :] = jnp.zeros((HEAD, D), BF)
    loads[3].wait()
    loads[4].wait()

    all_here(one(0), mrecv.at[pl.ds(0, C - 1)])
    for k in range(2):
        mr = mrecv[:, k].astype(F32).reshape(C, 2, W16 // 2, 128)
        merged[:, k * 128:(k + 1) * 128] = jnp.swapaxes(mr, 0, 1).reshape(tp, 128).astype(BF)
    for h in range(2):
        p_down[h].wait_recv()
        rs1_s[:, h * hw:(h + 1) * hw] = mm(
            merged[...], down_p[:, h * hw:(h + 1) * hw]).astype(BF)
        rs_start(7 * h, *halves(h, rs1_s, rs1_r, rs1_m)[:2])
    p_w = pair(1, w_t.at[x, pl.ds(0, 3 * HEAD)], w_t.at[x, pl.ds(0, 3 * HEAD)])
    p_w.start()
    p_out = pair(2, my_out, my_out)
    p_out.start()
    w_s[x] = flip(w_t[x]).astype(BF)
    for h in range(2):
        rs_mid(7 * h, *halves(h, rs1_s, rs1_r, rs1_m))
    dkv_acc[...] = jnp.zeros(dkv_acc.shape, F32)
    dq_acc[...] = jnp.zeros(dq_acc.shape, F32)

    def reduce_z(k, s_ref, r_ref):
        if Z == 8:
            rs_wait(k, r_ref, (3, 4, 5, 6))
            acc = zrow(s_ref, z)[...].astype(F32)
            for q in (3, 4, 5, 6):
                acc = acc + r_ref[q].astype(F32)
            return acc

        def one(i, acc):
            s = z_wait(sz(k), lambda q: r_ref.at[q], i)
            return acc + r_ref[s].astype(F32)
        return lax.fori_loop(1, Z, one, zrow(s_ref, z)[...].astype(F32))

    coarse = jnp.concatenate(
        [reduce_z(7 * h, *halves(h, rs1_s, rs1_r, rs1_m)[:2]) for h in range(2)],
        axis=1).astype(BF).astype(F32)
    coarse_s[...] = coarse
    inv = lax.rsqrt(jnp.mean(coarse * coarse, axis=-1, keepdims=True) + EPSILON)
    inv_s[...] = jnp.broadcast_to(inv, inv_s.shape)
    gain_f = gain[...].astype(F32).reshape(1, D)
    own(normed)[...] = (coarse * inv * gain_f).astype(BF)

    def own_at(ref):
        return lambda j: ref.at[pl.ds(pl.multiple_of(x * tp + j * tb, tb), tb)]
    ag_start(1, own_at(normed))
    ag_mid(1, own_at(normed))
    p_w.wait_recv()
    w_s[y] = flip(w_t[y]).astype(BF)
    ag_end(1, own_at(normed))

    temper = HEAD ** (-0.5)
    n_pl = plane(normed, x)[...]
    mine = pl.ds(pl.multiple_of(x * tp, tp), tp)

    def split(w):
        proj = mm(n_pl, w)
        return proj[:, :128].astype(BF), flip(proj[:, 128:].astype(BF).astype(F32) * temper)
    kv_y, q_y = split(w_s[y])
    px_kv[...] = kv_y
    p_kv = pair(3, px_kv, kv.at[b, mine])
    p_kv.start()
    px_q[...] = q_y[:HEAD].astype(BF)
    p_q = pair(4, px_q, qd_t.at[a, pl.ds(0, HEAD), mine])
    p_q.start()
    kv_x, q_x = split(w_s[x])
    kv[b, mine] = kv_x
    qd_t[a, :HEAD, mine] = q_x[:HEAD].astype(BF)

    def kv_at(p):
        return lambda j: kv.at[j, pl.ds(pl.multiple_of(p * tp, tp), tp)]
    b_send(sr(0), lambda j: kv_at(x)(b), kv_at(x))
    p_kv.wait_recv()
    b_send(sr(1), lambda j: kv_at(y)(b), kv_at(y))
    p_q.wait_recv()

    def q_at(j):
        return qd_t.at[j, pl.ds(0, HEAD)]
    a_send(sr(8), lambda j: q_at(a), q_at)

    lane = lax.broadcasted_iota(jnp.int32, (T, 128), 1)
    zero = jnp.zeros((T, 128), BF)

    def prep_kv(s):
        v = kv[s]
        kv_t[s] = flip(v).astype(BF)
        k_m[s] = jnp.where(lane < HEAD, v, zero)
        v_m[s] = jnp.where(lane >= HEAD, v, zero)

    def prep_qd(s):
        v = flip(qd_t[s]).astype(BF)
        q_m[s] = jnp.where(lane < HEAD, v, zero)
        d_m[s] = jnp.where(lane >= HEAD, v, zero)

    prep_kv(b)
    prep_qd(a)

    def kv_next(i):
        b_wait(sr(0), kv_at(x), i)
        prep_kv(b_wait(sr(1), kv_at(y), i))
    loop(B, kv_next)

    def qd_next(i):
        a_wait(sr(7), d_at, i)
        prep_qd(a_wait(sr(8), q_at, i))
    loop(A, qd_next)

    def fwd_q(qi):
        qs = qd_t[qi]
        ss = [mm(k_m[kj], qs) for kj in range(B)]
        top = functools.reduce(
            jnp.maximum, [jnp.max(v, axis=0, keepdims=True) for v in ss])
        ps = [jnp.exp(v - top) for v in ss]
        total = sum(jnp.sum(p, axis=0, keepdims=True) for p in ps)
        acc = sum(mm(kv_t[kj, HEAD:, :], p.astype(BF)) for kj, p in enumerate(ps))
        o_s[qi] = (acc / total).astype(BF)
        lse_s[qi] = jnp.broadcast_to(top + jnp.log(total), lse_s.shape[1:])

    def fwd_one(i):
        qi = lax.rem(a + i, A)
        fwd_q(qi)
        a_one(sr(2), o_s.at[qi], lambda j: o_r.at[j], qi)
        a_one(sr(3), lse_s.at[qi], lambda j: lse_r.at[j], qi)
    loop(A, fwd_one)
    fwd_q(a)
    o_r[a] = o_s[a]
    lse_r[a] = lse_s[a]
    loop(A, lambda i: (a_wait(sr(2), lambda s: o_r.at[s], i),
                       a_wait(sr(3), lambda s: lse_r.at[s], i)))

    lses = [lse_r[s, 0:1, :] for s in range(A)]
    top = functools.reduce(jnp.maximum, lses)
    lse = top + jnp.log(sum(jnp.exp(v - top) for v in lses))
    o_t = sum(jnp.exp(v - lse) * o_r[s].astype(F32) for s, v in enumerate(lses)).astype(BF)
    delta = jnp.sum(qd_t[a, HEAD:, :].astype(F32) * o_t.astype(F32), axis=0, keepdims=True)
    st[a] = jnp.concatenate([lse, delta, jnp.zeros((6, T), F32)], axis=0)
    a_send(sr(4), lambda j: st.at[a], lambda j: st.at[j])

    att_s[:, :HEAD] = flip(o_t).astype(BF)
    att_s[:, HEAD:] = jnp.zeros((T, 128 - HEAD), BF)
    p_att = pair(5, plane(att_s, y), att_r)
    p_att.start()
    g_t[3 * HEAD:, :] = mm(o_t, og[...])
    loop(A, lambda i: a_wait(sr(4), lambda s: st.at[s], i))

    def tile(kj, qi):
        qs = qd_t[qi]
        p = jnp.exp(mm(k_m[kj], qs) - st[qi, 0:1, :])
        ds = (p * (mm(v_m[kj], qs) - st[qi, 1:2, :])).astype(BF)
        dkv_acc[kj] += mm(ds, q_m[qi]) + mm(p.astype(BF), d_m[qi])
        dq_acc[qi] += mm(kv_t[kj, :HEAD, :], ds)

    def bwd_one(i):
        kj = lax.rem(b + i, B)

        def two(h, t0):
            tile(kj, lax.rem(a + 2 * h, A))
            tile(kj, lax.rem(a + 2 * h + 1, A))
            return t0
        lax.fori_loop(0, A // 2, two, 0)
        dkv_s[kj] = dkv_acc[kj].astype(BF)
        b_one(sr(5), dkv_s.at[kj], lambda j: dkv_r.at[j], kj)

        @pl.when(i == 1)
        def _():
            p_att.wait_recv()
            p_norm.start()
            p_out.wait_recv()
            rs2_s[...] = (mm(plane(att_s, x)[:, :HEAD], my_out[...])
                          + mm(att_r[:, :HEAD], blk(out_p, y, HEAD)[...])).astype(BF)
            rs_start(2, rs2_s, rs2_r)

        @pl.when(i == min(2, B - 1))
        def _():
            rs_mid(2, rs2_s, rs2_r, rs2_m)
    p_norm = pair(6, plane(normed, x), plane(normed, x))
    loop(B, bwd_one)

    mixed = reduce_z(2, rs2_s, rs2_r)
    own(co_o)[...] = (coarse_s[...] + mixed).astype(BF)
    ag_start(5, own_at(co_o))

    for i in range(1, A + 1):
        qi = lax.rem(a + i, A)
        tile(b, qi)
        if i < A:
            dq_s[qi] = dq_acc[qi].astype(BF)
            a_one(sr(6), dq_s.at[qi], lambda j: dq_r.at[j], qi)

    ag_mid(5, own_at(co_o))

    def dkv_sum(i, acc):
        s = b_wait(sr(5), lambda q: dkv_r.at[q], i)
        return acc + dkv_r[s].astype(F32)
    dkv = lax.fori_loop(1, B, dkv_sum, dkv_acc[b]).astype(BF)

    dpk_s[...] = dkv
    p_dpk = pair(7, plane(dpk_s, y), dpk_r)
    p_dpk.start()
    part = mm(plane(dpk_s, x)[...], w_t[x, :2 * HEAD, :])

    def dq_sum(i, acc):
        s = a_wait(sr(6), lambda q: dq_r.at[q], i)
        return acc + dq_r[s].astype(F32)
    dq_t = (lax.fori_loop(1, A, dq_sum, dq_acc[a]) * temper).astype(BF)
    dpq_s[...] = dq_t
    other = pl.ds(pl.multiple_of(y * tp, tp), tp)
    p_dpq = pair(10, dpq_s.at[:, other], dpq_r)
    p_dpq.start()
    part += mm(flip(dpq_s[:, mine]).astype(BF), w_t[x, 2 * HEAD:3 * HEAD, :])
    p_dpk.wait_recv()
    part += mm(dpk_r[...], w_t[y, :2 * HEAD, :])
    p_dpq.wait_recv()
    dq_y = flip(dpq_r[...]).astype(BF)
    for h in range(2):
        at = slice(h * hw, (h + 1) * hw)
        rs3_s[:, at] = (part[:, at] + mm(dq_y, w_t[y, 2 * HEAD:3 * HEAD, at])).astype(BF)
        rs_start(3 + 5 * h, *halves(h, rs3_s, rs3_r, rs3_m)[:2])

    ag_end(5, own_at(co_o))
    p_co = pair(8, plane(co_o, x), plane(co_o, x))
    p_co.start()

    p_norm.wait_recv()
    for h in range(2):
        rs_mid(3 + 5 * h, *halves(h, rs3_s, rs3_r, rs3_m))
    g_t[:2 * HEAD, :] = mm(flip(dkv).astype(BF), normed[...])
    g_t[2 * HEAD:3 * HEAD, :] = mm(dq_t, normed[...])
    g_s[...] = g_t[...].T.astype(BF)
    gb = D // R

    def g_rows(j):
        return blk(g_s, j, gb)
    row_send(one(2), g_rows, lambda j: g_r.at[j])

    ncot = jnp.concatenate(
        [reduce_z(3 + 5 * h, *halves(h, rs3_s, rs3_r, rs3_m)[:2]) for h in range(2)], axis=1)
    coarse = coarse_s[...]
    inv = inv_s[:, :1]
    gpart = jnp.sum(ncot * coarse * inv, axis=0, keepdims=True)
    scaled = ncot * gain_f
    ccot = own(og)[...].astype(F32) + inv * scaled - coarse * (inv * inv * inv) * jnp.mean(
        scaled * coarse, axis=-1, keepdims=True)
    zrow(cc, z)[...] = ccot.astype(BF)
    def cc_at(j):
        return zrow(cc, j)
    ag_start(4, cc_at)
    gp = jnp.concatenate([gpart[:, i * 128:(i + 1) * 128] for i in range(D // 128)], axis=0)
    gn_s[...] = gp
    gn_r[c] = gp
    col_send(one(1), lambda j: gn_s, lambda j: gn_r.at[j])

    ag_mid(4, cc_at)

    def g_sum(i, acc):
        return acc + g_r[lax.rem(r + i, R)].astype(F32)
    all_here(one(2), g_r.at[pl.ds(0, R - 1)])
    g_all = lax.fori_loop(1, R, g_sum, g_rows(r)[...].astype(F32))
    for k in range(3):
        qg_o[k] = g_all[:, (k + 2) % 3 * HEAD:(k + 2) % 3 * HEAD + HEAD]
    opg_o[...] = g_all[:, 3 * HEAD:].T

    m_t = [flip(merged[:, k * 128:(k + 1) * 128]).astype(BF) for k in range(2)]
    p_co.wait_recv()
    co_out = pltpu.make_async_copy(co_o, co_h, s_in.at[5])
    co_out.start()
    me = r * 2 + x

    def dn_src(j):
        return dn_s.at[lax.rem(j, 2), pl.ds(pl.multiple_of(lax.div(j, 2) * gb, gb), gb)]
    ag_end(4, cc_at)
    for h in range(2):
        for k in range(2):
            dn_s[k, h * hw:(h + 1) * hw, :] = mm(
                m_t[k], cc[:, h * hw:(h + 1) * hw]).T.astype(BF)

        def dn_one(i, t0):
            j = h * R + lax.rem(i + me, R)

            @pl.when(j != me)
            def _():
                rcopy(dn_src(j), dn_r.at[me], s_one.at[4], r_one.at[4],
                      (lax.div(j, 2), z * 2 + lax.rem(j, 2))).start()
            return t0
        lax.fori_loop(0, R, dn_one, 0)

    mg_s[...] = mm_nt(cc[...], blk(down_p, y, ch)[...]).astype(BF)
    p_mg = pair(9, mg_s, plane(mg_o, x))
    p_mg.start()
    all_here(one(1), gn_r.at[pl.ds(0, C - 1)])
    gt = jnp.sum(gn_r[...], axis=0)
    gt_s[...] = gt
    gt_r[r] = gt
    row_send(one(3), lambda j: gt_s, lambda j: gt_r.at[j])
    plane(mg_o, x)[...] = mm_nt(cc[...], my_down[...]).astype(BF)

    def d_sum(i, acc):
        return acc + dn_r[lax.rem(me + i, 2 * R)].astype(F32)
    all_here(one(4), dn_r.at[pl.ds(0, 2 * R - 1)])
    dg_o[...] = lax.fori_loop(1, 2 * R, d_sum, dn_src(me)[...].astype(F32))

    all_here(one(3), gt_r.at[pl.ds(0, R - 1)])
    gsum[...] = jnp.sum(gt_r[...], axis=0)
    g_row = gsum[pl.ds(lax.div(r, 2), 1), :]
    gg_o[...] = jnp.where(lax.rem(r, 2) == 0, g_row[:, :64], g_row[:, 64:])

    p_mg.wait_recv()
    co_out.wait()
    for p in (*p_down, p_w, p_out, p_kv, p_q, p_att, p_norm, p_dpk, p_dpq, p_co, p_mg):
        p.wait_send()
    all_sent(one(0), mrecv.at[pl.ds(0, C - 1)])
    all_sent(one(1), gn_r.at[pl.ds(0, C - 1)])
    all_sent(one(2), g_r.at[pl.ds(0, R - 1)])
    all_sent(one(3), gt_r.at[pl.ds(0, R - 1)])
    all_sent(one(4), dn_r.at[pl.ds(0, 2 * R - 1)])
    for k in (1, 2, 4, 5):
        all_sent(sz(k), rs1_r.at[pl.ds(0, Z - 1)])
    for k in (0, 3, 7, 8):
        all_sent(sz(k), rs1_r.at[pl.ds(0, Z - 1), :, pl.ds(0, hw)])
    for k in (0, 1):
        all_sent(sr(k), kv.at[pl.ds(0, B - 1), pl.ds(0, tp)])
    for k in (7, 8, 2, 6):
        all_sent(sr(k), o_s.at[pl.ds(0, A - 1)])
    for k in (3, 4):
        all_sent(sr(k), st.at[pl.ds(0, A - 1)])
    all_sent(sr(5), dkv_s.at[pl.ds(0, B - 1)])


def hand_over(parts, *refs):
    ins, outs, bufs, s_in, s_out = refs[:6], refs[6:12], refs[12:18], refs[18], refs[19]
    loads, stores = [], []
    for src, dst, buf, n in zip(ins, outs, bufs, parts):
        rows = src.shape[0] // n
        for k in range(n):
            at, q = pl.ds(k * rows, rows), len(loads)
            loads.append(pltpu.make_async_copy(src.at[at], buf.at[at], s_in.at[q]))
            stores.append(pltpu.make_async_copy(buf.at[at], dst.at[at], s_out.at[q]))
    for load in loads:
        load.start()
    for load, store in zip(loads, stores):
        load.wait()
        store.start()
    for store in stores:
        store.wait()


def body(R, C, fine_tiles, out_grad, down_proj, qkv_proj, out_proj, norm_gain):
    A = 2 ** ((R.bit_length() - 1) // 2)
    B = R // A
    D = out_grad.shape[-1]
    th, tw = out_grad.shape[0], out_grad.shape[1]
    T = th * tw
    Z = C // 2
    tp = T // 2
    tb = tp // Z
    H8, W16, D2 = fine_tiles.shape
    ch = down_proj.shape[0]
    gb = D // R
    V = pltpu.VMEM
    S = pltpu.SemaphoreType.DMA
    scratch = [
        V((T, D), BF), V((T, D), BF),
        V((D2 // 128, H8, W16, 128), F32), V((C, 32, 128), BF), V((C, 2, 16, 128), BF),
        V((tp, 2 * ch), BF), V((2 * ch, D), BF), V((2, D, 4 * HEAD), BF), V((2, 4 * HEAD, D), BF),
        V((2 * HEAD, D), BF),
        V((tp, D), BF), V((Z, tb, D), BF), V((2, tb, D), BF), V((tb, D), F32), V((tb, 128), F32),
        V((T, D), BF), V((tp, 128), BF), V((HEAD, tp), BF),
        V((B, T, 128), BF),
        V((B, 128, T), BF), V((A, 128, T), BF), V((B, T, 128), BF), V((B, T, 128), BF),
        V((A, T, 128), BF), V((A, T, 128), BF),
        V((A, HEAD, T), BF), V((A, HEAD, T), BF), V((A, 8, T), F32), V((A, 8, T), F32),
        V((A, 8, T), F32), V((T, 128), BF), V((tp, 128), BF),
        V((tp, D), BF), V((Z, tb, D), BF), V((2, tb, D), BF),
        V((B, T, 128), F32), V((B, T, 128), BF), V((B, T, 128), BF),
        V((A, HEAD, T), F32), V((A, HEAD, T), BF), V((A, HEAD, T), BF),
        V((T, 128), BF), V((tp, 128), BF), V((HEAD, T), BF), V((HEAD, tp), BF),
        V((tp, D), BF), V((Z, tb, D), BF), V((2, tb, D), BF),
        V((4 * HEAD, D), F32), V((D, 4 * HEAD), BF), V((R, gb, 4 * HEAD), BF),
        V((tp, D), BF), V((D // 128, 128), F32), V((C, D // 128, 128), F32),
        V((D // 128, 128), F32), V((R, D // 128, 128), F32), V((D // 128, 128), F32),
        V((tp, ch), BF), V((2, D, ch), BF), V((2 * R, gb, ch), BF),
        S((24,)), S((5,)), S((10, Z)), S((12,)), S((12,)), S((9, max(A, B))), S((6,)),
    ]
    vm = pl.BlockSpec(memory_space=pltpu.VMEM)
    hb = pl.BlockSpec(memory_space=pl.ANY)
    outs = pl.pallas_call(
        functools.partial(kernel, R, C, A),
        out_shape=(
            jax.ShapeDtypeStruct((T, D), BF),
            jax.ShapeDtypeStruct((T, ch), BF),
            jax.ShapeDtypeStruct((gb, ch), F32),
            jax.ShapeDtypeStruct((3, gb, HEAD), F32),
            jax.ShapeDtypeStruct((HEAD, gb), F32),
            jax.ShapeDtypeStruct((1, gb), F32),
        ),
        in_specs=[vm, hb, hb, hb, hb, vm],
        out_specs=(hb,) + (vm,) * 5,
        scratch_shapes=scratch,
        compiler_params=pltpu.CompilerParams(
            collective_id=0, has_side_effects=True, vmem_limit_bytes=56 * 1024 * 1024),
        name="block",
    )(fine_tiles, out_grad.reshape(T, D), down_proj, qkv_proj.transpose(1, 2, 0).reshape(3 * HEAD, D), out_proj,
      norm_gain)
    parts = [8, 1, 1, 1, 1, 1]
    co, mg, dg, qg, opg, gg = pl.pallas_call(
        functools.partial(hand_over, parts),
        out_shape=[jax.ShapeDtypeStruct(o.shape, o.dtype) for o in outs],
        in_specs=[hb] * 6,
        out_specs=[hb] * 6,
        scratch_shapes=[V(o.shape, o.dtype) for o in outs] + [S((sum(parts),))] * 2,
        name="hand_over",
    )(*outs)
    return (co.reshape(th, tw, D), mg.reshape(th, tw, ch), dg.T, qg.transpose(1, 0, 2), opg,
            gg.reshape(gb))


def solution(mesh):
    R, C = mesh.shape["row"], mesh.shape["col"]
    return jax.shard_map(
        functools.partial(body, R, C),
        mesh=mesh,
        in_specs=(P("row", "col", None), P("row", None, None), P("col", None),
                  P(None, None, "col"), P("col", None), P()),
        out_specs=(P("row", None, None), P("row", None, "col"), P("col", "row"),
                   P("row", None, "col"), P("col", "row"), P("row")),
        check_vma=False,
    )
```

```python
import functools

import jax
import jax.numpy as jnp
from jax import lax
from jax.experimental import pallas as pl
from jax.experimental.pallas import tpu as pltpu
from jax.sharding import PartitionSpec as P

HEAD = 64
EPSILON = 1e-06
BF = jnp.bfloat16
F32 = jnp.float32


def mm(x, y):
    return jnp.dot(x, y, preferred_element_type=F32)


def mm_nt(x, y):
    return lax.dot_general(x, y, (((1,), (1,)), ((), ())), preferred_element_type=F32)


def flip(x):
    return x.astype(F32).T


def kernel(R, C, A, *refs):
    (fine, og_h, down_h, qkv_h, outp_h, gain,
     co_h, mg_o, dg_o, qg_o, opg_o, gg_o,
     og, co_o, fine_f, a2a_s, mrecv, merged, down_p, w_s, w_t, out_p,
     rs1_s, rs1_r, rs1_m, coarse_s, inv_s, normed, px_kv, px_q,
     kv, kv_t, qd_t, k_m, v_m, q_m, d_m,
     o_s, o_r, lse_s, lse_r, st, att_s, att_r,
     rs2_s, rs2_r, rs2_m, dkv_acc, dkv_s, dkv_r, dq_acc, dq_s, dq_r, dpk_s, dpk_r, dpq_s, dpq_r,
     rs3_s, rs3_r, rs3_m, g_t, g_s, g_r, cc, gn_s, gn_r, gt_s, gt_r, gsum, mg_s, dn_s, dn_r,
     s_one, r_one, r_z, s_p, r_p, r_ab, s_in) = refs
    B = R // A
    Z = C // 2
    T, D = og.shape
    core = lax.rem(lax.axis_index("row"), 2)
    tp = T // 2
    tb = tp // Z
    r = lax.axis_index("row")
    c = lax.axis_index("col")
    a = lax.rem(r, A)
    b = lax.div(r, A)
    z = lax.div(c, 2)
    x = lax.rem(c, 2)
    y = 1 - x
    pc = z * 2 + y

    def rcopy(src, dst, ssem, rsem, dev):
        return pltpu.make_async_remote_copy(
            src_ref=src, dst_ref=dst, send_sem=ssem, recv_sem=rsem,
            device_id=dev, device_id_type=pl.DeviceIdType.MESH)

    def blk(ref, j, n):
        return ref.at[pl.ds(pl.multiple_of(j * n, n), n)]

    def zrow(ref, j):
        return blk(ref, j, tb)

    def own(ref):
        return ref.at[pl.ds(pl.multiple_of(x * tp + z * tb, tb), tb)]

    def plane(ref, p):
        return blk(ref, p, tp)

    def loop(n, fn):
        lax.fori_loop(1, n, lambda i, t: (fn(i), t)[1], 0)

    def ring(n, me, dev, near):
        def off(i):
            odd = lax.rem(i, 2)
            return odd * lax.div(i + 1, 2) + (1 - odd) * (n - lax.div(i, 2)) if near else i

        def send_one(sem, src, dst, j):
            rcopy(src, dst(me), sem[0], sem[1](me), dev(j)).start()

        def send(sem, src, dst):
            def one(i):
                j = lax.rem(me + off(i), n)
                send_one(sem, src(j), dst, j)
            loop(n, one)

        def wait(sem, dst, i):
            s = lax.rem(me + n - off(i), n)
            rcopy(dst(s), dst(s), sem[0], sem[1](s), dev(s)).wait_recv()
            return s
        return send_one, send, wait

    def all_sent(sem, size):
        rcopy(size, size, sem[0], sem[1](0), (r, pc)).wait_send()

    def all_here(sem, size):
        rcopy(size, size, sem[0], sem[1](0), (r, pc)).wait_recv()

    _, col_send, _ = ring(C, c, lambda j: (r, j), False)
    _, z_send, z_wait = ring(Z, z, lambda j: (r, j * 2 + x), True)
    _, row_send, _ = ring(R, r, lambda j: (j, c), False)
    a_one, a_send, a_wait = ring(A, a, lambda j: (b * A + j, c), False)
    b_one, b_send, b_wait = ring(B, b, lambda j: (j * A + a, c), False)

    def one(k):
        return s_one.at[k], lambda j: r_one.at[k]

    def sz(k):
        return s_one.at[5 + k], lambda j: r_z.at[k, j]

    def sr(k):
        return s_one.at[15 + k], lambda j: r_ab.at[k, j]

    def zd(d):
        return lax.rem(z + 8 + d, 8)

    def rs_copy(k, src, r_ref, q, d):
        return rcopy(src, r_ref.at[q], s_one.at[5 + k], r_z.at[k, q], (r, zd(d) * 2 + x))

    def rs_start(k, s_ref, r_ref):
        if Z != 8:
            z_send(sz(k), lambda j: zrow(s_ref, j), lambda j: r_ref.at[j])
            return
        rs_copy(k, zrow(s_ref, zd(4)), r_ref, 2, 4 * core - 2).start()
        rs_copy(k, zrow(s_ref, zd(-3)), r_ref, 0, -1).start()
        rs_copy(k, zrow(s_ref, zd(3)), r_ref, 1, 1).start()
        rs_copy(k, zrow(s_ref, zd(-1)), r_ref, 3, -1).start()
        rs_copy(k, zrow(s_ref, zd(1)), r_ref, 4, 1).start()

    def rs_wait(k, r_ref, qs):
        for q in qs:
            rs_copy(k, r_ref.at[q], r_ref, q, 1).wait_recv()

    def rs_mid(k, s_ref, r_ref, m_ref):
        if Z != 8:
            return
        rs_wait(k, r_ref, (0, 1, 2))
        far = r_ref[2].astype(F32)
        none = jnp.zeros_like(far)
        m_ref[0] = (zrow(s_ref, zd(-2))[...].astype(F32) + r_ref[0].astype(F32)
                    + jnp.where(core == 0, far, none)).astype(BF)
        rs_copy(k, m_ref.at[0], r_ref, 5, -2).start()
        m_ref[1] = (zrow(s_ref, zd(2))[...].astype(F32) + r_ref[1].astype(F32)
                    + jnp.where(core == 0, none, far)).astype(BF)
        rs_copy(k, m_ref.at[1], r_ref, 6, 2).start()

    def ag_copy(k, at, s, d):
        return rcopy(at(s), at(s), s_one.at[5 + k], r_z.at[k, s], (r, zd(d) * 2 + x))

    def ag_start(k, at):
        if Z != 8:
            z_send(sz(k), lambda j: at(z), at)
            return
        for d in (2, -2, 1, -1):
            ag_copy(k, at, z, d).start()

    def ag_wait(k, at, ds):
        for d in ds:
            ag_copy(k, at, zd(d), 1).wait_recv()

    def ag_mid(k, at):
        if Z != 8:
            return
        ag_wait(k, at, (-2,))
        ag_copy(k, at, zd(-2), 1).start()
        ag_wait(k, at, (2,))
        ag_copy(k, at, zd(2), -1).start()
        ag_copy(k, at, zd(4 * core - 2), 2 - 4 * core).start()

    def ag_end(k, at):
        if Z != 8:
            loop(Z, lambda i: z_wait(sz(k), at, i))
            return
        ag_wait(k, at, (-1, 1, -3, 3, 4))

    def pair(k, src, dst):
        return rcopy(src, dst, s_p.at[k], r_p.at[k], (r, pc))

    ch = down_h.shape[0]
    my_down = blk(down_p, x, ch)
    my_out = blk(out_p, x, HEAD)
    loads = [
        pltpu.make_async_copy(down_h, my_down, s_in.at[0]),
        pltpu.make_async_copy(outp_h, my_out, s_in.at[1]),
        pltpu.make_async_copy(og_h, og, s_in.at[2]),
        pltpu.make_async_copy(
            qkv_h.at[pl.ds(HEAD, 2 * HEAD)], w_t.at[x, pl.ds(0, 2 * HEAD)], s_in.at[3]),
        pltpu.make_async_copy(
            qkv_h.at[pl.ds(0, HEAD)], w_t.at[x, pl.ds(2 * HEAD, HEAD)], s_in.at[4]),
    ]
    for load in loads:
        load.start()

    barrier = pltpu.get_barrier_semaphore()

    def greet(dev):
        pl.semaphore_signal(barrier, inc=1, device_id=dev, device_id_type=pl.DeviceIdType.MESH)
    loop(C, lambda i: greet((r, lax.rem(c + i, C))))
    loop(R, lambda i: greet((lax.rem(r + i, R), c)))
    loop(R, lambda i: greet((lax.rem(r + i, R), pc)))

    H8, W16, D2 = fine.shape
    n_cb = D2 // 128
    for cb in range(n_cb):
        fine_f[cb] = fine[:, :, cb * 128:(cb + 1) * 128].astype(F32)
    for aa in range(2):
        for bb in range(2):
            for cb in range(n_cb):
                parts = [fine_f[cb, 2 * h + aa, pl.ds(bb, W16 // 2, stride=2), :]
                         for h in range(H8 // 2)]
                a2a_s[(aa * 2 + bb) * n_cb + cb] = jnp.concatenate(parts, axis=0).astype(BF)

    def a2a_src(j):
        return a2a_s.at[pl.ds(lax.div(j, 2) * 2, 2), pl.ds(pl.multiple_of(lax.rem(j, 2) * 16, 16), 16)]

    pl.semaphore_wait(barrier, C + 2 * R - 3)
    col_send(one(0), a2a_src, lambda j: mrecv.at[j])
    loads[0].wait()
    hw = D // 2

    def cols(h):
        return pl.ds(h * hw, hw)

    def halves(h, s_ref, r_ref, m_ref):
        return s_ref.at[:, cols(h)], r_ref.at[:, :, cols(h)], m_ref.at[:, :, cols(h)]
    p_down = [pair(k, my_down.at[:, cols(h)], my_down.at[:, cols(h)])
              for h, k in enumerate((0, 11))]
    for p in p_down:
        p.start()

    mrecv[c] = a2a_src(c)[...]
    loads[1].wait()
    loads[2].wait()
    qd_t[a, HEAD:, :] = mm_nt(my_out[...], og[...]).astype(BF)

    def d_at(j):
        return qd_t.at[j, pl.ds(HEAD, HEAD)]
    a_send(sr(7), lambda j: d_at(a), d_at)
    for k in range(2):
        w_t[k, 3 * HEAD:, :] = jnp.zeros((HEAD, D), BF)
    loads[3].wait()
    loads[4].wait()

    all_here(one(0), mrecv.at[pl.ds(0, C - 1)])
    for k in range(2):
        mr = mrecv[:, k].astype(F32).reshape(C, 2, W16 // 2, 128)
        merged[:, k * 128:(k + 1) * 128] = jnp.swapaxes(mr, 0, 1).reshape(tp, 128).astype(BF)
    for h in range(2):
        p_down[h].wait_recv()
        rs1_s[:, h * hw:(h + 1) * hw] = mm(
            merged[...], down_p[:, h * hw:(h + 1) * hw]).astype(BF)
        rs_start(7 * h, *halves(h, rs1_s, rs1_r, rs1_m)[:2])
    p_w = pair(1, w_t.at[x, pl.ds(0, 3 * HEAD)], w_t.at[x, pl.ds(0, 3 * HEAD)])
    p_w.start()
    p_out = pair(2, my_out, my_out)
    p_out.start()
    w_s[x] = flip(w_t[x]).astype(BF)
    for h in range(2):
        rs_mid(7 * h, *halves(h, rs1_s, rs1_r, rs1_m))
    dkv_acc[...] = jnp.zeros(dkv_acc.shape, F32)
    dq_acc[...] = jnp.zeros(dq_acc.shape, F32)

    def reduce_z(k, s_ref, r_ref):
        if Z == 8:
            rs_wait(k, r_ref, (3, 4, 5, 6))
            acc = zrow(s_ref, z)[...].astype(F32)
            for q in (3, 4, 5, 6):
                acc = acc + r_ref[q].astype(F32)
            return acc

        def one(i, acc):
            s = z_wait(sz(k), lambda q: r_ref.at[q], i)
            return acc + r_ref[s].astype(F32)
        return lax.fori_loop(1, Z, one, zrow(s_ref, z)[...].astype(F32))

    coarse = jnp.concatenate(
        [reduce_z(7 * h, *halves(h, rs1_s, rs1_r, rs1_m)[:2]) for h in range(2)],
        axis=1).astype(BF).astype(F32)
    coarse_s[...] = coarse
    inv = lax.rsqrt(jnp.mean(coarse * coarse, axis=-1, keepdims=True) + EPSILON)
    inv_s[...] = jnp.broadcast_to(inv, inv_s.shape)
    gain_f = gain[...].astype(F32).reshape(1, D)
    own(normed)[...] = (coarse * inv * gain_f).astype(BF)

    def own_at(ref):
        return lambda j: ref.at[pl.ds(pl.multiple_of(x * tp + j * tb, tb), tb)]
    ag_start(1, own_at(normed))
    ag_mid(1, own_at(normed))
    p_w.wait_recv()
    w_s[y] = flip(w_t[y]).astype(BF)
    ag_end(1, own_at(normed))

    temper = HEAD ** (-0.5)
    n_pl = plane(normed, x)[...]
    mine = pl.ds(pl.multiple_of(x * tp, tp), tp)

    def split(w):
        proj = mm(n_pl, w)
        return proj[:, :128].astype(BF), flip(proj[:, 128:].astype(BF).astype(F32) * temper)
    kv_y, q_y = split(w_s[y])
    px_kv[...] = kv_y
    p_kv = pair(3, px_kv, kv.at[b, mine])
    p_kv.start()
    px_q[...] = q_y[:HEAD].astype(BF)
    p_q = pair(4, px_q, qd_t.at[a, pl.ds(0, HEAD), mine])
    p_q.start()
    kv_x, q_x = split(w_s[x])
    kv[b, mine] = kv_x
    qd_t[a, :HEAD, mine] = q_x[:HEAD].astype(BF)

    def kv_at(p):
        return lambda j: kv.at[j, pl.ds(pl.multiple_of(p * tp, tp), tp)]
    b_send(sr(0), lambda j: kv_at(x)(b), kv_at(x))
    p_kv.wait_recv()
    b_send(sr(1), lambda j: kv_at(y)(b), kv_at(y))
    p_q.wait_recv()

    def q_at(j):
        return qd_t.at[j, pl.ds(0, HEAD)]
    a_send(sr(8), lambda j: q_at(a), q_at)

    lane = lax.broadcasted_iota(jnp.int32, (T, 128), 1)
    zero = jnp.zeros((T, 128), BF)

    def prep_kv(s):
        v = kv[s]
        kv_t[s] = flip(v).astype(BF)
        k_m[s] = jnp.where(lane < HEAD, v, zero)
        v_m[s] = jnp.where(lane >= HEAD, v, zero)

    def prep_qd(s):
        v = flip(qd_t[s]).astype(BF)
        q_m[s] = jnp.where(lane < HEAD, v, zero)
        d_m[s] = jnp.where(lane >= HEAD, v, zero)

    prep_kv(b)
    prep_qd(a)

    def kv_next(i):
        b_wait(sr(0), kv_at(x), i)
        prep_kv(b_wait(sr(1), kv_at(y), i))
    loop(B, kv_next)

    def qd_next(i):
        a_wait(sr(7), d_at, i)
        prep_qd(a_wait(sr(8), q_at, i))
    loop(A, qd_next)

    def fwd_q(qi):
        qs = qd_t[qi]
        ss = [mm(k_m[kj], qs) for kj in range(B)]
        top = functools.reduce(
            jnp.maximum, [jnp.max(v, axis=0, keepdims=True) for v in ss])
        ps = [jnp.exp(v - top) for v in ss]
        total = sum(jnp.sum(p, axis=0, keepdims=True) for p in ps)
        acc = sum(mm(kv_t[kj, HEAD:, :], p.astype(BF)) for kj, p in enumerate(ps))
        o_s[qi] = (acc / total).astype(BF)
        lse_s[qi] = jnp.broadcast_to(top + jnp.log(total), lse_s.shape[1:])

    def fwd_one(i):
        qi = lax.rem(a + i, A)
        fwd_q(qi)
        a_one(sr(2), o_s.at[qi], lambda j: o_r.at[j], qi)
        a_one(sr(3), lse_s.at[qi], lambda j: lse_r.at[j], qi)
    loop(A, fwd_one)
    fwd_q(a)
    o_r[a] = o_s[a]
    lse_r[a] = lse_s[a]
    loop(A, lambda i: (a_wait(sr(2), lambda s: o_r.at[s], i),
                       a_wait(sr(3), lambda s: lse_r.at[s], i)))

    lses = [lse_r[s, 0:1, :] for s in range(A)]
    top = functools.reduce(jnp.maximum, lses)
    lse = top + jnp.log(sum(jnp.exp(v - top) for v in lses))
    o_t = sum(jnp.exp(v - lse) * o_r[s].astype(F32) for s, v in enumerate(lses)).astype(BF)
    delta = jnp.sum(qd_t[a, HEAD:, :].astype(F32) * o_t.astype(F32), axis=0, keepdims=True)
    st[a] = jnp.concatenate([lse, delta, jnp.zeros((6, T), F32)], axis=0)
    a_send(sr(4), lambda j: st.at[a], lambda j: st.at[j])

    att_s[:, :HEAD] = flip(o_t).astype(BF)
    att_s[:, HEAD:] = jnp.zeros((T, 128 - HEAD), BF)
    p_att = pair(5, plane(att_s, y), att_r)
    p_att.start()
    o_s[a] = o_t
    loop(A, lambda i: a_wait(sr(4), lambda s: st.at[s], i))

    def tile(kj, qi):
        qs = qd_t[qi]
        p = jnp.exp(mm(k_m[kj], qs) - st[qi, 0:1, :])
        ds = (p * (mm(v_m[kj], qs) - st[qi, 1:2, :])).astype(BF)
        dkv_acc[kj] += mm(ds, q_m[qi]) + mm(p.astype(BF), d_m[qi])
        dq_acc[qi] += mm(kv_t[kj, :HEAD, :], ds)

    def bwd_one(i):
        kj = lax.rem(b + i, B)

        def two(h, t0):
            tile(kj, lax.rem(a + 2 * h, A))
            tile(kj, lax.rem(a + 2 * h + 1, A))
            return t0
        lax.fori_loop(0, A // 2, two, 0)
        dkv_s[kj] = dkv_acc[kj].astype(BF)
        b_one(sr(5), dkv_s.at[kj], lambda j: dkv_r.at[j], kj)

        @pl.when(i == 1)
        def _():
            p_att.wait_recv()
            p_norm.start()
            p_out.wait_recv()
            rs2_s[...] = (mm(plane(att_s, x)[:, :HEAD], my_out[...])
                          + mm(att_r[:, :HEAD], blk(out_p, y, HEAD)[...])).astype(BF)
            rs_start(2, rs2_s, rs2_r)

        @pl.when(i == min(2, B - 1))
        def _():
            rs_mid(2, rs2_s, rs2_r, rs2_m)
    p_norm = pair(6, plane(normed, x), plane(normed, x))
    loop(B, bwd_one)

    mixed = reduce_z(2, rs2_s, rs2_r)
    own(co_o)[...] = (coarse_s[...] + mixed).astype(BF)
    ag_start(5, own_at(co_o))

    for i in range(1, A + 1):
        qi = lax.rem(a + i, A)
        tile(b, qi)
        if i < A:
            dq_s[qi] = dq_acc[qi].astype(BF)
            a_one(sr(6), dq_s.at[qi], lambda j: dq_r.at[j], qi)

    ag_mid(5, own_at(co_o))

    def dkv_sum(i, acc):
        s = b_wait(sr(5), lambda q: dkv_r.at[q], i)
        return acc + dkv_r[s].astype(F32)
    dkv = lax.fori_loop(1, B, dkv_sum, dkv_acc[b]).astype(BF)

    dpk_s[...] = dkv
    p_dpk = pair(7, plane(dpk_s, y), dpk_r)
    p_dpk.start()
    part = mm(plane(dpk_s, x)[...], w_t[x, :2 * HEAD, :])

    def dq_sum(i, acc):
        s = a_wait(sr(6), lambda q: dq_r.at[q], i)
        return acc + dq_r[s].astype(F32)
    dq_t = (lax.fori_loop(1, A, dq_sum, dq_acc[a]) * temper).astype(BF)
    dpq_s[...] = dq_t
    other = pl.ds(pl.multiple_of(y * tp, tp), tp)
    p_dpq = pair(10, dpq_s.at[:, other], dpq_r)
    p_dpq.start()
    part += mm(flip(dpq_s[:, mine]).astype(BF), w_t[x, 2 * HEAD:3 * HEAD, :])
    p_dpk.wait_recv()
    part += mm(dpk_r[...], w_t[y, :2 * HEAD, :])
    p_dpq.wait_recv()
    dq_y = flip(dpq_r[...]).astype(BF)
    for h in range(2):
        at = slice(h * hw, (h + 1) * hw)
        rs3_s[:, at] = (part[:, at] + mm(dq_y, w_t[y, 2 * HEAD:3 * HEAD, at])).astype(BF)
        rs_start(3 + 5 * h, *halves(h, rs3_s, rs3_r, rs3_m)[:2])

    ag_end(5, own_at(co_o))
    p_co = pair(8, plane(co_o, x), plane(co_o, x))
    p_co.start()

    p_norm.wait_recv()
    for h in range(2):
        rs_mid(3 + 5 * h, *halves(h, rs3_s, rs3_r, rs3_m))
    g_t[3 * HEAD:, :] = mm(o_s[a], og[...])
    g_t[:2 * HEAD, :] = mm(flip(dkv).astype(BF), normed[...])
    g_t[2 * HEAD:3 * HEAD, :] = mm(dq_t, normed[...])
    g_s[...] = g_t[...].T.astype(BF)
    gb = D // R

    def g_rows(j):
        return blk(g_s, j, gb)
    row_send(one(2), g_rows, lambda j: g_r.at[j])

    ncot = jnp.concatenate(
        [reduce_z(3 + 5 * h, *halves(h, rs3_s, rs3_r, rs3_m)[:2]) for h in range(2)], axis=1)
    coarse = coarse_s[...]
    inv = inv_s[:, :1]
    gpart = jnp.sum(ncot * coarse * inv, axis=0, keepdims=True)
    scaled = ncot * gain_f
    ccot = own(og)[...].astype(F32) + inv * scaled - coarse * (inv * inv * inv) * jnp.mean(
        scaled * coarse, axis=-1, keepdims=True)
    zrow(cc, z)[...] = ccot.astype(BF)
    def cc_at(j):
        return zrow(cc, j)
    ag_start(4, cc_at)
    gp = jnp.concatenate([gpart[:, i * 128:(i + 1) * 128] for i in range(D // 128)], axis=0)
    gn_s[...] = gp
    gn_r[c] = gp
    col_send(one(1), lambda j: gn_s, lambda j: gn_r.at[j])

    ag_mid(4, cc_at)

    def g_sum(i, acc):
        return acc + g_r[lax.rem(r + i, R)].astype(F32)
    all_here(one(2), g_r.at[pl.ds(0, R - 1)])
    g_all = lax.fori_loop(1, R, g_sum, g_rows(r)[...].astype(F32))
    for k in range(3):
        qg_o[k] = g_all[:, (k + 2) % 3 * HEAD:(k + 2) % 3 * HEAD + HEAD]
    opg_o[...] = g_all[:, 3 * HEAD:].T

    m_t = [flip(merged[:, k * 128:(k + 1) * 128]).astype(BF) for k in range(2)]
    p_co.wait_recv()
    co_out = pltpu.make_async_copy(co_o, co_h, s_in.at[5])
    co_out.start()
    me = r * 2 + x

    def dn_src(j):
        return dn_s.at[lax.rem(j, 2), pl.ds(pl.multiple_of(lax.div(j, 2) * gb, gb), gb)]
    ag_end(4, cc_at)
    for h in range(2):
        for k in range(2):
            dn_s[k, h * hw:(h + 1) * hw, :] = mm(
                m_t[k], cc[:, h * hw:(h + 1) * hw]).T.astype(BF)

        def dn_one(i, t0):
            j = h * R + lax.rem(i + me, R)

            @pl.when(j != me)
            def _():
                rcopy(dn_src(j), dn_r.at[me], s_one.at[4], r_one.at[4],
                      (lax.div(j, 2), z * 2 + lax.rem(j, 2))).start()
            return t0
        lax.fori_loop(0, R, dn_one, 0)

    mg_s[...] = mm_nt(cc[...], blk(down_p, y, ch)[...]).astype(BF)
    p_mg = pair(9, mg_s, plane(mg_o, x))
    p_mg.start()
    all_here(one(1), gn_r.at[pl.ds(0, C - 1)])
    gt = jnp.sum(gn_r[...], axis=0)
    gt_s[...] = gt
    gt_r[r] = gt
    row_send(one(3), lambda j: gt_s, lambda j: gt_r.at[j])
    plane(mg_o, x)[...] = mm_nt(cc[...], my_down[...]).astype(BF)

    def d_sum(i, acc):
        return acc + dn_r[lax.rem(me + i, 2 * R)].astype(F32)
    all_here(one(4), dn_r.at[pl.ds(0, 2 * R - 1)])
    dg_o[...] = lax.fori_loop(1, 2 * R, d_sum, dn_src(me)[...].astype(F32))

    all_here(one(3), gt_r.at[pl.ds(0, R - 1)])
    gsum[...] = jnp.sum(gt_r[...], axis=0)
    g_row = gsum[pl.ds(lax.div(r, 2), 1), :]
    gg_o[...] = jnp.where(lax.rem(r, 2) == 0, g_row[:, :64], g_row[:, 64:])

    p_mg.wait_recv()
    co_out.wait()
    for p in (*p_down, p_w, p_out, p_kv, p_q, p_att, p_norm, p_dpk, p_dpq, p_co, p_mg):
        p.wait_send()
    all_sent(one(0), mrecv.at[pl.ds(0, C - 1)])
    all_sent(one(1), gn_r.at[pl.ds(0, C - 1)])
    all_sent(one(2), g_r.at[pl.ds(0, R - 1)])
    all_sent(one(3), gt_r.at[pl.ds(0, R - 1)])
    all_sent(one(4), dn_r.at[pl.ds(0, 2 * R - 1)])
    for k in (1, 2, 4, 5):
        all_sent(sz(k), rs1_r.at[pl.ds(0, Z - 1)])
    for k in (0, 3, 7, 8):
        all_sent(sz(k), rs1_r.at[pl.ds(0, Z - 1), :, pl.ds(0, hw)])
    for k in (0, 1):
        all_sent(sr(k), kv.at[pl.ds(0, B - 1), pl.ds(0, tp)])
    for k in (7, 8, 2, 6):
        all_sent(sr(k), o_s.at[pl.ds(0, A - 1)])
    for k in (3, 4):
        all_sent(sr(k), st.at[pl.ds(0, A - 1)])
    all_sent(sr(5), dkv_s.at[pl.ds(0, B - 1)])


def hand_over(parts, *refs):
    ins, outs, bufs, s_in, s_out = refs[:6], refs[6:12], refs[12:18], refs[18], refs[19]
    loads, stores = [], []
    for src, dst, buf, n in zip(ins, outs, bufs, parts):
        rows = src.shape[0] // n
        for k in range(n):
            at, q = pl.ds(k * rows, rows), len(loads)
            loads.append(pltpu.make_async_copy(src.at[at], buf.at[at], s_in.at[q]))
            stores.append(pltpu.make_async_copy(buf.at[at], dst.at[at], s_out.at[q]))
    for load in loads:
        load.start()
    for load, store in zip(loads, stores):
        load.wait()
        store.start()
    for store in stores:
        store.wait()


def body(R, C, fine_tiles, out_grad, down_proj, qkv_proj, out_proj, norm_gain):
    A = 2 ** ((R.bit_length() - 1) // 2)
    B = R // A
    D = out_grad.shape[-1]
    th, tw = out_grad.shape[0], out_grad.shape[1]
    T = th * tw
    Z = C // 2
    tp = T // 2
    tb = tp // Z
    H8, W16, D2 = fine_tiles.shape
    ch = down_proj.shape[0]
    gb = D // R
    V = pltpu.VMEM
    S = pltpu.SemaphoreType.DMA
    scratch = [
        V((T, D), BF), V((T, D), BF),
        V((D2 // 128, H8, W16, 128), F32), V((C, 32, 128), BF), V((C, 2, 16, 128), BF),
        V((tp, 2 * ch), BF), V((2 * ch, D), BF), V((2, D, 4 * HEAD), BF), V((2, 4 * HEAD, D), BF),
        V((2 * HEAD, D), BF),
        V((tp, D), BF), V((Z, tb, D), BF), V((2, tb, D), BF), V((tb, D), F32), V((tb, 128), F32),
        V((T, D), BF), V((tp, 128), BF), V((HEAD, tp), BF),
        V((B, T, 128), BF),
        V((B, 128, T), BF), V((A, 128, T), BF), V((B, T, 128), BF), V((B, T, 128), BF),
        V((A, T, 128), BF), V((A, T, 128), BF),
        V((A, HEAD, T), BF), V((A, HEAD, T), BF), V((A, 8, T), F32), V((A, 8, T), F32),
        V((A, 8, T), F32), V((T, 128), BF), V((tp, 128), BF),
        V((tp, D), BF), V((Z, tb, D), BF), V((2, tb, D), BF),
        V((B, T, 128), F32), V((B, T, 128), BF), V((B, T, 128), BF),
        V((A, HEAD, T), F32), V((A, HEAD, T), BF), V((A, HEAD, T), BF),
        V((T, 128), BF), V((tp, 128), BF), V((HEAD, T), BF), V((HEAD, tp), BF),
        V((tp, D), BF), V((Z, tb, D), BF), V((2, tb, D), BF),
        V((4 * HEAD, D), F32), V((D, 4 * HEAD), BF), V((R, gb, 4 * HEAD), BF),
        V((tp, D), BF), V((D // 128, 128), F32), V((C, D // 128, 128), F32),
        V((D // 128, 128), F32), V((R, D // 128, 128), F32), V((D // 128, 128), F32),
        V((tp, ch), BF), V((2, D, ch), BF), V((2 * R, gb, ch), BF),
        S((24,)), S((5,)), S((10, Z)), S((12,)), S((12,)), S((9, max(A, B))), S((6,)),
    ]
    vm = pl.BlockSpec(memory_space=pltpu.VMEM)
    hb = pl.BlockSpec(memory_space=pl.ANY)
    outs = pl.pallas_call(
        functools.partial(kernel, R, C, A),
        out_shape=(
            jax.ShapeDtypeStruct((T, D), BF),
            jax.ShapeDtypeStruct((T, ch), BF),
            jax.ShapeDtypeStruct((gb, ch), F32),
            jax.ShapeDtypeStruct((3, gb, HEAD), F32),
            jax.ShapeDtypeStruct((HEAD, gb), F32),
            jax.ShapeDtypeStruct((1, gb), F32),
        ),
        in_specs=[vm, hb, hb, hb, hb, vm],
        out_specs=(hb,) + (vm,) * 5,
        scratch_shapes=scratch,
        compiler_params=pltpu.CompilerParams(
            collective_id=0, has_side_effects=True, vmem_limit_bytes=56 * 1024 * 1024),
        name="block",
    )(fine_tiles, out_grad.reshape(T, D), down_proj, qkv_proj.transpose(1, 2, 0).reshape(3 * HEAD, D), out_proj,
      norm_gain)
    parts = [8, 1, 1, 1, 1, 1]
    co, mg, dg, qg, opg, gg = pl.pallas_call(
        functools.partial(hand_over, parts),
        out_shape=[jax.ShapeDtypeStruct(o.shape, o.dtype) for o in outs],
        in_specs=[hb] * 6,
        out_specs=[hb] * 6,
        scratch_shapes=[V(o.shape, o.dtype) for o in outs] + [S((sum(parts),))] * 2,
        name="hand_over",
    )(*outs)
    return (co.reshape(th, tw, D), mg.reshape(th, tw, ch), dg.T, qg.transpose(1, 0, 2), opg,
            gg.reshape(gb))


def solution(mesh):
    R, C = mesh.shape["row"], mesh.shape["col"]
    return jax.shard_map(
        functools.partial(body, R, C),
        mesh=mesh,
        in_specs=(P("row", "col", None), P("row", None, None), P("col", None),
                  P(None, None, "col"), P("col", None), P()),
        out_specs=(P("row", None, None), P("row", None, "col"), P("col", "row"),
                   P("row", None, "col"), P("col", "row"), P("row")),
        check_vma=False,
    )
```
